32 devices in a mesh: dp: 4 (over z), freq: 8 (over y, x, core).
Axes of the slice: x: 2, y: 2, z: 4, core: 2. Of those that a mesh axis runs over, the one named last changes fastest.
Arguments:
- tokens: bfloat16 [8, 2048, 768], P('dp', 'freq'), may hold values from -6 to 6
- offsets: int32 [8], P('dp'), may hold values from 0 to 1023, as said below
- kernel_lengths: int32 [768], replicated, may hold values from 512 to 2048, as said below
- norm1_gain: float32 [768], replicated, may hold values from 0.5 to 1.5
- norm1_bias: float32 [768], replicated, may hold values from -3 to 3
- input_projection_weight: bfloat16 [768, 2304], replicated, may hold values from -0.21875 to 0.21875
- in_bias: float32 [2304], replicated, may hold values from -2 to 2
- kernel_taps: float32 [768, 2048], P(None, 'freq'), may hold values from -0.25 to 0.25
- skip_gain: float32 [768], P('freq'), may hold values from -3 to 3
- out_weight: bfloat16 [768, 768], replicated, may hold values from -0.21875 to 0.21875
- out_bias: float32 [768], replicated, may hold values from -2 to 2
- norm2_gain: float32 [768], replicated, may hold values from 0.5 to 1.5
- norm2_bias: float32 [768], replicated, may hold values from -3 to 3
- up_projection_weight: bfloat16 [768, 3072], replicated, may hold values from -0.21875 to 0.21875
- fc1_bias: float32 [3072], replicated, may hold values from -2 to 2
- down_projection_weight: bfloat16 [3072, 768], replicated, may hold values from -0.109375 to 0.109375
- fc2_bias: float32 [768], replicated, may hold values from -2 to 2
- cotangent: bfloat16 [8, 2048, 768], P('dp', 'freq'), may hold values from -6 to 6
Outputs:
- block_out: bfloat16 [8, 2048, 768], P('dp', 'freq')
- input_grad: bfloat16 [8, 2048, 768], P('dp', 'freq')
- norm1_gain_grad: float32 [768], P('freq')
- norm1_bias_grad: float32 [768], P('freq')
- in_weight_grad: float32 [768, 2304], P('dp', 'freq')
- in_bias_grad: float32 [2304], P('freq')
- kernel_taps_grad: float32 [768, 2048], P(None, 'freq')
- skip_grad: float32 [768], P('freq')
- out_weight_grad: float32 [768, 768], P('dp', 'freq')
- out_bias_grad: float32 [768], P('freq')
- norm2_gain_grad: float32 [768], P('freq')
- norm2_bias_grad: float32 [768], P('freq')
- fc1_weight_grad: float32 [768, 3072], P('dp', 'freq')
- fc1_bias_grad: float32 [3072], P('freq')
- fc2_weight_grad: float32 [3072, 768], P('dp', 'freq')
- fc2_bias_grad: float32 [768], P('freq')
The draws below stay inside these ranges and needn't reach their ends.
Inputs may be any that keep to these rules, and one draw needn't show every extreme that they name: `offsets`: in every run of 2 consecutive sequences (those of one index of dp) at least one has offset 0; some sequence has offset 2048 / 2 - 1. `kernel_lengths`: at least one channel's kernel has all 2048 taps.
All inputs are finite; a program needn't handle non-finite values.
Results may differ from the reference program's by a relative error of at most 0.018.
Values may be sent and summed in bfloat16 or wider, within the bound.
No kernel may reach another device: no remote copies, remote signals or barrier semaphores. Data moves between devices by JAX's collectives and lax.ppermute only.
A program may use at most 192 MiB of HBM per device.

```python
import jax
import jax.numpy as jnp
from jax import lax

D = 768
FF = 3072
K = 2048
SEQS_DEV = 2
SEQS = 8
SEQ_LEN = 2048
N_DP = 4


def draw_offsets(key, part):
    key = jax.random.fold_in(key, 11)
    start_key, pick_key = jax.random.split(key)
    starts = jax.random.randint(start_key, (SEQS,), 0, SEQ_LEN // 2, dtype=jnp.int32)
    chosen = jax.random.randint(pick_key, (N_DP,), 0, SEQS_DEV, dtype=jnp.int32)
    places = jnp.arange(SEQS, dtype=jnp.int32)
    group_of = places // SEQS_DEV
    inside = places % SEQS_DEV
    picked = jnp.take(chosen, group_of)
    topped = jnp.logical_and(group_of == 0, inside == (chosen[0] + 1) % SEQS_DEV)
    starts = jnp.where(topped, SEQ_LEN // 2 - 1, starts)
    return jnp.where(inside == picked, 0, starts)


def draw_kernel_lengths(key, part):
    key = jax.random.fold_in(key, 23)
    length_key, pick_key = jax.random.split(key)
    lengths = jax.random.randint(length_key, (D,), K // 4, K + 1, dtype=jnp.int32)
    chosen = jax.random.randint(pick_key, (), 0, D, dtype=jnp.int32)
    return jnp.where(jnp.arange(D, dtype=jnp.int32) == chosen, K, lengths)


def raised(entries, stream_key, source, target, parts, factor):
    def block_of(dim):
        return (jnp.arange(entries.shape[dim]) // (entries.shape[dim] // parts)).reshape((-1,) + (1,) * (entries.ndim - 1 - dim))

    first = jax.random.permutation(stream_key, parts)[block_of(target)]
    far = (block_of(target) + parts // 2) % parts
    return jnp.where((block_of(source) == first) | (block_of(source) == far), factor * entries, entries)


def shard_levels(rng, dims, shards, least, high):
    def one(position, parts):
        steps = jax.random.uniform(jax.random.fold_in(jax.random.fold_in(rng, 6), position), (parts,), jnp.float32, least / len(shards), high / len(shards))
        return jnp.repeat(jnp.exp(steps), dims[position] // parts).reshape((-1,) + (1,) * (len(dims) - position - 1))

    factor_of = one(*shards[0])
    for cut in shards[1:]:
        factor_of = factor_of * one(*cut)
    return factor_of


def scatter_about(stream_key, extent, deviation, bound, shards=(), kind=jnp.bfloat16):
    entries = deviation * jax.random.normal(stream_key, extent, jnp.float32)
    if shards:
        entries = entries * shard_levels(stream_key, extent, shards, -0.22, 0.18)
    return jnp.clip(entries, -bound, bound).astype(kind)


def heavy_noise(own_key, extent, scale, most, cuts, heavy, kind=jnp.bfloat16):
    array = scale * jax.random.normal(own_key, extent, jnp.float32)
    if cuts:
        array = array * shard_levels(own_key, extent, cuts, -0.22, 0.18)
    return jnp.clip(raised(array, jax.random.fold_in(own_key, 3), *heavy), -most, most).astype(kind)


def setup_inputs(seed: int = 0) -> dict:
    seeds = jax.random.split(jax.random.key(seed), 19)
    tokens = scatter_about(seeds[0], (SEQS, SEQ_LEN, D), 1.0, 6.0, ((0, 4), (1, 8)))
    offsets = draw_offsets(jax.random.fold_in(seeds[18], 71), 0)
    kernel_lengths = draw_kernel_lengths(jax.random.fold_in(seeds[18], 71), 0)
    norm1_gain = jnp.clip(1.0 + 0.1 * jax.random.normal(seeds[3], (D,), jnp.float32), 0.5, 1.5)
    norm1_bias = scatter_about(seeds[4], (D,), 0.5, 3.0, (), jnp.float32)
    input_projection_weight = scatter_about(seeds[5], (D, 3 * D), D ** -0.5, 0.21875)
    in_bias = scatter_about(seeds[6], (3 * D,), 0.3, 2.0, (), jnp.float32)
    kernel_taps = scatter_about(seeds[7], (D, K), (K // 4) ** -0.5, 0.25, ((1, 8),), jnp.float32)
    skip_gain = scatter_about(seeds[8], (D,), 0.5, 3.0, ((0, 8),), jnp.float32)
    out_weight = scatter_about(seeds[9], (D, D), D ** -0.5, 0.21875)
    out_bias = scatter_about(seeds[10], (D,), 0.3, 2.0, (), jnp.float32)
    norm2_gain = jnp.clip(1.0 + 0.1 * jax.random.normal(seeds[11], (D,), jnp.float32), 0.5, 1.5)
    norm2_bias = scatter_about(seeds[12], (D,), 0.5, 3.0, (), jnp.float32)
    up_projection_weight = scatter_about(seeds[13], (D, FF), D ** -0.5, 0.21875)
    fc1_bias = scatter_about(seeds[14], (FF,), 0.3, 2.0, (), jnp.float32)
    down_projection_weight = scatter_about(seeds[15], (FF, D), FF ** -0.5, 0.109375)
    fc2_bias = scatter_about(seeds[16], (D,), 0.3, 2.0, (), jnp.float32)
    cotangent = heavy_noise(seeds[17], (SEQS, SEQ_LEN, D), 1.0, 6.0, ((0, 4), (1, 8)), (1, 2, 8, 2.0))
    return {"tokens": tokens, "offsets": offsets, "kernel_lengths": kernel_lengths, "norm1_gain": norm1_gain, "norm1_bias": norm1_bias, "input_projection_weight": input_projection_weight, "in_bias": in_bias, "kernel_taps": kernel_taps, "skip_gain": skip_gain, "out_weight": out_weight, "out_bias": out_bias, "norm2_gain": norm2_gain, "norm2_bias": norm2_bias, "up_projection_weight": up_projection_weight, "fc1_bias": fc1_bias, "down_projection_weight": down_projection_weight, "fc2_bias": fc2_bias, "cotangent": cotangent}


NORM_EPS = 1e-05
SHRINK = 0.003
PRECISE = lax.Precision.HIGHEST

@jax.custom_vjp
def low(v):
    return lax.optimization_barrier(v.astype(jnp.bfloat16)).astype(jnp.float32)

@jax.custom_vjp
def low_back(v):
    return v

def low_keep(v):
    return (low(v), None)

def low_pass(kept, grad):
    return (grad,)

def back_keep(v):
    return (v, None)

def back_low(kept, grad):
    return (low(grad),)
low.defvjp(low_keep, low_pass)
low_back.defvjp(back_keep, back_low)

def layer_norm(values, norm_gain, norm_shift):
    centred = values - lax.optimization_barrier(jnp.mean(values, axis=-1, keepdims=True))
    spread = lax.optimization_barrier(jnp.mean(centred * centred, axis=-1, keepdims=True))
    return centred * lax.rsqrt(spread + NORM_EPS) * norm_gain + norm_shift

def shaped_kernel(kernel_taps, kernel_lengths):
    shrunk = kernel_taps - SHRINK * jnp.tanh(kernel_taps / SHRINK)
    padded = jnp.pad(shrunk, ((0, 0), (1, 1)))
    pooled = (padded[:, :-2] + padded[:, 1:-1] + padded[:, 2:]) / 3.0
    places = jnp.arange(kernel_taps.shape[1], dtype=jnp.int32)
    return pooled * (places[None, :] < kernel_lengths[:, None]).astype(jnp.float32)

def block_forward(inputs, offsets, kernel_lengths, norm1_gain, norm1_bias, input_projection_weight, in_bias, kernel_taps, skip_gain, out_weight, out_bias, norm2_gain, norm2_bias, up_projection_weight, fc1_bias, down_projection_weight, fc2_bias):
    seq_len = inputs.shape[1]
    model_width = inputs.shape[2]
    first_normalized_input = low(layer_norm(inputs, norm1_gain, norm1_bias))
    projected = low_back(jnp.einsum('bsd,de->bse', first_normalized_input, input_projection_weight, precision=PRECISE) + in_bias)
    value_part = projected[..., :model_width]
    first_gate = projected[..., model_width:2 * model_width]
    second_gate = projected[..., 2 * model_width:]
    places = jnp.arange(seq_len, dtype=jnp.int32)
    live_mask = (places[None, :, None] >= offsets[:, None, None]).astype(jnp.float32)
    mixed_in = low_back(low(live_mask * first_gate * value_part))
    kernel = shaped_kernel(kernel_taps, kernel_lengths)
    length = 2 * seq_len
    spectrum = jnp.fft.rfft(mixed_in, n=length, axis=1) * jnp.fft.rfft(kernel.T, n=length, axis=0)[None]
    conv_out = jnp.fft.irfft(spectrum, n=length, axis=1)[:, :seq_len]
    conv_out = low_back(low(conv_out + skip_gain * mixed_in))
    gated = low(second_gate * conv_out)
    branch = low_back(jnp.einsum('bsd,de->bse', gated, out_weight, precision=PRECISE) + out_bias)
    residual = inputs + branch
    second_normalized_input = low(layer_norm(residual, norm2_gain, norm2_bias))
    hidden = low_back(jnp.einsum('bsd,df->bsf', second_normalized_input, up_projection_weight, precision=PRECISE) + fc1_bias)
    gelu_activation = low(jax.nn.gelu(hidden, approximate=True))
    return residual + jnp.einsum('bsf,fd->bsd', gelu_activation, down_projection_weight, precision=PRECISE) + fc2_bias

def reference(tokens, offsets, kernel_lengths, norm1_gain, norm1_bias, input_projection_weight, in_bias, kernel_taps, skip_gain, out_weight, out_bias, norm2_gain, norm2_bias, up_projection_weight, fc1_bias, down_projection_weight, fc2_bias, cotangent):
    params = tuple((member.astype(jnp.float32) for member in (norm1_gain, norm1_bias, input_projection_weight, in_bias, kernel_taps, skip_gain, out_weight, out_bias, norm2_gain, norm2_bias, up_projection_weight, fc1_bias, down_projection_weight, fc2_bias)))
    seq_count, seq_len, model_width = tokens.shape
    per_step = max(1, min(seq_count, 4096 // seq_len))
    while seq_count % per_step:
        per_step = per_step - 1
    step_count = seq_count // per_step
    inputs_all = tokens.astype(jnp.float32).reshape(step_count, per_step, seq_len, model_width)
    upstream_all = cotangent.astype(jnp.float32).reshape(step_count, per_step, seq_len, model_width)
    offsets_all = offsets.reshape(step_count, per_step)

    def one_step(running, pieces):
        inputs_now, upstream_now, offsets_now = pieces

        def forward(inputs_in, *weights):
            return block_forward(inputs_in, offsets_now, kernel_lengths, *weights)
        result, pullback = jax.vjp(forward, inputs_now, *params)
        gradients = pullback(upstream_now)
        running = tuple((total_now + update for total_now, update in zip(running, gradients[1:])))
        return (running, (result, gradients[0]))
    zero_sums = tuple((jnp.zeros_like(member) for member in params))
    totals, (results, input_grads) = lax.scan(one_step, zero_sums, (inputs_all, upstream_all, offsets_all))
    block_out = results.reshape(tokens.shape).astype(jnp.bfloat16)
    input_grad = input_grads.reshape(tokens.shape).astype(jnp.bfloat16)
    return (block_out, input_grad, totals[0], totals[1], totals[2], totals[3], totals[4], totals[5], totals[6], totals[7], totals[8], totals[9], totals[10], totals[11], totals[12], totals[13])
```

```python
import functools

import jax
import jax.numpy as jnp
import numpy as np
from jax import lax
from jax.experimental import pallas as pl
from jax.experimental.pallas import tpu as pltpu
from jax.sharding import PartitionSpec as P

NORM_EPS = 1e-05
SHRINK = 0.003
GELU_C = 0.7978845608028654
GELU_A = 0.044715
F32 = jnp.float32
BF16 = jnp.bfloat16
MIB = 1 << 20

NN = (((1,), (0,)), ((), ()))
NT = (((1,), (1,)), ((), ()))


def mm(left, right, dims=NN):
    return lax.dot_general(left, right, dims, preferred_element_type=F32)


def params(mib, grid_rank=0):
    kind = ("arbitrary",) * grid_rank if grid_rank else None
    return pltpu.CompilerParams(vmem_limit_bytes=mib * MIB, dimension_semantics=kind)


def vmem():
    return pl.BlockSpec(memory_space=pltpu.VMEM)


def smem():
    return pl.BlockSpec(memory_space=pltpu.SMEM)


def shape(dims, dtype):
    return jax.ShapeDtypeStruct(dims, dtype)


def cost(flops, moved, special=0):
    return pl.CostEstimate(flops=int(flops), bytes_accessed=int(moved), transcendentals=int(special))


def split16(table):
    high = np.asarray(table, np.float32).astype(jnp.bfloat16)
    low = (np.asarray(table, np.float64) - high.astype(np.float64)).astype(np.float32).astype(jnp.bfloat16)
    return high, low


@functools.lru_cache(maxsize=None)
def tables(width):
    order = np.concatenate([np.arange(0, width, 2), np.arange(1, width, 2)])
    turns = (2 * order[None, :] + 1) * np.arange(width)[:, None] % (4 * width)
    angle = np.pi * turns / (2 * width)
    forward = np.concatenate([np.cos(angle), -np.sin(angle)], axis=1)
    inverse = forward.T / width
    return split16(forward) + split16(inverse)


def split_value(value):
    high = value.astype(BF16)
    return high, (value - high.astype(F32)).astype(BF16)


def spectrum_of(block, fhi, flo):
    return mm(block, fhi) + mm(block, flo)


def signal_of(spec, ghi, glo):
    high, low = split_value(spec)
    return mm(high, ghi) + (mm(low, ghi) + mm(high, glo))


def each(count, step, unroll):
    if unroll:
        for i in range(count):
            step(i)
    else:
        lax.fori_loop(0, count, lambda i, c: (step(i), c)[1], 0)


def blocks_to_spectra(x_ref, spec_ref, fhi, flo, batch, width):
    count, chans = x_ref.shape[0], x_ref.shape[1]
    for b in range(batch):
        lanes = slice(b * width, (b + 1) * width)
        if chans % 16 == 0:
            rows = x_ref[:, :, lanes].reshape(count * chans, width)
            spec_ref[b] = spectrum_of(rows, fhi[...], flo[...]).reshape(count, chans, 2 * width)
        else:

            def step(j, b=b, lanes=lanes):
                spec_ref[b, j] = spectrum_of(x_ref[j, :, lanes], fhi[...], flo[...])

            each(count, step, False)


def tiles(chans, width, step):
    lane_tiles = width // 128

    def rows_step(rt):
        start = rt * 8 if isinstance(rt, int) else pl.multiple_of(rt * 8, 8)
        for lane in range(lane_tiles):
            step(pl.ds(start, 8), lane)

    each(chans // 8, rows_step, False)


def pair(ref, lead, rows, lane, width):
    return (
        ref[lead + (rows, slice(lane * 128, (lane + 1) * 128))],
        ref[lead + (rows, slice(width + lane * 128, width + (lane + 1) * 128))],
    )


def put_pair(ref, lead, rows, lane, width, value):
    ref[lead + (rows, slice(lane * 128, (lane + 1) * 128))] = value[0]
    ref[lead + (rows, slice(width + lane * 128, width + (lane + 1) * 128))] = value[1]


def times(a, k):
    return a[0] * k[0] - a[1] * k[1], a[0] * k[1] + a[1] * k[0]


def times_conj(a, k):
    return a[0] * k[0] + a[1] * k[1], a[1] * k[0] - a[0] * k[1]


def plus(a, b):
    return b if a is None else (a[0] + b[0], a[1] + b[1])


def quarter(now, before, sign):
    if before is None:
        return now
    if sign > 0:
        return now[0] - before[1], now[1] + before[0]
    return now[0] + before[1], now[1] - before[0]


def wide_quarter(now, before, width):
    lane = lax.broadcasted_iota(jnp.int32, (1, width), 1)
    sign = jnp.where(lane < width // 2, 1.0, -1.0)
    return jnp.concatenate(
        [now[:, :width] - sign * before[:, width:], now[:, width:] + sign * before[:, :width]], axis=1
    )


def wide_times(a, k, width, conj):
    ar, ai, kr, ki = a[:, :width], a[:, width:], k[:, :width], k[:, width:]
    if conj:
        return jnp.concatenate([ar * kr + ai * ki, ai * kr - ar * ki], axis=1)
    return jnp.concatenate([ar * kr - ai * ki, ar * ki + ai * kr], axis=1)


UNROLLED = 8


def small(count, chans, width):
    return count <= UNROLLED and chans % 16 == 0 and width % 256 == 0


def conv_products(spec_ref, k_ref, z_ref, batch, width, adjoint):
    reach, chans = k_ref.shape[0], k_ref.shape[1]
    count = spec_ref.shape[1]
    if small(count, chans, width):

        def step(rows, lane):
            k = [pair(k_ref, (d,), rows, lane, width) for d in range(reach)]
            for b in range(batch):
                x = [pair(spec_ref, (b, j), rows, lane, width) for j in range(count)]
                for i in range(count):
                    total = None
                    if adjoint:
                        for d in range(min(count - i, reach)):
                            total = plus(total, times_conj(x[i + d], k[d]))
                    else:
                        for d in range(min(i + 1, reach)):
                            total = plus(total, times(x[i - d], k[d]))
                    put_pair(z_ref, (b, i), rows, lane, width, total)

        tiles(chans, width, step)
        return
    for b in range(batch):

        def row(i, b=b):
            def term(d, total):
                src = i + d if adjoint else i - d
                return total + wide_times(spec_ref[b, src], k_ref[d], width, adjoint)

            terms = jnp.minimum(count - i if adjoint else i + 1, reach)
            z_ref[b, i] = lax.fori_loop(0, terms, term, jnp.zeros((chans, 2 * width), F32))

        each(count, row, False)


def conv_kernel(adjoint, x_ref, k_ref, skip_ref, fhi, flo, ghi, glo, out_ref, spec_ref, z_ref):
    count, chans, lanes = x_ref.shape
    width = fhi.shape[0]
    batch = lanes // width
    blocks_to_spectra(x_ref, spec_ref, fhi, flo, batch, width)
    conv_products(spec_ref, k_ref, z_ref, batch, width, adjoint)
    for b in range(batch):
        cut = slice(b * width, (b + 1) * width)
        if chans % 16 == 0:
            y = signal_of(z_ref[b].reshape(count * chans, 2 * width), ghi[...], glo[...])
            y = y.reshape(count, chans, width) + skip_ref[...][None] * x_ref[:, :, cut].astype(F32)
            out_ref[:, :, cut] = y.astype(BF16)
        else:

            def step(j, b=b, cut=cut):
                y = signal_of(z_ref[b, j], ghi[...], glo[...])
                out_ref[j, :, cut] = (y + skip_ref[...] * x_ref[j, :, cut].astype(F32)).astype(BF16)

            each(count, step, False)


def conv_call(x, k_spec, skip, adjoint):
    count, chans, lanes = x.shape
    width = k_spec.shape[2] // 2
    batch = lanes // width
    tabs = tables(width)
    spec = pltpu.VMEM((batch, count, chans, 2 * width), F32)
    return pl.pallas_call(
        functools.partial(conv_kernel, adjoint),
        out_shape=shape(x.shape, BF16),
        in_specs=[vmem()] * 7,
        out_specs=vmem(),
        scratch_shapes=[spec, spec],
        compiler_params=params(32),
        cost_estimate=cost(x.size * width * 20, x.size * 4 + k_spec.size * 4 + 4 * width * width * 4),
        name="conv_adjoint" if adjoint else "conv_forward",
    )(x, k_spec, skip, *tabs)


def pooled_rows(full):
    span = full.shape[1]
    place = lax.broadcasted_iota(jnp.int32, (1, span), 1)
    before = jnp.where(place == 0, 0.0, pltpu.roll(full, 1, 1))
    after = jnp.where(place == span - 1, 0.0, pltpu.roll(full, span - 1, 1))
    return (before + full + after) / 3.0


def taps_kernel(s_ref, len_ref, fhi, flo, out_ref, raw_ref):
    count, chans, width = s_ref.shape
    full = jnp.concatenate([s_ref[d].astype(F32) for d in range(count)], axis=1)
    place = lax.broadcasted_iota(jnp.int32, (1, count * width), 1)
    kernel = jnp.where(place < len_ref[...], pooled_rows(full), 0.0)
    for d in range(count):
        high, low = split_value(kernel[:, d * width : (d + 1) * width])
        raw_ref[d] = mm(high, fhi[...]) + (mm(low, fhi[...]) + mm(high, flo[...]))
    out_ref[0] = raw_ref[0]
    for d in range(1, count):
        out_ref[d] = wide_quarter(raw_ref[d], raw_ref[d - 1], width)
    if out_ref.shape[0] > count:
        out_ref[count] = wide_quarter(jnp.zeros((chans, 2 * width), F32), raw_ref[count - 1], width)


def taps_call(blocks, lens, token_blocks):
    count, chans, width = blocks.shape
    tabs = tables(width)
    return pl.pallas_call(
        taps_kernel,
        out_shape=shape((min(count + 1, token_blocks), chans, 2 * width), F32),
        in_specs=[vmem()] * 4,
        out_specs=vmem(),
        scratch_shapes=[pltpu.VMEM((count, chans, 2 * width), F32)],
        compiler_params=params(24),
        cost_estimate=cost(blocks.size * width * 12, blocks.size * 10),
        name="taps_spectra",
    )(blocks, lens, tabs[0], tabs[1])


def taps_grad_kernel(x_ref, g_ref, len_ref, fhi, flo, ghi, glo, out_ref, skip_ref, xs_ref, gs_ref, z_ref):
    count, chans, lanes = x_ref.shape
    reach = out_ref.shape[0]
    width = fhi.shape[0]
    batch = lanes // width
    blocks_to_spectra(x_ref, xs_ref, fhi, flo, batch, width)
    blocks_to_spectra(g_ref, gs_ref, fhi, flo, batch, width)
    if small(count, chans, width):

        def step(rows, lane):
            sign = 1 if lane < width // 256 else -1
            total = [None] * reach
            for b in range(batch):
                x = [pair(xs_ref, (b, j), rows, lane, width) for j in range(count)]
                x = [quarter(x[j], x[j - 1] if j else None, sign) for j in range(count)]
                for i in range(count):
                    g = pair(gs_ref, (b, i), rows, lane, width)
                    for d in range(min(i + 1, reach)):
                        total[d] = plus(total[d], times_conj(g, x[i - d]))
            for d in range(reach):
                put_pair(z_ref, (d,), rows, lane, width, total[d])

        tiles(chans, width, step)
        rows = signal_of(z_ref[...].reshape(reach * chans, 2 * width), ghi[...], glo[...])
        rows = rows.reshape(reach, chans, width)
        pieces = [rows[d] for d in range(reach)]
    else:

        def shift(t, c):
            j = count - 1 - t
            for b in range(batch):
                xs_ref[b, j] = wide_quarter(xs_ref[b, j], xs_ref[b, j - 1], width)
            return c

        lax.fori_loop(0, count - 1, shift, 0)

        def lag(d):
            total = jnp.zeros((chans, 2 * width), F32)
            for b in range(batch):

                def term(i, acc, b=b):
                    return acc + wide_times(gs_ref[b, i], xs_ref[b, i - d], width, True)

                total = lax.fori_loop(d, count, term, total)
            z_ref[d] = total

        each(reach, lag, False)
        pieces = [signal_of(z_ref[d], ghi[...], glo[...]) for d in range(reach)]
    full = jnp.concatenate(pieces, axis=1)
    place = lax.broadcasted_iota(jnp.int32, (1, reach * width), 1)
    full = pooled_rows(jnp.where(place < len_ref[...], full, 0.0))
    for d in range(reach):
        out_ref[d] = full[:, d * width : (d + 1) * width].astype(BF16)
    dot = jnp.zeros((chans, lanes), F32)
    for j in range(count):
        dot = dot + x_ref[j].astype(F32) * g_ref[j].astype(F32)
    skip_ref[...] = jnp.sum(dot, axis=1, keepdims=True)


def taps_grad_call(x, g, lens, width, reach):
    count, chans, lanes = x.shape
    batch = lanes // width
    tabs = tables(width)
    spec = pltpu.VMEM((batch, count, chans, 2 * width), F32)
    return pl.pallas_call(
        taps_grad_kernel,
        out_shape=(shape((reach, chans, width), BF16), shape((chans, 1), F32)),
        in_specs=[vmem()] * 7,
        out_specs=(vmem(), vmem()),
        scratch_shapes=[spec, spec, pltpu.VMEM((reach, chans, 2 * width), F32)],
        compiler_params=params(32),
        cost_estimate=cost(x.size * width * 20, x.size * 6),
        name="taps_gradient",
    )(x, g, lens, *tabs)


def normalized(values):
    centred = values - jnp.mean(values, axis=-1, keepdims=True)
    rate = lax.rsqrt(jnp.mean(centred * centred, axis=-1, keepdims=True) + NORM_EPS)
    return centred * rate, rate


def live_rows(offs_ref, batch, tok_rows, rows):
    row = lax.broadcasted_iota(jnp.int32, (rows, 1), 0)
    limit = jnp.zeros((rows, 1), jnp.int32)
    base = lax.axis_index("freq") * tok_rows
    position = base + row
    for b in range(batch):
        inside = jnp.logical_and(row >= b * tok_rows, row < (b + 1) * tok_rows)
        limit = jnp.where(inside, offs_ref[b] + b * tok_rows, limit)
    return position >= limit


def front_kernel(batch, tok_rows, offs_ref, tok, gain, bias, wv, wg, ws, bv, bg, bs, normed, mixed, value, gate, second):
    rows = tok.shape[0]

    @pl.when(pl.program_id(0) == 0)
    def _():
        n, _ = normalized(tok[...].astype(F32))
        normed[...] = (n * gain[...] + bias[...]).astype(BF16)

    x = normed[...]
    v = mm(x, wv[...]) + bv[...]
    g = mm(x, wg[...]) + bg[...]
    live = live_rows(offs_ref, batch, tok_rows, rows)
    mixed[...] = jnp.where(live, g * v, 0.0).T.astype(BF16)
    value[...] = jnp.where(live, v, 0.0).astype(BF16)
    gate[...] = jnp.where(live, g, 0.0).astype(BF16)
    second[...] = (mm(x, ws[...]) + bs[...]).astype(BF16)


def front_call(tok, offsets, gain, bias, weight, in_bias, batch, tok_rows):
    rows, width = tok.shape
    cut = 256
    per = width // cut

    def full(i):
        return (0, 0)

    def col(part):
        return lambda i: (0, part * per + i)

    act = shape((rows, width), BF16)
    return pl.pallas_call(
        functools.partial(front_kernel, batch, tok_rows),
        grid=(per,),
        out_shape=(act, shape((width, rows), BF16), act, act, act),
        in_specs=[smem(), pl.BlockSpec((rows, width), full), pl.BlockSpec((1, width), full), pl.BlockSpec((1, width), full)]
        + [pl.BlockSpec((width, cut), col(k)) for k in range(3)]
        + [pl.BlockSpec((1, cut), col(k)) for k in range(3)],
        out_specs=(
            pl.BlockSpec((rows, width), full),
            pl.BlockSpec((cut, rows), lambda i: (i, 0)),
            pl.BlockSpec((rows, cut), lambda i: (0, i)),
            pl.BlockSpec((rows, cut), lambda i: (0, i)),
            pl.BlockSpec((rows, cut), lambda i: (0, i)),
        ),
        compiler_params=params(32, 1),
        cost_estimate=cost(2 * rows * width * 3 * width, weight.size * 2 + rows * width * 12),
        name="norm_project",
    )(offsets, tok, gain, bias, weight, weight, weight, in_bias, in_bias, in_bias)


def gelu_parts(h):
    square = h * h
    t = jnp.tanh(GELU_C * h * (1.0 + GELU_A * square))
    half = 0.5 + 0.5 * t
    slope = half + (0.5 * GELU_C) * h * (1.0 - t * t) * (1.0 + (3.0 * GELU_A) * square)
    return h * half, slope


def mlp_kernel(paired, tok, convt, second, wo, ob, gain, bias, wup, b1, wdown, cot, *outs):
    gated, conv, res, n2t, act = outs[:5]
    hidden_outs, b1g, n2 = outs[5:-2], outs[-2], outs[-1]

    @pl.when(pl.program_id(0) == 0)
    def _():
        c = convt[...].astype(F32).T
        conv[...] = c.astype(BF16)
        g = (second[...].astype(F32) * c).astype(BF16)
        gated[...] = g
        r = tok[...].astype(F32) + (mm(g, wo[...]) + ob[...])
        res[...] = r
        n, _ = normalized(r)
        m = n * gain[...] + bias[...]
        n2[...] = m.astype(BF16)
        n2t[...] = m.T.astype(BF16)

    h = mm(n2[...], wup[...]) + b1[...]
    ag = mm(cot[...], wdown[...], NT)
    a, slope = gelu_parts(h)
    act[...] = a.astype(BF16)
    hg = (ag * slope).astype(BF16)
    b1g[...] = jnp.sum(hg.astype(F32), axis=0, keepdims=True)
    if not paired:
        hidden_outs[0][...] = hg
        return
    half = hg.shape[1] // 2
    mine, other = hidden_outs
    core = lax.rem(lax.axis_index("freq"), 2)

    @pl.when(core == 0)
    def _():
        mine[...] = hg[:, :half]
        other[...] = hg[:, half:]

    @pl.when(core == 1)
    def _():
        mine[...] = hg[:, half:]
        other[...] = hg[:, :half]


def mlp_call(tok, convt, second, wo, ob, gain, bias, wup, b1, wdown, cot, cut, paired):
    rows, width = tok.shape
    ff = wup.shape[1]

    def full(i):
        return (0, 0)

    def along(i):
        return (0, i)

    token = pl.BlockSpec((rows, width), full)
    vec = pl.BlockSpec((1, width), full)
    act = shape((rows, width), BF16)
    hidden = [shape((rows, ff // 2), BF16)] * 2 if paired else [shape((rows, ff), BF16)]
    hcut = cut // 2 if paired else cut
    return pl.pallas_call(
        functools.partial(mlp_kernel, paired),
        grid=(ff // cut,),
        out_shape=(act, act, shape((rows, width), F32), shape((width, rows), BF16), shape((rows, ff), BF16), *hidden, shape((1, ff), F32)),
        in_specs=[
            token,
            pl.BlockSpec((width, rows), full),
            token,
            pl.BlockSpec((width, width), full),
            vec,
            vec,
            vec,
            pl.BlockSpec((width, cut), along),
            pl.BlockSpec((1, cut), along),
            pl.BlockSpec((cut, width), lambda i: (i, 0)),
            token,
        ],
        out_specs=(
            token,
            token,
            token,
            pl.BlockSpec((width, rows), full),
            pl.BlockSpec((rows, cut), along),
            *[pl.BlockSpec((rows, hcut), along) for _ in hidden],
            pl.BlockSpec((1, cut), along),
        ),
        scratch_shapes=[pltpu.VMEM((rows, width), BF16)],
        compiler_params=params(48, 1),
        cost_estimate=cost(2 * rows * width * (2 * ff + width), wup.size * 4 + rows * ff * 4 + rows * width * 14, rows * ff),
        name="mix_out_mlp",
    )(tok, convt, second, wo, ob, gain, bias, wup, b1, wdown, cot)


def mlp_back_kernel(paired, freq_parts, *refs):
    hidden, rest = refs[: 2 if paired else 1], refs[2 if paired else 1 :]
    wup, res, gain, cot, wo, second, conv = rest[:7]
    rgrad, convgt, sgrad, brt_mine, brt_other, sgt_mine, sgt_other, vecs, acc = rest[7:]
    step = pl.program_id(0)
    core = lax.rem(lax.axis_index("freq"), 2)
    if paired:
        first = jnp.where(core == 0, hidden[0][...], hidden[1][...])
        later = jnp.where(core == 0, hidden[1][...], hidden[0][...])
        hg = jnp.concatenate([first, later], axis=1)
    else:
        hg = hidden[0][...]
    part = mm(hg, wup[...], NT)

    @pl.when(step == 0)
    def _():
        acc[...] = part

    @pl.when(step > 0)
    def _():
        acc[...] += part

    @pl.when(step == pl.num_programs(0) - 1)
    def _():
        ng = acc[...]
        n, rate = normalized(res[...])
        e = ng * gain[...]
        pulled = e - jnp.mean(e, axis=-1, keepdims=True) - n * jnp.mean(e * n, axis=-1, keepdims=True)
        r = cot[...].astype(F32) + rate * pulled
        rgrad[...] = r
        br = r.astype(BF16)
        brf = br.astype(F32)
        gg = mm(br, wo[...], NT)
        convgt[...] = (gg * second[...].astype(F32)).T.astype(BF16)
        sg = (gg * conv[...].astype(F32)).astype(BF16)
        sgrad[...] = sg
        sgf = sg.astype(F32)
        vecs[0:1] = jnp.sum(ng * n, axis=0, keepdims=True)
        vecs[1:2] = jnp.sum(ng, axis=0, keepdims=True)
        vecs[2:3] = jnp.sum(brf, axis=0, keepdims=True)
        vecs[3:4] = jnp.sum(sgf, axis=0, keepdims=True)
        put_halves(brf.T.astype(BF16), brt_mine, brt_other, core, freq_parts)
        put_halves(sgf.T.astype(BF16), sgt_mine, sgt_other, core, freq_parts)


def put_halves(value, mine, other, core, freq_parts):
    per = value.shape[0] // freq_parts
    even = [value[(2 * k) * per : (2 * k + 1) * per] for k in range(freq_parts // 2)]
    odd = [value[(2 * k + 1) * per : (2 * k + 2) * per] for k in range(freq_parts // 2)]

    def put(ref, blocks):
        for k, block in enumerate(blocks):
            ref[k * per : (k + 1) * per] = block

    @pl.when(core == 0)
    def _():
        put(mine, even)
        put(other, odd)

    @pl.when(core == 1)
    def _():
        put(mine, odd)
        put(other, even)


def mlp_back_call(hidden, wup, res, gain, cot, wo, second, conv, cut, paired, freq_parts):
    rows, width = res.shape
    ff = wup.shape[1]

    def full(i):
        return (0, 0)

    def along(i):
        return (0, i)

    token = pl.BlockSpec((rows, width), full)
    half = shape((width // 2, rows), BF16)
    half_spec = pl.BlockSpec((width // 2, rows), full)
    hcut = cut // 2 if paired else cut
    return pl.pallas_call(
        functools.partial(mlp_back_kernel, paired, freq_parts),
        grid=(ff // cut,),
        out_shape=(shape((rows, width), F32), shape((width, rows), BF16), shape((rows, width), BF16), half, half, half, half, shape((8, width), F32)),
        in_specs=[pl.BlockSpec((rows, hcut), along) for _ in hidden]
        + [pl.BlockSpec((width, cut), along), token, pl.BlockSpec((1, width), full), token, pl.BlockSpec((width, width), full), token, token],
        out_specs=(token, pl.BlockSpec((width, rows), full), token, half_spec, half_spec, half_spec, half_spec, pl.BlockSpec((8, width), full)),
        scratch_shapes=[pltpu.VMEM((rows, width), F32)],
        compiler_params=params(40, 1),
        cost_estimate=cost(2 * rows * width * (ff + width), wup.size * 2 + rows * ff * 2 + rows * width * 20),
        name="mlp_back",
    )(*hidden, wup, res, gain, cot, wo, second, conv)


def block_out_kernel(act, wdown, res, b2, cot, out, b2g, acc):
    step = pl.program_id(0)
    part = mm(act[...], wdown[...])

    @pl.when(step == 0)
    def _():
        acc[...] = res[...] + b2[...] + part
        b2g[...] = jnp.sum(cot[...].astype(F32), axis=0, keepdims=True)

    @pl.when(step > 0)
    def _():
        acc[...] += part

    @pl.when(step == pl.num_programs(0) - 1)
    def _():
        out[...] = acc[...].astype(BF16)


def block_out_call(act, wdown, res, b2, cot, cut):
    rows, width = res.shape
    ff = act.shape[1]

    def full(i):
        return (0, 0)

    token = pl.BlockSpec((rows, width), full)
    vec = pl.BlockSpec((1, width), full)
    return pl.pallas_call(
        block_out_kernel,
        grid=(ff // cut,),
        out_shape=(shape((rows, width), BF16), shape((1, width), F32)),
        in_specs=[pl.BlockSpec((rows, cut), lambda i: (0, i)), pl.BlockSpec((cut, width), lambda i: (i, 0)), token, vec, token],
        out_specs=(token, vec),
        scratch_shapes=[pltpu.VMEM((rows, width), F32)],
        compiler_params=params(24, 1),
        cost_estimate=cost(2 * rows * width * ff, wdown.size * 2 + rows * ff * 2 + rows * width * 8),
        name="block_out",
    )(act, wdown, res, b2, cot)


def back_kernel(freq_parts, mgt, value, gate, sgrad, weight, tok, gain, rgrad, out, v_mine, v_other, g_mine, g_other, vecs, mg, acc):
    step = pl.program_id(0)
    core = lax.rem(lax.axis_index("freq"), 2)

    @pl.when(step == 0)
    def _():
        m = mgt[...].astype(F32).T
        mg[...] = m.astype(BF16)
        acc[...] = mm(sgrad[...], weight[...], NT)

    @pl.when(step == 1)
    def _():
        pv = (gate[...].astype(F32) * mg[...].astype(F32)).astype(BF16)
        acc[...] += mm(pv, weight[...], NT)
        pf = pv.astype(F32)
        vecs[2:3] = jnp.sum(pf, axis=0, keepdims=True)
        put_halves(pf.T.astype(BF16), v_mine, v_other, core, freq_parts)

    @pl.when(step == 2)
    def _():
        pg = (value[...].astype(F32) * mg[...].astype(F32)).astype(BF16)
        ng = acc[...] + mm(pg, weight[...], NT)
        pf = pg.astype(F32)
        vecs[3:4] = jnp.sum(pf, axis=0, keepdims=True)
        put_halves(pf.T.astype(BF16), g_mine, g_other, core, freq_parts)
        n, rate = normalized(tok[...].astype(F32))
        vecs[0:1] = jnp.sum(ng * n, axis=0, keepdims=True)
        vecs[1:2] = jnp.sum(ng, axis=0, keepdims=True)
        e = ng * gain[...]
        pulled = e - jnp.mean(e, axis=-1, keepdims=True) - n * jnp.mean(e * n, axis=-1, keepdims=True)
        out[...] = (rgrad[...] + rate * pulled).astype(BF16)


def back_call(mgt, value, gate, sgrad, weight, tok, gain, rgrad, freq_parts):
    rows, width = tok.shape

    def full(i):
        return (0, 0)

    token = pl.BlockSpec((rows, width), full)
    half = shape((width // 2, rows), BF16)
    half_spec = pl.BlockSpec((width // 2, rows), full)
    return pl.pallas_call(
        functools.partial(back_kernel, freq_parts),
        grid=(3,),
        out_shape=(shape((rows, width), BF16), half, half, half, half, shape((8, width), F32)),
        in_specs=[
            pl.BlockSpec((width, rows), full),
            token,
            token,
            token,
            pl.BlockSpec((width, width), lambda i: (0, lax.rem(i + 2, 3))),
            token,
            pl.BlockSpec((1, width), full),
            token,
        ],
        out_specs=(token, half_spec, half_spec, half_spec, half_spec, pl.BlockSpec((8, width), full)),
        scratch_shapes=[pltpu.VMEM((rows, width), BF16), pltpu.VMEM((rows, width), F32)],
        compiler_params=params(32, 1),
        cost_estimate=cost(2 * rows * width * width * 3, weight.size * 2 + rows * width * 16),
        name="project_back",
    )(mgt, value, gate, sgrad, weight, tok, gain, rgrad)


def bit_order(chips, low_first):
    bits = list(range(chips.bit_length() - 1))
    return bits if low_first else bits[::-1]


def place_of(rel, order):
    place = 0
    for level, bit in enumerate(order):
        digit = lax.shift_right_logical(rel, bit) & 1
        place = place + digit * (1 << (len(order) - 1 - level))
    return place


def store_slot(keep, send, place, index, block):
    half = keep.shape[0]

    @pl.when(place < half)
    def _():
        keep[(place,) + index] = block

    @pl.when(place >= half)
    def _():
        send[(place - half,) + index] = block


def rows_kernel(chips, per, order, count, *refs):
    ins, (keep, send) = refs[: 4 * count], refs[4 * count :]
    chip = lax.axis_index("freq") // 2
    for p in range(count):
        lt, rt, ltp, rtp = ins[4 * p : 4 * p + 4]
        total = (mm(lt[...], rt[...]) + mm(ltp[...], rtp[...])).astype(BF16)
        for k in range(chips):
            place = place_of(jnp.int32(k) ^ chip, order)
            store_slot(keep, send, place, (slice(p * per, (p + 1) * per), slice(None)), total[k * per : (k + 1) * per])


def rows_pair(problems, chips, low_first, cut):
    order = bit_order(chips, low_first)
    rows, inner = problems[0][0].shape
    width = problems[0][1].shape[1]
    per = rows // chips
    if per % 16 or chips < 2:
        blocks = []
        for lt, rt, ltp, rtp in problems:
            blocks.append((mm(lt, rt) + mm(ltp, rtp)).astype(BF16).reshape(chips, per, width))
        return halves_of(jnp.concatenate(blocks, axis=1), order)
    count = len(problems)
    out = shape((chips // 2, count * per, width), BF16)
    out_spec = pl.BlockSpec((chips // 2, count * per, cut), lambda i: (0, 0, i))
    left = pl.BlockSpec((rows, inner), lambda i: (0, 0))
    right = pl.BlockSpec((inner, cut), lambda i: (0, i))
    return pl.pallas_call(
        functools.partial(rows_kernel, chips, per, order, count),
        grid=(width // cut,),
        out_shape=(out, out),
        in_specs=[left, right, left, right] * count,
        out_specs=(out_spec, out_spec),
        compiler_params=params(32, 1),
        cost_estimate=cost(4 * count * rows * inner * width, count * (rows * inner + inner * width + rows * width) * 4),
        name="row_gradients",
    )(*[x for problem in problems for x in problem])


def halves_of(blocks, order):
    chips = blocks.shape[0]
    chip = lax.axis_index("freq") // 2
    picks = np.zeros(chips, np.int32)
    for rel in range(chips):
        place = sum(((rel >> bit) & 1) << (len(order) - 1 - level) for level, bit in enumerate(order))
        picks[place] = rel
    moved = jnp.take(blocks, jnp.asarray(picks) ^ chip, axis=0)
    return moved[: chips // 2], moved[chips // 2 :]


def cols_kernel(order, lt, rt, ltp, rtp, keep, send):
    chip = lax.axis_index("freq") // 2
    total = (mm(lt[...], rt[...]) + mm(ltp[...], rtp[...])).astype(BF16)
    store_slot(keep, send, place_of(pl.program_id(0) ^ chip, order), (), total)


def cols_pair(lt, rt, ltp, rtp, chips, low_first):
    order = bit_order(chips, low_first)
    rows, inner = lt.shape
    per = rt.shape[1] // chips
    if per % 128 or chips < 2:
        total = (mm(lt, rt) + mm(ltp, rtp)).astype(BF16)
        return halves_of(total.reshape(rows, chips, per).transpose(1, 0, 2), order)
    out = shape((chips // 2, rows, per), BF16)
    out_spec = pl.BlockSpec((chips // 2, rows, per), lambda i: (0, 0, 0))
    left = pl.BlockSpec((rows, inner), lambda i: (0, 0))
    right = pl.BlockSpec((inner, per), lambda i: (0, i))
    return pl.pallas_call(
        functools.partial(cols_kernel, order),
        grid=(chips,),
        out_shape=(out, out),
        in_specs=[left, right, left, right],
        out_specs=(out_spec, out_spec),
        compiler_params=params(32, 1),
        cost_estimate=cost(4 * rows * inner * rt.shape[1], (rows * inner + inner * rt.shape[1] * 2) * 4),
        name="column_gradients",
    )(lt, rt, ltp, rtp)


def flip(value, freq_parts, bit):
    return lax.ppermute(value, "freq", [(i, i ^ bit) for i in range(freq_parts)])


def halving(keep, send, freq_parts, low_first):
    order = bit_order(freq_parts // 2, low_first)
    for level, bit in enumerate(order):
        got = flip(send, freq_parts, 2 << bit)
        total = keep.astype(F32) + got.astype(F32)
        if level == len(order) - 1:
            return total[0]
        half = total.shape[0] // 2
        keep, send = total[:half].astype(BF16), total[half:].astype(BF16)


def across(blocks):
    got = lax.all_to_all(blocks.astype(BF16), "dp", split_axis=0, concat_axis=0, tiled=True)
    return jnp.sum(got.astype(F32), axis=0)


def everywhere(rows):
    dp, freq = lax.axis_size("dp"), lax.axis_size("freq")
    wide = jnp.broadcast_to(rows[None], (dp,) + rows.shape).reshape(dp * freq, 1, rows.shape[1])
    got = lax.all_to_all(wide, ("dp", "freq"), split_axis=0, concat_axis=0, tiled=True)
    return jnp.sum(got, axis=(0, 1))


def reblocked(blocks, count, width):
    if blocks.shape[0] == count and blocks.shape[2] == width:
        return blocks
    whole = blocks.transpose(1, 0, 2).reshape(blocks.shape[1], -1)
    need = count * width
    whole = jnp.pad(whole, ((0, 0), (0, max(0, need - whole.shape[1]))))[:, :need]
    return whole.reshape(-1, count, width).transpose(1, 0, 2)


def body(tokens, offsets, kernel_lengths, norm1_gain, norm1_bias, w_in, in_bias, kernel_taps, skip_gain, w_out, out_bias, norm2_gain, norm2_bias, w_up, fc1_bias, w_down, fc2_bias, cotangent):
    freq = lax.axis_size("freq")
    dp = lax.axis_size("dp")
    chips = freq // 2
    batch, tok_rows, width = tokens.shape
    rows = batch * tok_rows
    ff = w_up.shape[1]
    chans = width // freq
    me = lax.axis_index("freq")
    core = lax.rem(me, 2)

    def row(v):
        return v.reshape(1, -1)

    tok = tokens.reshape(rows, width)
    cot = cotangent.reshape(rows, width)
    shrunk = (kernel_taps - SHRINK * jnp.tanh(kernel_taps / SHRINK)).astype(BF16)
    tap_rows = shrunk.shape[1]
    shrunk = lax.all_to_all(shrunk.reshape(freq, chans, tap_rows), "freq", split_axis=0, concat_axis=0, tiled=True)
    reach = -(-freq * tap_rows // tok_rows)
    shrunk = reblocked(shrunk, reach, tok_rows)
    lens = lax.dynamic_slice_in_dim(kernel_lengths, me * chans, chans).reshape(chans, 1)
    normed, mixed_t, value, gate, second = front_call(tok, offsets, row(norm1_gain), row(norm1_bias), w_in, row(in_bias), batch, tok_rows)
    mixed = lax.all_to_all(mixed_t.reshape(freq, chans, rows), "freq", split_axis=0, concat_axis=0, tiled=True)
    k_spec = taps_call(shrunk, lens, freq)
    skip = skip_gain.reshape(chans, 1)
    conv = conv_call(mixed, k_spec, skip, False)
    conv_t = lax.all_to_all(conv, "freq", split_axis=0, concat_axis=0, tiled=True).reshape(width, rows)
    cut = 768
    paired = (ff // freq) % 128 == 0 and 2 * (ff // freq) == cut
    outs = mlp_call(tok, conv_t, second, w_out, row(out_bias), row(norm2_gain), row(norm2_bias), w_up, row(fc1_bias), w_down, cot, cut, paired)
    gated, conv_tok, res, n2t, act = outs[:5]
    hidden, b1g = outs[5:-1], outs[-1]
    rgrad, convg_t, sgrad, br_mine, br_other, sg_mine, sg_other, vec_two = mlp_back_call(
        hidden, w_up, res, row(norm2_gain), cot, w_out, second, conv_tok, cut, paired, freq
    )
    convg = lax.all_to_all(convg_t.reshape(freq, chans, rows), "freq", split_axis=0, concat_axis=0, tiled=True)
    if paired:
        hg_mine, hg_other = hidden
    else:
        split = hidden[0].reshape(rows, chips, 2, ff // freq)
        hg_mine = jnp.take(split, core, axis=2).reshape(rows, ff // 2)
        hg_other = jnp.take(split, 1 - core, axis=2).reshape(rows, ff // 2)
    cot_t = cot.T.reshape(chips, 2, chans, rows)
    cot_mine = jnp.take(cot_t, core, axis=1).reshape(width // 2, rows)
    cot_other = jnp.take(cot_t, 1 - core, axis=1).reshape(width // 2, rows)

    def swap(v):
        return flip(v, freq, 1)

    normed_p, gated_p, n2t_p, act_p = swap(normed), swap(gated), swap(n2t), swap(act)
    fc2 = rows_pair([(cot_mine, act, swap(cot_other), act_p)], chips, True, 768)
    fc1 = cols_pair(n2t, hg_mine, n2t_p, swap(hg_other), chips, False)
    mixer = rows_pair([(br_mine, gated, swap(br_other), gated_p), (sg_mine, normed, swap(sg_other), normed_p)], chips, True, 384)
    block_out, b2g = block_out_call(act, w_down, res, row(fc2_bias), cot, cut)
    mixed_grad = conv_call(convg, k_spec, skip, True)
    mixed_grad_t = lax.all_to_all(mixed_grad, "freq", split_axis=0, concat_axis=0, tiled=True).reshape(width, rows)
    taps_g, skip_g = taps_grad_call(mixed, convg, lens, tok_rows, reach)
    taps_g = reblocked(taps_g, freq, tap_rows)
    taps_g = lax.all_to_all(taps_g, "freq", split_axis=0, concat_axis=0, tiled=True).reshape(width, tap_rows)
    taps_g = taps_g.astype(F32) * jnp.square(jnp.tanh(kernel_taps / SHRINK))
    taps_final = lax.psum(taps_g.astype(BF16), "dp").astype(F32)
    fc2 = halving(*fc2, freq, True)
    fc2_final = across(fc2.reshape(chans, dp, ff // dp).transpose(1, 0, 2)).T
    fc1 = halving(*fc1, freq, False)
    fc1_final = across(fc1.reshape(dp, width // dp, ff // freq))
    mixer = halving(*mixer, freq, True)
    input_grad, v_mine, v_other, g_mine, g_other, vec_one = back_call(mixed_grad_t, value, gate, sgrad, w_in, tok, row(norm1_gain), rgrad, freq)
    gates = rows_pair([(v_mine, normed, swap(v_other), normed_p), (g_mine, normed, swap(g_other), normed_p)], chips, False, 384)
    gates = halving(*gates, freq, False)
    split = jnp.concatenate([mixer, gates], axis=0).reshape(4 * chans, dp, width // dp).transpose(1, 0, 2)
    late = across(split)
    out_final = late[:chans].T
    parts = jnp.stack([late[2 * chans : 3 * chans], late[3 * chans :], late[chans : 2 * chans]]).astype(BF16)
    pieces = []
    for r in range(3):
        part = lax.rem((freq % 3) * (r - me + 3 * freq), 3)
        piece = lax.dynamic_index_in_dim(parts, part, 0, keepdims=False)
        pieces.append(lax.ppermute(piece, "freq", [((3 * d + r) % freq, d) for d in range(freq)]))
    in_final = jnp.concatenate(pieces, axis=0).T.astype(F32)
    early = everywhere(
        jnp.concatenate([b1g.reshape(freq, -1), b2g.reshape(freq, -1)] + [vec_two[k].reshape(freq, -1) for k in range(3)], axis=1)
    )
    own = (jnp.arange(freq, dtype=jnp.int32) == me).astype(F32)[:, None] * skip_g.reshape(1, chans)
    bias_in = jnp.concatenate([vec_one[2], vec_one[3], vec_two[3]]).reshape(freq, -1)
    final = everywhere(jnp.concatenate([vec_one[0].reshape(freq, -1), vec_one[1].reshape(freq, -1), bias_in, own], axis=1))
    fa = ff // freq
    n1g, n1b, inb, skg = final[:chans], final[chans : 2 * chans], final[2 * chans : 5 * chans], final[5 * chans :]
    b1f, b2f = early[:fa], early[fa : fa + chans]
    n2g, n2b, outb = (early[fa + k * chans : fa + (k + 1) * chans] for k in (1, 2, 3))
    return (
        block_out.reshape(tokens.shape),
        input_grad.reshape(tokens.shape),
        n1g,
        n1b,
        in_final,
        inb,
        taps_final,
        skg,
        out_final,
        outb,
        n2g,
        n2b,
        fc1_final,
        b1f,
        fc2_final,
        b2f,
    )


def solution(mesh):
    token, whole, lead = P("dp", "freq", None), P(), P("freq")
    both = P("dp", "freq")
    in_specs = (token, P("dp"), whole, whole, whole, whole, whole, P(None, "freq"), lead) + (whole,) * 8 + (token,)
    out_specs = (token, token, lead, lead, both, lead, P(None, "freq"), lead, both, lead, lead, lead, both, lead, both, lead)
    return jax.shard_map(body, mesh=mesh, in_specs=in_specs, out_specs=out_specs, check_vma=False)
```

```python
import functools

import jax
import jax.numpy as jnp
import numpy as np
from jax import lax
from jax.experimental import pallas as pl
from jax.experimental.pallas import tpu as pltpu
from jax.sharding import PartitionSpec as P

NORM_EPS = 1e-05
SHRINK = 0.003
GELU_C = 0.7978845608028654
GELU_A = 0.044715
F32 = jnp.float32
BF16 = jnp.bfloat16
MIB = 1 << 20

NN = (((1,), (0,)), ((), ()))
NT = (((1,), (1,)), ((), ()))


def mm(left, right, dims=NN):
    return lax.dot_general(left, right, dims, preferred_element_type=F32)


def whole(dims):
    return pl.BlockSpec(tuple(dims), lambda i: (0,) * len(dims))


def anywhere():
    return pl.BlockSpec(memory_space=pl.ANY)


def smem():
    return pl.BlockSpec(memory_space=pltpu.SMEM)


def shape(dims, dtype):
    return jax.ShapeDtypeStruct(dims, dtype)


def launch(kernel, grid, ins, in_specs, outs, out_specs, scratch, estimate, name, after=(), carry=()):
    count, extra, given = len(ins), len(after) + len(carry), len(outs)

    def run(*refs):
        made = refs[count + extra : count + extra + given]
        kernel(*refs[:count], *made, *refs[count + extra + given + len(carry) :])

    first = count + len(after)
    results = pl.pallas_call(
        run,
        grid=grid,
        out_shape=tuple(outs) + tuple(shape(v.shape, v.dtype) for v in carry),
        in_specs=list(in_specs) + [anywhere()] * extra,
        out_specs=tuple(out_specs) + (anywhere(),) * len(carry),
        scratch_shapes=scratch,
        input_output_aliases={first + k: given + k for k in range(len(carry))},
        compiler_params=pltpu.CompilerParams(vmem_limit_bytes=60 * MIB, dimension_semantics=("arbitrary",)),
        cost_estimate=estimate,
        name=name,
    )(*ins, *after, *carry)
    made = results[0] if given == 1 else results[:given]
    return (made, results[given:]) if carry else made


def cost(flops, moved, special=0):
    return pl.CostEstimate(flops=int(flops) * 64, bytes_accessed=int(moved) * 64, transcendentals=0)


def split16(table):
    high = np.asarray(table, np.float32).astype(jnp.bfloat16)
    low = (np.asarray(table, np.float64) - high.astype(np.float64)).astype(np.float32).astype(jnp.bfloat16)
    return high, low


@functools.lru_cache(maxsize=None)
def tables(width):
    order = np.concatenate([np.arange(0, width, 2), np.arange(1, width, 2)])
    turns = (2 * order[None, :] + 1) * np.arange(width)[:, None] % (4 * width)
    angle = np.pi * turns / (2 * width)
    forward = np.concatenate([np.cos(angle), -np.sin(angle)], axis=1)
    inverse = forward.T / width
    return split16(forward) + split16(inverse)


def split_value(value):
    high = value.astype(BF16)
    return high, (value - high.astype(F32)).astype(BF16)


def spectrum_of(block, fhi, flo):
    return mm(block, fhi) + mm(block, flo)


def signal_of(spec, ghi, glo):
    high, low = split_value(spec)
    return mm(high, ghi) + (mm(low, ghi) + mm(high, glo))


def each(count, step, unroll):
    if unroll:
        for i in range(count):
            step(i)
    else:
        lax.fori_loop(0, count, lambda i, c: (step(i), c)[1], 0)


def blocks_to_spectra(x_ref, spec_ref, fhi, flo, batch, width):
    count, chans = x_ref.shape[0], x_ref.shape[1]
    for b in range(batch):
        lanes = slice(b * width, (b + 1) * width)
        if chans % 16 == 0:
            rows = x_ref[:, :, lanes].reshape(count * chans, width)
            spec_ref[b] = spectrum_of(rows, fhi[...], flo[...]).reshape(count, chans, 2 * width)
        else:

            def step(j, b=b, lanes=lanes):
                spec_ref[b, j] = spectrum_of(x_ref[j, :, lanes], fhi[...], flo[...])

            each(count, step, False)


def tiles(chans, width, step):
    lane_tiles = width // 128

    def rows_step(rt):
        start = rt * 8 if isinstance(rt, int) else pl.multiple_of(rt * 8, 8)
        for lane in range(lane_tiles):
            step(pl.ds(start, 8), lane)

    each(chans // 8, rows_step, False)


def pair(ref, lead, rows, lane, width):
    return (
        ref[lead + (rows, slice(lane * 128, (lane + 1) * 128))],
        ref[lead + (rows, slice(width + lane * 128, width + (lane + 1) * 128))],
    )


def put_pair(ref, lead, rows, lane, width, value):
    ref[lead + (rows, slice(lane * 128, (lane + 1) * 128))] = value[0]
    ref[lead + (rows, slice(width + lane * 128, width + (lane + 1) * 128))] = value[1]


def times(a, k):
    return a[0] * k[0] - a[1] * k[1], a[0] * k[1] + a[1] * k[0]


def times_conj(a, k):
    return a[0] * k[0] + a[1] * k[1], a[1] * k[0] - a[0] * k[1]


def plus(a, b):
    return b if a is None else (a[0] + b[0], a[1] + b[1])


def quarter(now, before, sign):
    if before is None:
        return now
    if sign > 0:
        return now[0] - before[1], now[1] + before[0]
    return now[0] + before[1], now[1] - before[0]


def wide_quarter(now, before, width):
    lane = lax.broadcasted_iota(jnp.int32, (1, width), 1)
    sign = jnp.where(lane < width // 2, 1.0, -1.0)
    return jnp.concatenate(
        [now[:, :width] - sign * before[:, width:], now[:, width:] + sign * before[:, :width]], axis=1
    )


def wide_times(a, k, width, conj):
    ar, ai, kr, ki = a[:, :width], a[:, width:], k[:, :width], k[:, width:]
    if conj:
        return jnp.concatenate([ar * kr + ai * ki, ai * kr - ar * ki], axis=1)
    return jnp.concatenate([ar * kr - ai * ki, ar * ki + ai * kr], axis=1)


UNROLLED = 8


def small(count, chans, width):
    return count <= UNROLLED and chans % 16 == 0 and width % 256 == 0


def conv_products(spec_ref, k_ref, z_ref, batch, width, adjoint):
    reach, chans = k_ref.shape[0], k_ref.shape[1]
    count = spec_ref.shape[1]
    if small(count, chans, width):

        def step(rows, lane):
            k = [pair(k_ref, (d,), rows, lane, width) for d in range(reach)]
            for b in range(batch):
                x = [pair(spec_ref, (b, j), rows, lane, width) for j in range(count)]
                for i in range(count):
                    total = None
                    if adjoint:
                        for d in range(min(count - i, reach)):
                            total = plus(total, times_conj(x[i + d], k[d]))
                    else:
                        for d in range(min(i + 1, reach)):
                            total = plus(total, times(x[i - d], k[d]))
                    put_pair(z_ref, (b, i), rows, lane, width, total)

        tiles(chans, width, step)
        return
    for b in range(batch):

        def row(i, b=b):
            def term(d, total):
                src = i + d if adjoint else i - d
                return total + wide_times(spec_ref[b, src], k_ref[d], width, adjoint)

            terms = jnp.minimum(count - i if adjoint else i + 1, reach)
            z_ref[b, i] = lax.fori_loop(0, terms, term, jnp.zeros((chans, 2 * width), F32))

        each(count, row, False)


def conv_kernel(adjoint, x_ref, k_ref, skip_ref, fhi, flo, ghi, glo, out_ref, spec_ref, z_ref):
    count, chans, lanes = x_ref.shape
    width = fhi.shape[0]
    batch = lanes // width
    blocks_to_spectra(x_ref, spec_ref, fhi, flo, batch, width)
    conv_products(spec_ref, k_ref, z_ref, batch, width, adjoint)
    for b in range(batch):
        cut = slice(b * width, (b + 1) * width)
        if chans % 16 == 0:
            y = signal_of(z_ref[b].reshape(count * chans, 2 * width), ghi[...], glo[...])
            y = y.reshape(count, chans, width) + skip_ref[...][None] * x_ref[:, :, cut].astype(F32)
            out_ref[:, :, cut] = y.astype(BF16)
        else:

            def step(j, b=b, cut=cut):
                y = signal_of(z_ref[b, j], ghi[...], glo[...])
                out_ref[j, :, cut] = (y + skip_ref[...] * x_ref[j, :, cut].astype(F32)).astype(BF16)

            each(count, step, False)


def conv_call(x, k_spec, skip, adjoint, after=(), carry=()):
    count, chans, lanes = x.shape
    width = k_spec.shape[2] // 2
    batch = lanes // width
    tabs = tables(width)
    spec = pltpu.VMEM((batch, count, chans, 2 * width), F32)
    return launch(
        functools.partial(conv_kernel, adjoint),
        (1,),
        (x, k_spec, skip, *tabs,),
        [whole(v.shape) for v in (x, k_spec, skip, *tabs)],
        (shape(x.shape, BF16),),
        (whole(x.shape),),
        [spec, spec],
        cost(x.size * width * 20, x.size * 4 + k_spec.size * 4 + 4 * width * width * 4),
        "conv_adjoint" if adjoint else "conv_forward",
        after,
        carry,
    )


def pooled_rows(full):
    span = full.shape[1]
    place = lax.broadcasted_iota(jnp.int32, (1, span), 1)
    before = jnp.where(place == 0, 0.0, pltpu.roll(full, 1, 1))
    after = jnp.where(place == span - 1, 0.0, pltpu.roll(full, span - 1, 1))
    return (before + full + after) / 3.0


def taps_kernel(s_ref, len_ref, fhi, flo, out_ref, raw_ref):
    count, chans, width = s_ref.shape
    full = jnp.concatenate([s_ref[d].astype(F32) for d in range(count)], axis=1)
    place = lax.broadcasted_iota(jnp.int32, (1, count * width), 1)
    kernel = jnp.where(place < len_ref[...], pooled_rows(full), 0.0)
    for d in range(count):
        high, low = split_value(kernel[:, d * width : (d + 1) * width])
        raw_ref[d] = mm(high, fhi[...]) + (mm(low, fhi[...]) + mm(high, flo[...]))
    out_ref[0] = raw_ref[0]
    for d in range(1, count):
        out_ref[d] = wide_quarter(raw_ref[d], raw_ref[d - 1], width)
    if out_ref.shape[0] > count:
        out_ref[count] = wide_quarter(jnp.zeros((chans, 2 * width), F32), raw_ref[count - 1], width)


def taps_call(blocks, lens, token_blocks):
    count, chans, width = blocks.shape
    tabs = tables(width)
    return launch(
        taps_kernel,
        (1,),
        (blocks, lens, tabs[0], tabs[1],),
        [whole(v.shape) for v in (blocks, lens, tabs[0], tabs[1])],
        (shape((min(count + 1, token_blocks), chans, 2 * width), F32),),
        (whole((min(count + 1, token_blocks), chans, 2 * width)),),
        [pltpu.VMEM((count, chans, 2 * width), F32)],
        cost(blocks.size * width * 12, blocks.size * 10),
        "taps_spectra",
            )


def taps_grad_kernel(x_ref, g_ref, len_ref, fhi, flo, ghi, glo, out_ref, skip_ref, xs_ref, gs_ref, z_ref):
    count, chans, lanes = x_ref.shape
    reach = out_ref.shape[0]
    width = fhi.shape[0]
    batch = lanes // width
    blocks_to_spectra(x_ref, xs_ref, fhi, flo, batch, width)
    blocks_to_spectra(g_ref, gs_ref, fhi, flo, batch, width)
    if small(count, chans, width):

        def step(rows, lane):
            sign = 1 if lane < width // 256 else -1
            total = [None] * reach
            for b in range(batch):
                x = [pair(xs_ref, (b, j), rows, lane, width) for j in range(count)]
                x = [quarter(x[j], x[j - 1] if j else None, sign) for j in range(count)]
                for i in range(count):
                    g = pair(gs_ref, (b, i), rows, lane, width)
                    for d in range(min(i + 1, reach)):
                        total[d] = plus(total[d], times_conj(g, x[i - d]))
            for d in range(reach):
                put_pair(z_ref, (d,), rows, lane, width, total[d])

        tiles(chans, width, step)
        rows = signal_of(z_ref[...].reshape(reach * chans, 2 * width), ghi[...], glo[...])
        rows = rows.reshape(reach, chans, width)
        pieces = [rows[d] for d in range(reach)]
    else:

        def shift(t, c):
            j = count - 1 - t
            for b in range(batch):
                xs_ref[b, j] = wide_quarter(xs_ref[b, j], xs_ref[b, j - 1], width)
            return c

        lax.fori_loop(0, count - 1, shift, 0)

        def lag(d):
            total = jnp.zeros((chans, 2 * width), F32)
            for b in range(batch):

                def term(i, acc, b=b):
                    return acc + wide_times(gs_ref[b, i], xs_ref[b, i - d], width, True)

                total = lax.fori_loop(d, count, term, total)
            z_ref[d] = total

        each(reach, lag, False)
        pieces = [signal_of(z_ref[d], ghi[...], glo[...]) for d in range(reach)]
    full = jnp.concatenate(pieces, axis=1)
    place = lax.broadcasted_iota(jnp.int32, (1, reach * width), 1)
    full = pooled_rows(jnp.where(place < len_ref[...], full, 0.0))
    for d in range(reach):
        out_ref[d] = full[:, d * width : (d + 1) * width].astype(BF16)
    dot = jnp.zeros((chans, lanes), F32)
    for j in range(count):
        dot = dot + x_ref[j].astype(F32) * g_ref[j].astype(F32)
    skip_ref[...] = jnp.sum(dot, axis=1, keepdims=True)


def taps_grad_call(x, g, lens, width, reach, after=(), carry=()):
    count, chans, lanes = x.shape
    batch = lanes // width
    tabs = tables(width)
    spec = pltpu.VMEM((batch, count, chans, 2 * width), F32)
    return launch(
        taps_grad_kernel,
        (1,),
        (x, g, lens, *tabs,),
        [whole(v.shape) for v in (x, g, lens, *tabs)],
        (shape((reach, chans, width), BF16), shape((chans, 1), F32)),
        (whole((reach, chans, width)), whole((chans, 1))),
        [spec, spec, pltpu.VMEM((reach, chans, 2 * width), F32)],
        cost(x.size * width * 20, x.size * 6),
        "taps_gradient",
        after,
        carry,
    )


def normalized(values):
    centred = values - jnp.mean(values, axis=-1, keepdims=True)
    rate = lax.rsqrt(jnp.mean(centred * centred, axis=-1, keepdims=True) + NORM_EPS)
    return centred * rate, rate


def live_rows(offs_ref, batch, tok_rows, rows):
    row = lax.broadcasted_iota(jnp.int32, (rows, 1), 0)
    limit = jnp.zeros((rows, 1), jnp.int32)
    base = lax.axis_index("freq") * tok_rows
    position = base + row
    for b in range(batch):
        inside = jnp.logical_and(row >= b * tok_rows, row < (b + 1) * tok_rows)
        limit = jnp.where(inside, offs_ref[b] + b * tok_rows, limit)
    return position >= limit


def front_kernel(batch, tok_rows, offs_ref, tok, gain, bias, wv, wg, ws, bv, bg, bs, normed, mixed, value, gate, second):
    rows = tok.shape[0]

    @pl.when(pl.program_id(0) == 0)
    def _():
        n, _ = normalized(tok[...].astype(F32))
        normed[...] = (n * gain[...] + bias[...]).astype(BF16)

    x = normed[...]
    v = mm(x, wv[...]) + bv[...]
    g = mm(x, wg[...]) + bg[...]
    live = live_rows(offs_ref, batch, tok_rows, rows)
    mixed[...] = jnp.where(live, g * v, 0.0).T.astype(BF16)
    value[...] = jnp.where(live, v, 0.0).astype(BF16)
    gate[...] = jnp.where(live, g, 0.0).astype(BF16)
    second[...] = (mm(x, ws[...]) + bs[...]).astype(BF16)


def front_call(tok, offsets, gain, bias, weight, in_bias, batch, tok_rows):
    rows, width = tok.shape
    cut = 256
    per = width // cut

    def full(i):
        return (0, 0)

    def col(part):
        return lambda i: (0, part * per + i)

    act = shape((rows, width), BF16)
    return launch(
        functools.partial(front_kernel, batch, tok_rows),
        (per,),
        (offsets, tok, gain, bias, weight, weight, weight, in_bias, in_bias, in_bias,),
        [smem(), pl.BlockSpec((rows, width), full), pl.BlockSpec((1, width), full), pl.BlockSpec((1, width), full)]
        + [pl.BlockSpec((width, cut), col(k)) for k in range(3)]
        + [pl.BlockSpec((1, cut), col(k)) for k in range(3)],
        (act, shape((width, rows), BF16), act, act, act),
        (
            pl.BlockSpec((rows, width), full),
            pl.BlockSpec((cut, rows), lambda i: (i, 0)),
            pl.BlockSpec((rows, cut), lambda i: (0, i)),
            pl.BlockSpec((rows, cut), lambda i: (0, i)),
            pl.BlockSpec((rows, cut), lambda i: (0, i)),
        ),
        [],
        cost(2 * rows * width * 3 * width, weight.size * 2 + rows * width * 12),
        "norm_project",
            )


def gelu_parts(h):
    square = h * h
    t = jnp.tanh(GELU_C * h * (1.0 + GELU_A * square))
    half = 0.5 + 0.5 * t
    slope = half + (0.5 * GELU_C) * h * (1.0 - t * t) * (1.0 + (3.0 * GELU_A) * square)
    return h * half, slope


def mlp_kernel(paired, tok, convt, second, wo, ob, gain, bias, wup, b1, wdown, cot, pack, conv, res, b1g, *rest):
    mine, (n2, gn) = rest[:-2], rest[-2:]
    step = pl.program_id(0)
    cut, part = wup.shape[1], gn.shape[2]

    @pl.when(step == 0)
    def _():
        c = convt[...].astype(F32).T
        conv[...] = c.astype(BF16)
        g = (second[...].astype(F32) * c).astype(BF16)
        r = tok[...].astype(F32) + (mm(g, wo[...]) + ob[...])
        res[...] = r
        n, _ = normalized(r)
        m = (n * gain[...] + bias[...]).astype(BF16)
        n2[...] = m
        both = [g, m]
        for k in range(gn.shape[0]):
            start = k * part
            gn[k] = both[start // g.shape[1]][:, start % g.shape[1] : start % g.shape[1] + part]

    h = mm(n2[...], wup[...]) + b1[...]
    ag = mm(cot[...], wdown[...], NT)
    a, slope = gelu_parts(h)
    pack[:, :cut] = a.astype(BF16)
    hg = (ag * slope).astype(BF16)
    b1g[...] = jnp.sum(hg.astype(F32), axis=0, keepdims=True)
    pack[:, pack.shape[1] - part :] = gn[step]
    if not paired:
        pack[:, cut : 2 * cut] = hg
        return
    half = cut // 2
    core = lax.rem(lax.axis_index("freq"), 2)

    @pl.when(core == 0)
    def _():
        mine[0][...] = hg[:, :half]
        pack[:, cut : cut + half] = hg[:, half:]

    @pl.when(core == 1)
    def _():
        mine[0][...] = hg[:, half:]
        pack[:, cut : cut + half] = hg[:, :half]


def mlp_call(tok, convt, second, wo, ob, gain, bias, wup, b1, wdown, cot, cut, paired):
    rows, width = tok.shape
    ff = wup.shape[1]
    steps = ff // cut
    part = 2 * width // steps
    span = cut + (cut // 2 if paired else cut) + part

    def full(i):
        return (0, 0)

    def along(i):
        return (0, i)

    token = pl.BlockSpec((rows, width), full)
    vec = pl.BlockSpec((1, width), full)
    act = shape((rows, width), BF16)
    mine = [shape((rows, ff // 2), BF16)] if paired else []
    return launch(
        functools.partial(mlp_kernel, paired),
        (steps,),
        (tok, convt, second, wo, ob, gain, bias, wup, b1, wdown, cot),
        [
            token,
            pl.BlockSpec((width, rows), full),
            token,
            pl.BlockSpec((width, width), full),
            vec,
            vec,
            vec,
            pl.BlockSpec((width, cut), along),
            pl.BlockSpec((1, cut), along),
            pl.BlockSpec((cut, width), lambda i: (i, 0)),
            token,
        ],
        (shape((rows, span * steps), BF16), act, shape((rows, width), F32), shape((1, ff), F32), *mine),
        (
            pl.BlockSpec((rows, span), along),
            token,
            token,
            pl.BlockSpec((1, cut), along),
            *[pl.BlockSpec((rows, cut // 2), along) for _ in mine],
        ),
        [pltpu.VMEM((rows, width), BF16), pltpu.VMEM((steps, rows, part), BF16)],
        cost(2 * rows * width * (2 * ff + width), wup.size * 4 + rows * ff * 4 + rows * width * 14, rows * ff),
        "mix_out_mlp",
    )


def unpacked(pack, hidden, steps, cut):
    rows = pack.shape[0]
    blocks = pack.reshape(rows, steps, -1)
    tail = blocks[:, :, cut + hidden :].reshape(rows, -1)
    return blocks[:, :, :cut].reshape(rows, -1), blocks[:, :, cut : cut + hidden].reshape(rows, -1), tail[:, : tail.shape[1] // 2], tail[:, tail.shape[1] // 2 :]


def mlp_back_kernel(paired, freq_parts, *refs):
    hidden, rest = refs[: 2 if paired else 1], refs[2 if paired else 1 :]
    wup, res, gain, cot, wo, second, conv = rest[:7]
    rgrad, convgt, sgrad, mine, other, vecs, acc = rest[7:]
    step = pl.program_id(0)
    core = lax.rem(lax.axis_index("freq"), 2)
    if paired:
        first = jnp.where(core == 0, hidden[0][...], hidden[1][...])
        later = jnp.where(core == 0, hidden[1][...], hidden[0][...])
        hg = jnp.concatenate([first, later], axis=1)
    else:
        hg = hidden[0][...]
    part = mm(hg, wup[...], NT)

    @pl.when(step == 0)
    def _():
        acc[...] = part

    @pl.when(step > 0)
    def _():
        acc[...] += part

    @pl.when(step == pl.num_programs(0) - 1)
    def _():
        ng = acc[...]
        n, rate = normalized(res[...])
        e = ng * gain[...]
        pulled = e - jnp.mean(e, axis=-1, keepdims=True) - n * jnp.mean(e * n, axis=-1, keepdims=True)
        r = cot[...].astype(F32) + rate * pulled
        rgrad[...] = r
        br = r.astype(BF16)
        brf = br.astype(F32)
        gg = mm(br, wo[...], NT)
        convgt[...] = (gg * second[...].astype(F32)).T.astype(BF16)
        sg = (gg * conv[...].astype(F32)).astype(BF16)
        sgrad[...] = sg
        sgf = sg.astype(F32)
        vecs[0:1] = jnp.sum(ng * n, axis=0, keepdims=True)
        vecs[1:2] = jnp.sum(ng, axis=0, keepdims=True)
        vecs[2:3] = jnp.sum(brf, axis=0, keepdims=True)
        vecs[3:4] = jnp.sum(sgf, axis=0, keepdims=True)
        put_halves(brf.T.astype(BF16), mine, other, 0, core, freq_parts)
        put_halves(sgf.T.astype(BF16), mine, other, 1, core, freq_parts)


def put_halves(value, mine, other, half, core, freq_parts):
    per = value.shape[0] // freq_parts
    even = [value[(2 * k) * per : (2 * k + 1) * per] for k in range(freq_parts // 2)]
    odd = [value[(2 * k + 1) * per : (2 * k + 2) * per] for k in range(freq_parts // 2)]

    base = half * per * (freq_parts // 2)

    def put(ref, blocks):
        for k, block in enumerate(blocks):
            ref[base + k * per : base + (k + 1) * per] = block

    @pl.when(core == 0)
    def _():
        put(mine, even)
        put(other, odd)

    @pl.when(core == 1)
    def _():
        put(mine, odd)
        put(other, even)


def mlp_back_call(pack, mine, wup, res, gain, cot, wo, second, conv, cut, freq_parts):
    rows, width = res.shape
    ff = wup.shape[1]
    paired = mine is not None
    span = pack.shape[1] // (ff // cut)

    def full(i):
        return (0, 0)

    def along(i):
        return (0, i)

    token = pl.BlockSpec((rows, width), full)
    half = shape((width, rows), BF16)
    turned = pl.BlockSpec((width, rows), full)
    if paired:
        hidden = [mine, pack]
        step = 2 * span // cut
        hidden_specs = [pl.BlockSpec((rows, cut // 2), along), pl.BlockSpec((rows, cut // 2), lambda i: (0, step * i + 2))]
    else:
        hidden = [unpacked(pack, cut, ff // cut, cut)[1]]
        hidden_specs = [pl.BlockSpec((rows, cut), along)]
    return launch(
        functools.partial(mlp_back_kernel, paired, freq_parts),
        (ff // cut,),
        (*hidden, wup, res, gain, cot, wo, second, conv),
        hidden_specs
        + [pl.BlockSpec((width, cut), along), token, pl.BlockSpec((1, width), full), token, pl.BlockSpec((width, width), full), token, token],
        (shape((rows, width), F32), half, shape((rows, width), BF16), half, half, shape((8, width), F32)),
        (token, turned, token, turned, turned, pl.BlockSpec((8, width), full)),
        [pltpu.VMEM((rows, width), F32)],
        cost(2 * rows * width * (ff + width), wup.size * 2 + rows * ff * 2 + rows * width * 20),
        "mlp_back",
    )


def block_out_kernel(act, wdown, res, b2, cot, out, b2g, acc):
    step = pl.program_id(0)
    part = mm(act[...], wdown[...])

    @pl.when(step == 0)
    def _():
        acc[...] = res[...] + b2[...] + part
        b2g[...] = jnp.sum(cot[...].astype(F32), axis=0, keepdims=True)

    @pl.when(step > 0)
    def _():
        acc[...] += part

    @pl.when(step == pl.num_programs(0) - 1)
    def _():
        out[...] = acc[...].astype(BF16)


def block_out_call(pack, wdown, res, b2, cot, cut, after=(), carry=()):
    rows, width = res.shape
    ff = wdown.shape[0]
    step = pack.shape[1] // ff
    if step * ff != pack.shape[1]:
        pack, step = unpacked(pack, cut, ff // cut, cut)[0], 1

    def full(i):
        return (0, 0)

    token = pl.BlockSpec((rows, width), full)
    vec = pl.BlockSpec((1, width), full)
    return launch(
        block_out_kernel,
        (ff // cut,),
        (pack, wdown, res, b2, cot),
        [pl.BlockSpec((rows, cut), lambda i: (0, step * i)), pl.BlockSpec((cut, width), lambda i: (i, 0)), token, vec, token],
        (shape((rows, width), BF16), shape((1, width), F32)),
        (token, vec),
        [pltpu.VMEM((rows, width), F32)],
        cost(2 * rows * width * ff, wdown.size * 2 + rows * ff * 2 + rows * width * 8),
        "block_out",
        after,
        carry,
    )


def back_kernel(mgt, value, gate, sgrad, weight, tok, gain, rgrad, out, vecs, mg, acc):
    step = pl.program_id(0)

    @pl.when(step == 0)
    def _():
        mg[...] = mgt[...].astype(F32).T.astype(BF16)
        acc[...] = mm(sgrad[...], weight[...], NT)

    @pl.when(step == 1)
    def _():
        pv = (gate[...].astype(F32) * mg[...].astype(F32)).astype(BF16)
        acc[...] += mm(pv, weight[...], NT)
        vecs[2:3] = jnp.sum(pv.astype(F32), axis=0, keepdims=True)

    @pl.when(step == 2)
    def _():
        pg = (value[...].astype(F32) * mg[...].astype(F32)).astype(BF16)
        ng = acc[...] + mm(pg, weight[...], NT)
        vecs[3:4] = jnp.sum(pg.astype(F32), axis=0, keepdims=True)
        n, rate = normalized(tok[...].astype(F32))
        vecs[0:1] = jnp.sum(ng * n, axis=0, keepdims=True)
        vecs[1:2] = jnp.sum(ng, axis=0, keepdims=True)
        e = ng * gain[...]
        pulled = e - jnp.mean(e, axis=-1, keepdims=True) - n * jnp.mean(e * n, axis=-1, keepdims=True)
        out[...] = (rgrad[...] + rate * pulled).astype(BF16)


def back_call(mgt, value, gate, sgrad, weight, tok, gain, rgrad, after=(), carry=()):
    rows, width = tok.shape

    def full(i):
        return (0, 0)

    token = pl.BlockSpec((rows, width), full)
    return launch(
        back_kernel,
        (3,),
        (mgt, value, gate, sgrad, weight, tok, gain, rgrad,),
        [
            pl.BlockSpec((width, rows), full),
            token,
            token,
            token,
            pl.BlockSpec((width, width), lambda i: (0, lax.rem(i + 2, 3))),
            token,
            pl.BlockSpec((1, width), full),
            token,
        ],
        (shape((rows, width), BF16), shape((8, width), F32)),
        (token, pl.BlockSpec((8, width), full)),
        [pltpu.VMEM((rows, width), BF16), pltpu.VMEM((rows, width), F32)],
        cost(2048 * 2 * rows * width * width * 3, 2048 * (weight.size * 2 + rows * width * 16)),
        "project_back",
        after,
        carry,
    )


def owner_part(offs_ref, wt, bias, x, mg, source, batch, tok_rows):
    chans = wt.shape[0] // 2
    vg = mm(wt, x, NT) + bias
    lane = lax.broadcasted_iota(jnp.int32, (1, x.shape[0]), 1)
    limit = jnp.zeros_like(lane)
    for b in range(batch):
        inside = jnp.logical_and(lane >= b * tok_rows, lane < (b + 1) * tok_rows)
        limit = jnp.where(inside, offs_ref[b] + b * tok_rows, limit)
    m = jnp.where(source * tok_rows + lane >= limit, mg.astype(F32), 0.0)
    return jnp.concatenate([vg[chans:] * m, vg[:chans] * m], axis=0).astype(BF16)


def owner_list_kernel(batch, tok_rows, parts, offs_ref, wt, bias, mg, *refs):
    xs, out = refs[:parts], refs[parts]
    me = lax.axis_index("freq")
    total = None
    for r in range(parts):
        x = xs[r][...]
        source = me ^ r
        pg = owner_part(offs_ref, wt[...], bias[...], x, mg[source], source, batch, tok_rows)
        part = mm(pg, x)
        total = part if total is None else total + part
    out[...] = total.astype(BF16)


def owner_grid_kernel(batch, tok_rows, offs_ref, wt, bias, mg, x, out, acc):
    step = pl.program_id(0)

    @pl.when(step == 0)
    def _():
        acc[...] = jnp.zeros_like(acc)

    pg = owner_part(offs_ref, wt[...], bias[...], x[0], mg[0], step, batch, tok_rows)
    acc[...] += mm(pg, x[0])

    @pl.when(step == pl.num_programs(0) - 1)
    def _():
        out[...] = acc[...].astype(BF16)


def owner_call(offsets, wt, bias, mg, xs, batch, tok_rows, after=(), carry=()):
    chans, rows = mg.shape[1:]
    width = wt.shape[1]
    listed = isinstance(xs, list)
    count = mg.shape[0]
    if listed:
        kernel = functools.partial(owner_list_kernel, batch, tok_rows, count)
        grid, x_specs, scratch, mg_spec = (1,), [whole((rows, width))] * count, [], whole(mg.shape)
    else:
        kernel = functools.partial(owner_grid_kernel, batch, tok_rows)
        xs = [xs]
        grid, x_specs = (count,), [pl.BlockSpec((1, rows, width), lambda i: (i, 0, 0))]
        scratch = [pltpu.VMEM((2 * chans, width), F32)]
        mg_spec = pl.BlockSpec((1, chans, rows), lambda i: (i, 0, 0))
    return launch(
        kernel,
        grid,
        (offsets, wt, bias, mg, *xs,),
        [smem(), whole(wt.shape), whole(bias.shape), mg_spec] + x_specs,
        (shape((2 * chans, width), BF16),),
        (whole((2 * chans, width)),),
        scratch,
        cost(8 * count * rows * chans * width, count * rows * width * 2),
        "owner_gradients",
        after,
        carry,
    )


def near_values(value, freq_parts):
    return [flip(value, freq_parts, r) for r in (2, 4, 6)]


def bit_order(chips, low_first):
    bits = list(range(chips.bit_length() - 1))
    return bits if low_first else bits[::-1]


def place_of(rel, order):
    place = 0
    for level, bit in enumerate(order):
        digit = lax.shift_right_logical(rel, bit) & 1
        place = place + digit * (1 << (len(order) - 1 - level))
    return place


def store_slot(keep, send, place, index, block):
    half = keep.shape[0]

    @pl.when(place < half)
    def _():
        keep[(place,) + index] = block

    @pl.when(place >= half)
    def _():
        send[(place - half,) + index] = block


def rows_kernel(chips, per, order, count, *refs):
    ins, (keep, send) = refs[: 4 * count], refs[4 * count :]
    chip = lax.axis_index("freq") // 2
    for p in range(count):
        lt, rt, ltp, rtp = ins[4 * p : 4 * p + 4]
        total = (mm(lt[...], rt[...]) + mm(ltp[...], rtp[...])).astype(BF16)
        for k in range(chips):
            place = place_of(jnp.int32(k) ^ chip, order)
            store_slot(keep, send, place, (slice(p * per, (p + 1) * per), slice(None)), total[k * per : (k + 1) * per])


def rows_pair(problems, rows, width, chips, low_first, cut, name, after=(), carry=()):
    order = bit_order(chips, low_first)
    per = rows // chips
    count = len(problems)
    inner = problems[0][0][0].shape[1]
    out = shape((chips // 2, count * per, width), BF16)
    out_spec = pl.BlockSpec((chips // 2, count * per, cut), lambda i: (0, 0, i))
    arrays, specs = [], []
    for problem in problems:
        for k in range(2):
            (left, place), (right, lanes) = problem[2 * k], problem[2 * k + 1]
            arrays += [left, right]
            specs.append(pl.BlockSpec((rows, inner), lambda i, place=place: (place, 0)))
            specs.append(pl.BlockSpec((inner, cut), lambda i, lanes=lanes: (0, lanes(i))))
    return launch(
        functools.partial(rows_kernel, chips, per, order, count),
        (width // cut,),
        tuple(arrays),
        specs,
        (out, out),
        (out_spec, out_spec),
        [],
        cost(4 * count * rows * inner * width, count * (rows * inner + inner * width + rows * width) * 4),
        name,
        after,
        carry,
    )


def rows_plain(problems, chips, low_first):
    blocks = [(mm(lt, rt) + mm(ltp, rtp)).astype(BF16).reshape(chips, lt.shape[0] // chips, -1) for lt, rt, ltp, rtp in problems]
    return halves_of(jnp.concatenate(blocks, axis=1), bit_order(chips, low_first))


def halves_of(blocks, order):
    chips = blocks.shape[0]
    chip = lax.axis_index("freq") // 2
    picks = np.zeros(chips, np.int32)
    for rel in range(chips):
        place = sum(((rel >> bit) & 1) << (len(order) - 1 - level) for level, bit in enumerate(order))
        picks[place] = rel
    moved = jnp.take(blocks, jnp.asarray(picks) ^ chip, axis=0)
    return moved[: chips // 2], moved[chips // 2 :]


def cols_kernel(order, la, lb, rt, lap, lbp, rtp, keep, send, left):
    step = pl.program_id(0)
    chip = lax.axis_index("freq") // 2
    half = la.shape[1]

    @pl.when(step == 0)
    def _():
        for k, ref in enumerate((la, lb, lap, lbp)):
            left[k // 2, (k % 2) * half : (k % 2 + 1) * half] = ref[...].astype(F32).T.astype(BF16)

    total = (mm(left[0], rt[...]) + mm(left[1], rtp[...])).astype(BF16)
    store_slot(keep, send, place_of(step ^ chip, order), (), total)


def cols_pair(mine, pack, pack_p, width, cut, chips, low_first, after=(), carry=()):
    order = bit_order(chips, low_first)
    rows = mine.shape[0]
    per = mine.shape[1] // chips
    last = pack.shape[1] // per - 1
    step = pack.shape[1] // chips // per
    out = shape((chips // 2, width, per), BF16)
    out_spec = pl.BlockSpec((chips // 2, width, per), lambda i: (0, 0, 0))

    def at(place):
        return pl.BlockSpec((rows, per), place)

    first, second = (lambda i: (0, last - step)), (lambda i: (0, last))
    return launch(
        functools.partial(cols_kernel, order),
        (chips,),
        (pack, pack, mine, pack_p, pack_p, pack_p),
        [at(first), at(second), at(lambda i: (0, i)), at(first), at(second), at(lambda i: (0, step * i + 2))],
        (out, out),
        (out_spec, out_spec),
        [pltpu.VMEM((2, width, rows), BF16)],
        cost(4 * width * rows * mine.shape[1], (width * rows + rows * mine.shape[1] * 2) * 4),
        "fc1_gradient",
        after,
        carry,
    )


def cols_plain(lt, rt, ltp, rtp, chips, low_first):
    total = (mm(lt.T, rt) + mm(ltp.T, rtp)).astype(BF16)
    return halves_of(total.reshape(lt.shape[1], chips, -1).transpose(1, 0, 2), bit_order(chips, low_first))


def flip(value, freq_parts, bit):
    return lax.ppermute(value, "freq", [(i, i ^ bit) for i in range(freq_parts)])


def halving(keep, send, freq_parts, low_first, first=0, last=None):
    order = bit_order(freq_parts // 2, low_first)
    for level in range(first, len(order)):
        if level == last:
            return keep, send
        got = flip(send, freq_parts, 2 << order[level])
        total = keep.astype(F32) + got.astype(F32)
        if level == len(order) - 1:
            return total[0]
        half = total.shape[0] // 2
        keep, send = total[:half].astype(BF16), total[half:].astype(BF16)


def across(blocks):
    blocks = blocks.astype(BF16)
    me, count = lax.axis_index("dp"), blocks.shape[0]

    def block(k):
        return lax.dynamic_index_in_dim(blocks, me ^ k, 0, keepdims=False)

    got = [lax.ppermute(block(k), "dp", [(i, i ^ k) for i in range(count)]) for k in range(count - 1, 0, -1)]
    return functools.reduce(jnp.add, [v.astype(F32) for v in [block(0)] + got])


def everywhere(taps, rows):
    dp, freq = lax.axis_size("dp"), lax.axis_size("freq")
    lines, span = taps.shape[1:]
    flat = rows.reshape(freq, -1)
    high, low = split_value(flat)
    parts = jnp.concatenate([high, low], axis=1)
    more = -(-parts.shape[1] // span)
    parts = jnp.pad(parts, ((0, 0), (0, more * span - parts.shape[1]))).reshape(freq, more, span)
    sent = jnp.concatenate([taps, parts], axis=1)
    sent = jnp.broadcast_to(sent[None], (dp,) + sent.shape).reshape(dp * freq, lines + more, span)
    got = lax.all_to_all(sent, ("dp", "freq"), split_axis=0, concat_axis=0, tiled=True)
    total = jnp.sum(got[:, lines:].astype(F32), axis=0).reshape(-1)
    count = flat.shape[1]
    return got[:, :lines], (total[:count] + total[count : 2 * count]).reshape(rows.shape[1:])


def reblocked(blocks, count, width):
    if blocks.shape[0] == count and blocks.shape[2] == width:
        return blocks
    whole = blocks.transpose(1, 0, 2).reshape(blocks.shape[1], -1)
    need = count * width
    whole = jnp.pad(whole, ((0, 0), (0, max(0, need - whole.shape[1]))))[:, :need]
    return whole.reshape(-1, count, width).transpose(1, 0, 2)


def body(tokens, offsets, kernel_lengths, norm1_gain, norm1_bias, w_in, in_bias, kernel_taps, skip_gain, w_out, out_bias, norm2_gain, norm2_bias, w_up, fc1_bias, w_down, fc2_bias, cotangent):
    freq = lax.axis_size("freq")
    dp = lax.axis_size("dp")
    chips = freq // 2
    batch, tok_rows, width = tokens.shape
    rows = batch * tok_rows
    ff = w_up.shape[1]
    chans = width // freq
    me = lax.axis_index("freq")
    core = lax.rem(me, 2)

    def row(v):
        return v.reshape(1, -1)

    tok = tokens.reshape(rows, width)
    cot = cotangent.reshape(rows, width)
    shrunk = (kernel_taps - SHRINK * jnp.tanh(kernel_taps / SHRINK)).astype(BF16)
    tap_rows = shrunk.shape[1]
    shrunk = lax.all_to_all(shrunk.reshape(freq, chans, tap_rows), "freq", split_axis=0, concat_axis=0, tiled=True)
    reach = -(-freq * tap_rows // tok_rows)
    shrunk = reblocked(shrunk, reach, tok_rows)
    lens = lax.dynamic_slice_in_dim(kernel_lengths, me * chans, chans).reshape(chans, 1)
    normed, mixed_t, value, gate, second = front_call(tok, offsets, row(norm1_gain), row(norm1_bias), w_in, row(in_bias), batch, tok_rows)
    mixed = lax.all_to_all(mixed_t.reshape(freq, chans, rows), "freq", split_axis=0, concat_axis=0, tiled=True)
    k_spec = taps_call(shrunk, lens, freq)
    skip = skip_gain.reshape(chans, 1)
    cot_t = cot.T.reshape(chips, 2, chans, rows)
    cot_mine = jnp.take(cot_t, core, axis=1).reshape(width // 2, rows)
    cot_other = jnp.take(cot_t, 1 - core, axis=1).reshape(width // 2, rows)

    def swap(v):
        return flip(v, freq, 1)

    conv, (cot_p, normed_p) = conv_call(mixed, k_spec, skip, False, carry=(swap(cot_other), swap(normed)))
    near = near_values(normed, freq) if freq == 8 else []
    conv_t = lax.all_to_all(conv, "freq", split_axis=0, concat_axis=0, tiled=True).reshape(width, rows)
    cut = 768
    paired = freq == 8 and ff == 4 * cut
    pack, conv_tok, res, b1g, *mine = mlp_call(
        tok, conv_t, second, w_out, row(out_bias), row(norm2_gain), row(norm2_bias), w_up, row(fc1_bias), w_down, cot, cut, paired
    )
    mine = mine[0] if paired else None
    rgrad, convg_t, sgrad, turned, turned_other, vec_two = mlp_back_call(pack, mine, w_up, res, row(norm2_gain), cot, w_out, second, conv_tok, cut, freq)
    convg = lax.all_to_all(convg_t.reshape(freq, chans, rows), "freq", split_axis=0, concat_axis=0, tiled=True)
    half = width // 2
    if paired:
        pack_p, turned_p = swap(pack), swap(turned_other)
        fc2, near = rows_pair(
            [((cot_mine, 0), (pack, lambda i: 2 * i), (cot_p, 0), (pack_p, lambda i: 2 * i))],
            half, ff, chips, True, cut, "fc2_gradient", after=(rgrad,), carry=near,
        )
        far = [swap(v) for v in near]
        fc1 = cols_pair(mine, pack, pack_p, width, cut, chips, False, after=(fc2[1],))
        mixed_grad, far = conv_call(convg, k_spec, skip, True, after=(fc1[1],), carry=far)
        normed_all = [v for pair_of in zip([normed, *near], [normed_p, *far]) for v in pair_of]
        mixer = rows_pair(
            [
                ((turned, 0), (pack, lambda i: 3 + 4 * i), (turned_p, 0), (pack_p, lambda i: 3 + 4 * i)),
                ((turned, 1), (normed, lambda i: i), (turned_p, 1), (normed_p, lambda i: i)),
            ],
            half, width, chips, True, width // 2, "mixer_gradient", after=(mixed_grad,),
        )
    else:
        normed_all = lax.all_gather(normed, "freq", axis=0, tiled=False)
        act, hg, gated, n2 = unpacked(pack, cut, ff // cut, cut)
        hg = hg.reshape(rows, chips, 2, ff // freq)
        hg_mine = jnp.take(hg, core, axis=2).reshape(rows, ff // 2)
        hg_other = jnp.take(hg, 1 - core, axis=2).reshape(rows, ff // 2)
        act_p, gated_p, n2_p, turned_p = swap(act), swap(gated), swap(n2), swap(turned_other)
        fc2 = rows_plain([(cot_mine, act, cot_p, act_p)], chips, True)
        fc1 = cols_plain(n2, hg_mine, n2_p, swap(hg_other), chips, False)
        mixed_grad = conv_call(convg, k_spec, skip, True)
        mixer = rows_plain([(turned[:half], gated, turned_p[:half], gated_p), (turned[half:], normed, turned_p[half:], normed_p)], chips, True)
    mixed_grad_t = lax.all_to_all(mixed_grad, "freq", split_axis=0, concat_axis=0, tiled=True).reshape(width, rows)
    own_w = jnp.concatenate([lax.dynamic_slice_in_dim(w_in, k * width + me * chans, chans, axis=1) for k in range(2)], axis=1).T
    own_b = jnp.concatenate([lax.dynamic_slice_in_dim(in_bias, k * width + me * chans, chans) for k in range(2)]).reshape(-1, 1)
    owned, (fc2_keep,) = owner_call(offsets, own_w, own_b, mixed_grad, normed_all, batch, tok_rows, after=(mixer[1],), carry=(fc2[0],))
    fc2 = halving(fc2_keep, fc2[1], freq, True, 0, 1)
    (taps_g, skip_g), (fc1_keep,) = taps_grad_call(mixed, convg, lens, tok_rows, reach, after=(fc2[1],), carry=(fc1[0],))
    fc1 = halving(fc1_keep, fc1[1], freq, False, 0, 1)
    fc2 = halving(*fc2, freq, True, 1)
    (block_out, b2g), (mixer_keep,) = block_out_call(pack, w_down, res, row(fc2_bias), cot, cut, after=(fc1[1],), carry=(mixer[0],))
    mixer = halving(mixer_keep, mixer[1], freq, True, 0, 1)
    (input_grad, vec_one), (fc1_keep, mixer_keep) = back_call(
        mixed_grad_t, value, gate, sgrad, w_in, tok, row(norm1_gain), rgrad, after=(mixer[1], fc2), carry=(fc1[0], mixer[0])
    )
    taps_g = reblocked(taps_g, freq, tap_rows)
    fc2_final = across(fc2.reshape(chans, dp, ff // dp).transpose(1, 0, 2)).T
    fc1 = halving(fc1_keep, fc1[1], freq, False, 1)
    fc1_final = across(fc1.reshape(dp, width // dp, ff // freq))
    mixer = halving(mixer_keep, mixer[1], freq, True, 1).astype(BF16)
    parts = jnp.concatenate([owned, mixer[chans:]]).reshape(3, chans, width)
    pieces = []
    for r in range(3):
        part = lax.rem((freq % 3) * (r - me + 3 * freq), 3)
        piece = lax.dynamic_index_in_dim(parts, part, 0, keepdims=False)
        pieces.append(lax.ppermute(piece, "freq", [((3 * d + r) % freq, d) for d in range(freq)]))
    late = jnp.concatenate(pieces + [mixer[:chans]], axis=0).T
    late = across(late.reshape(dp, width // dp, 4 * chans))
    in_final, out_final = late[:, : 3 * chans], late[:, 3 * chans :]
    quarter_sum = across(taps_g.reshape(freq, dp, chans // dp, tap_rows).transpose(1, 0, 2, 3)).astype(BF16)
    own = (jnp.arange(freq, dtype=jnp.int32) == me).astype(F32)[:, None, None] * skip_g.reshape(1, 1, chans)
    bias_in = jnp.concatenate([vec_one[2:4], vec_two[3:4]]).reshape(freq, 3, chans)
    plain = jnp.concatenate([vec_one[:2], vec_two[:3], b2g]).reshape(6, freq, chans).transpose(1, 0, 2)
    spread, final = everywhere(quarter_sum, jnp.concatenate([plain, bias_in, b1g.reshape(freq, -1, chans), own], axis=1))
    spread = spread.reshape(dp, freq, chans // dp, tap_rows).transpose(1, 0, 2, 3).reshape(width, tap_rows)
    taps_final = spread.astype(F32) * jnp.square(jnp.tanh(kernel_taps / SHRINK))
    n1g, n1b, n2g, n2b, outb, b2f = (final[k] for k in range(6))
    inb, b1f, skg = final[6:9].reshape(-1), final[9:-1].reshape(-1), final[-1]
    return (
        block_out.reshape(tokens.shape),
        input_grad.reshape(tokens.shape),
        n1g,
        n1b,
        in_final,
        inb,
        taps_final,
        skg,
        out_final,
        outb,
        n2g,
        n2b,
        fc1_final,
        b1f,
        fc2_final,
        b2f,
    )


def solution(mesh):
    token, whole, lead = P("dp", "freq", None), P(), P("freq")
    both = P("dp", "freq")
    in_specs = (token, P("dp"), whole, whole, whole, whole, whole, P(None, "freq"), lead) + (whole,) * 8 + (token,)
    out_specs = (token, token, lead, lead, both, lead, P(None, "freq"), lead, both, lead, lead, lead, both, lead, both, lead)
    return jax.shard_map(body, mesh=mesh, in_specs=in_specs, out_specs=out_specs, check_vma=False)
```

```python
import functools

import jax
import jax.numpy as jnp
import numpy as np
from jax import lax
from jax.experimental import pallas as pl
from jax.experimental.pallas import tpu as pltpu
from jax.sharding import PartitionSpec as P

NORM_EPS = 1e-05
SHRINK = 0.003
GELU_C = 0.7978845608028654
GELU_A = 0.044715
F32 = jnp.float32
BF16 = jnp.bfloat16
MIB = 1 << 20

NN = (((1,), (0,)), ((), ()))
NT = (((1,), (1,)), ((), ()))


def mm(left, right, dims=NN):
    return lax.dot_general(left, right, dims, preferred_element_type=F32)


def whole(dims):
    return pl.BlockSpec(tuple(dims), lambda i: (0,) * len(dims))


def anywhere():
    return pl.BlockSpec(memory_space=pl.ANY)


def smem():
    return pl.BlockSpec(memory_space=pltpu.SMEM)


def shape(dims, dtype):
    return jax.ShapeDtypeStruct(dims, dtype)


def launch(kernel, grid, ins, in_specs, outs, out_specs, scratch, estimate, name, after=(), carry=()):
    count, extra, given = len(ins), len(after) + len(carry), len(outs)

    def run(*refs):
        made = refs[count + extra : count + extra + given]
        kernel(*refs[:count], *made, *refs[count + extra + given + len(carry) :])

    first = count + len(after)
    results = pl.pallas_call(
        run,
        grid=grid,
        out_shape=tuple(outs) + tuple(shape(v.shape, v.dtype) for v in carry),
        in_specs=list(in_specs) + [anywhere()] * extra,
        out_specs=tuple(out_specs) + (anywhere(),) * len(carry),
        scratch_shapes=scratch,
        input_output_aliases={first + k: given + k for k in range(len(carry))},
        compiler_params=pltpu.CompilerParams(vmem_limit_bytes=60 * MIB, dimension_semantics=("arbitrary",)),
        cost_estimate=estimate,
        name=name,
    )(*ins, *after, *carry)
    made = results[0] if given == 1 else results[:given]
    return (made, results[given:]) if carry else made


def cost(flops, moved, special=0):
    return pl.CostEstimate(flops=int(flops) * 64, bytes_accessed=int(moved) * 64, transcendentals=0)


def split16(table):
    high = np.asarray(table, np.float32).astype(jnp.bfloat16)
    low = (np.asarray(table, np.float64) - high.astype(np.float64)).astype(np.float32).astype(jnp.bfloat16)
    return high, low


@functools.lru_cache(maxsize=None)
def tables(width):
    order = np.concatenate([np.arange(0, width, 2), np.arange(1, width, 2)])
    turns = (2 * order[None, :] + 1) * np.arange(width)[:, None] % (4 * width)
    angle = np.pi * turns / (2 * width)
    forward = np.concatenate([np.cos(angle), -np.sin(angle)], axis=1)
    inverse = forward.T / width
    return split16(forward) + split16(inverse)


def split_value(value):
    high = value.astype(BF16)
    return high, (value - high.astype(F32)).astype(BF16)


def spectrum_of(block, fhi, flo):
    return mm(block, fhi) + mm(block, flo)


def signal_of(spec, ghi, glo):
    high, low = split_value(spec)
    return mm(high, ghi) + (mm(low, ghi) + mm(high, glo))


def each(count, step, unroll):
    if unroll:
        for i in range(count):
            step(i)
    else:
        lax.fori_loop(0, count, lambda i, c: (step(i), c)[1], 0)


def blocks_to_spectra(x_ref, spec_ref, fhi, flo, batch, width):
    count, chans = x_ref.shape[0], x_ref.shape[1]
    for b in range(batch):
        lanes = slice(b * width, (b + 1) * width)
        if chans % 16 == 0:
            rows = x_ref[:, :, lanes].reshape(count * chans, width)
            spec_ref[b] = spectrum_of(rows, fhi[...], flo[...]).reshape(count, chans, 2 * width)
        else:

            def step(j, b=b, lanes=lanes):
                spec_ref[b, j] = spectrum_of(x_ref[j, :, lanes], fhi[...], flo[...])

            each(count, step, False)


def tiles(chans, width, step):
    lane_tiles = width // 128

    def rows_step(rt):
        start = rt * 8 if isinstance(rt, int) else pl.multiple_of(rt * 8, 8)
        for lane in range(lane_tiles):
            step(pl.ds(start, 8), lane)

    each(chans // 8, rows_step, False)


def pair(ref, lead, rows, lane, width):
    return (
        ref[lead + (rows, slice(lane * 128, (lane + 1) * 128))],
        ref[lead + (rows, slice(width + lane * 128, width + (lane + 1) * 128))],
    )


def put_pair(ref, lead, rows, lane, width, value):
    ref[lead + (rows, slice(lane * 128, (lane + 1) * 128))] = value[0]
    ref[lead + (rows, slice(width + lane * 128, width + (lane + 1) * 128))] = value[1]


def times(a, k):
    return a[0] * k[0] - a[1] * k[1], a[0] * k[1] + a[1] * k[0]


def times_conj(a, k):
    return a[0] * k[0] + a[1] * k[1], a[1] * k[0] - a[0] * k[1]


def plus(a, b):
    return b if a is None else (a[0] + b[0], a[1] + b[1])


def quarter(now, before, sign):
    if before is None:
        return now
    if sign > 0:
        return now[0] - before[1], now[1] + before[0]
    return now[0] + before[1], now[1] - before[0]


def wide_quarter(now, before, width):
    lane = lax.broadcasted_iota(jnp.int32, (1, width), 1)
    sign = jnp.where(lane < width // 2, 1.0, -1.0)
    return jnp.concatenate(
        [now[:, :width] - sign * before[:, width:], now[:, width:] + sign * before[:, :width]], axis=1
    )


def wide_times(a, k, width, conj):
    ar, ai, kr, ki = a[:, :width], a[:, width:], k[:, :width], k[:, width:]
    if conj:
        return jnp.concatenate([ar * kr + ai * ki, ai * kr - ar * ki], axis=1)
    return jnp.concatenate([ar * kr - ai * ki, ar * ki + ai * kr], axis=1)


UNROLLED = 8


def small(count, chans, width):
    return count <= UNROLLED and chans % 16 == 0 and width % 256 == 0


def conv_products(spec_ref, k_ref, z_ref, batch, width, adjoint):
    reach, chans = k_ref.shape[0], k_ref.shape[1]
    count = spec_ref.shape[1]
    if small(count, chans, width):

        def step(rows, lane):
            k = [pair(k_ref, (d,), rows, lane, width) for d in range(reach)]
            for b in range(batch):
                x = [pair(spec_ref, (b, j), rows, lane, width) for j in range(count)]
                for i in range(count):
                    total = None
                    if adjoint:
                        for d in range(min(count - i, reach)):
                            total = plus(total, times_conj(x[i + d], k[d]))
                    else:
                        for d in range(min(i + 1, reach)):
                            total = plus(total, times(x[i - d], k[d]))
                    put_pair(z_ref, (b, i), rows, lane, width, total)

        tiles(chans, width, step)
        return
    for b in range(batch):

        def row(i, b=b):
            def term(d, total):
                src = i + d if adjoint else i - d
                return total + wide_times(spec_ref[b, src], k_ref[d], width, adjoint)

            terms = jnp.minimum(count - i if adjoint else i + 1, reach)
            z_ref[b, i] = lax.fori_loop(0, terms, term, jnp.zeros((chans, 2 * width), F32))

        each(count, row, False)


def conv_body(adjoint, batch, x_ref, k_ref, skip_ref, fhi, flo, ghi, glo, out_ref, spec_ref, z_ref):
    count, chans = x_ref.shape[:2]
    width = fhi.shape[0]
    blocks_to_spectra(x_ref, spec_ref, fhi, flo, batch, width)
    conv_products(spec_ref, k_ref, z_ref, batch, width, adjoint)
    for b in range(batch):
        cut = slice(b * width, (b + 1) * width)
        if chans % 16 == 0:
            y = signal_of(z_ref[b].reshape(count * chans, 2 * width), ghi[...], glo[...])
            y = y.reshape(count, chans, width) + skip_ref[...][None] * x_ref[:, :, cut].astype(F32)
            out_ref[:, :, cut] = y.astype(BF16)
        else:

            def step(j, b=b, cut=cut):
                y = signal_of(z_ref[b, j], ghi[...], glo[...])
                out_ref[j, :, cut] = (y + skip_ref[...] * x_ref[j, :, cut].astype(F32)).astype(BF16)

            each(count, step, False)


def forward_kernel(batch, x_ref, s_ref, len_ref, skip_ref, fhi, flo, ghi, glo, out_ref, k_ref, spec_ref, z_ref, raw_ref):
    taps_spectra(s_ref, s_ref.shape[2] - fhi.shape[0], len_ref, fhi, flo, k_ref, raw_ref)
    conv_body(False, batch, x_ref, k_ref, skip_ref, fhi, flo, ghi, glo, out_ref, spec_ref, z_ref)


def forward_call(x, batch, width, taps, lens, skip, after=(), carry=()):
    count, chans = x.shape[:2]
    reach = taps.shape[0]
    tabs = tables(width)
    spec = pltpu.VMEM((batch, count, chans, 2 * width), F32)
    span = min(reach + 1, count)
    same = taps is x
    args = (x,) if same else (x, taps)

    def kernel(*refs):
        forward_kernel(batch, refs[0], *(refs if same else refs[1:]))

    return launch(
        kernel,
        (1,),
        (*args, lens, skip, *tabs),
        [whole(v.shape) for v in (*args, lens, skip, *tabs)],
        (shape((count, chans, batch * width), BF16), shape((span, chans, 2 * width), F32)),
        (whole((count, chans, batch * width)), whole((span, chans, 2 * width))),
        [spec, spec, pltpu.VMEM((reach, chans, 2 * width), F32)],
        cost(x.size * width * 20, x.size * 8 + 4 * width * width * 4),
        "conv_forward",
        after,
        carry,
    )


def adjoint_kernel(batch, *refs):
    conv_body(True, batch, *refs)


def adjoint_call(x, batch, k_spec, skip, after=(), carry=()):
    count, chans, lanes = x.shape
    width = k_spec.shape[2] // 2
    tabs = tables(width)
    spec = pltpu.VMEM((batch, count, chans, 2 * width), F32)
    return launch(
        functools.partial(adjoint_kernel, batch),
        (1,),
        (x, k_spec, skip, *tabs),
        [whole(v.shape) for v in (x, k_spec, skip, *tabs)],
        (shape(x.shape, BF16),),
        (whole(x.shape),),
        [spec, spec],
        cost(x.size * width * 20, x.size * 4 + k_spec.size * 4 + 4 * width * width * 4),
        "conv_adjoint",
        after,
        carry,
    )


def pooled_rows(full):
    span = full.shape[1]
    place = lax.broadcasted_iota(jnp.int32, (1, span), 1)
    before = jnp.where(place == 0, 0.0, pltpu.roll(full, 1, 1))
    after = jnp.where(place == span - 1, 0.0, pltpu.roll(full, span - 1, 1))
    return (before + full + after) / 3.0


def taps_spectra(s_ref, start, len_ref, fhi, flo, out_ref, raw_ref):
    count, chans = s_ref.shape[:2]
    width = fhi.shape[0]
    full = jnp.concatenate([s_ref[d, :, start : start + width].astype(F32) for d in range(count)], axis=1)
    place = lax.broadcasted_iota(jnp.int32, (1, count * width), 1)
    kernel = jnp.where(place < len_ref[...], pooled_rows(full), 0.0)
    for d in range(count):
        high, low = split_value(kernel[:, d * width : (d + 1) * width])
        raw_ref[d] = mm(high, fhi[...]) + (mm(low, fhi[...]) + mm(high, flo[...]))
    out_ref[0] = raw_ref[0]
    for d in range(1, count):
        out_ref[d] = wide_quarter(raw_ref[d], raw_ref[d - 1], width)
    if out_ref.shape[0] > count:
        out_ref[count] = wide_quarter(jnp.zeros((chans, 2 * width), F32), raw_ref[count - 1], width)


def taps_grad_kernel(x_ref, g_ref, len_ref, fhi, flo, ghi, glo, out_ref, skip_ref, xs_ref, gs_ref, z_ref):
    count, chans, lanes = g_ref.shape
    reach = out_ref.shape[0]
    width = fhi.shape[0]
    batch = lanes // width
    blocks_to_spectra(x_ref, xs_ref, fhi, flo, batch, width)
    blocks_to_spectra(g_ref, gs_ref, fhi, flo, batch, width)
    if small(count, chans, width):

        def step(rows, lane):
            sign = 1 if lane < width // 256 else -1
            total = [None] * reach
            for b in range(batch):
                x = [pair(xs_ref, (b, j), rows, lane, width) for j in range(count)]
                x = [quarter(x[j], x[j - 1] if j else None, sign) for j in range(count)]
                for i in range(count):
                    g = pair(gs_ref, (b, i), rows, lane, width)
                    for d in range(min(i + 1, reach)):
                        total[d] = plus(total[d], times_conj(g, x[i - d]))
            for d in range(reach):
                put_pair(z_ref, (d,), rows, lane, width, total[d])

        tiles(chans, width, step)
        rows = signal_of(z_ref[...].reshape(reach * chans, 2 * width), ghi[...], glo[...])
        rows = rows.reshape(reach, chans, width)
        pieces = [rows[d] for d in range(reach)]
    else:

        def shift(t, c):
            j = count - 1 - t
            for b in range(batch):
                xs_ref[b, j] = wide_quarter(xs_ref[b, j], xs_ref[b, j - 1], width)
            return c

        lax.fori_loop(0, count - 1, shift, 0)

        def lag(d):
            total = jnp.zeros((chans, 2 * width), F32)
            for b in range(batch):

                def term(i, acc, b=b):
                    return acc + wide_times(gs_ref[b, i], xs_ref[b, i - d], width, True)

                total = lax.fori_loop(d, count, term, total)
            z_ref[d] = total

        each(reach, lag, False)
        pieces = [signal_of(z_ref[d], ghi[...], glo[...]) for d in range(reach)]
    full = jnp.concatenate(pieces, axis=1)
    place = lax.broadcasted_iota(jnp.int32, (1, reach * width), 1)
    full = pooled_rows(jnp.where(place < len_ref[...], full, 0.0))
    for d in range(reach):
        out_ref[d] = full[:, d * width : (d + 1) * width].astype(BF16)
    dot = jnp.zeros((chans, lanes), F32)
    for j in range(count):
        dot = dot + x_ref[j, :, :lanes].astype(F32) * g_ref[j].astype(F32)
    skip_ref[...] = jnp.sum(dot, axis=1, keepdims=True)


def taps_grad_call(x, g, lens, width, reach, after=(), carry=()):
    count, chans, lanes = g.shape
    batch = lanes // width
    tabs = tables(width)
    spec = pltpu.VMEM((batch, count, chans, 2 * width), F32)
    return launch(
        taps_grad_kernel,
        (1,),
        (x, g, lens, *tabs,),
        [whole(v.shape) for v in (x, g, lens, *tabs)],
        (shape((reach, chans, width), BF16), shape((chans, 1), F32)),
        (whole((reach, chans, width)), whole((chans, 1))),
        [spec, spec, pltpu.VMEM((reach, chans, 2 * width), F32)],
        cost(x.size * width * 20, x.size * 6),
        "taps_gradient",
        after,
        carry,
    )


def normalized(values):
    centred = values - jnp.mean(values, axis=-1, keepdims=True)
    rate = lax.rsqrt(jnp.mean(centred * centred, axis=-1, keepdims=True) + NORM_EPS)
    return centred * rate, rate


def live_rows(offs_ref, batch, tok_rows, rows):
    row = lax.broadcasted_iota(jnp.int32, (rows, 1), 0)
    limit = jnp.zeros((rows, 1), jnp.int32)
    base = lax.axis_index("freq") * tok_rows
    position = base + row
    for b in range(batch):
        inside = jnp.logical_and(row >= b * tok_rows, row < (b + 1) * tok_rows)
        limit = jnp.where(inside, offs_ref[b] + b * tok_rows, limit)
    return position >= limit


def front_kernel(batch, tok_rows, offs_ref, tok, gain, bias, wv, wg, ws, bv, bg, bs, taps, normed, mixed, value, gate, second):
    rows = tok.shape[0]

    @pl.when(pl.program_id(0) == 0)
    def _():
        n, _ = normalized(tok[...].astype(F32))
        normed[...] = (n * gain[...].reshape(1, -1) + bias[...].reshape(1, -1)).astype(BF16)

    x = normed[...]
    v = mm(x, wv[...]) + bv[...]
    g = mm(x, wg[...]) + bg[...]
    live = live_rows(offs_ref, batch, tok_rows, rows)
    mixed[:, :rows] = jnp.where(live, g * v, 0.0).T.astype(BF16)
    t = taps[...]
    mixed[:, rows:] = (t - SHRINK * jnp.tanh(t / SHRINK)).astype(BF16)
    value[...] = jnp.where(live, v, 0.0).astype(BF16)
    gate[...] = jnp.where(live, g, 0.0).astype(BF16)
    second[...] = (mm(x, ws[...]) + bs[...]).astype(BF16)


def front_call(tok, offsets, gain, bias, weight, in_bias, taps, batch, tok_rows):
    rows, width = tok.shape
    span = rows + taps.shape[1]
    cut = 256
    per = width // cut

    def full(i):
        return (0, 0)

    def col(part):
        return lambda i: (0, part * per + i)

    act = shape((rows, width), BF16)
    return launch(
        functools.partial(front_kernel, batch, tok_rows),
        (per,),
        (offsets, tok, gain, bias, weight, weight, weight, in_bias, in_bias, in_bias, taps),
        [smem(), pl.BlockSpec((rows, width), full), whole((width,)), whole((width,))]
        + [pl.BlockSpec((width, cut), col(k)) for k in range(3)]
        + [pl.BlockSpec((1, cut), col(k)) for k in range(3)]
        + [pl.BlockSpec((cut, taps.shape[1]), lambda i: (i, 0))],
        (act, shape((width, span), BF16), act, act, act),
        (
            pl.BlockSpec((rows, width), full),
            pl.BlockSpec((cut, span), lambda i: (i, 0)),
            pl.BlockSpec((rows, cut), lambda i: (0, i)),
            pl.BlockSpec((rows, cut), lambda i: (0, i)),
            pl.BlockSpec((rows, cut), lambda i: (0, i)),
        ),
        [],
        cost(2 * rows * width * 3 * width, weight.size * 2 + rows * width * 12),
        "norm_project",
            )


def active_grad_kernel(freq_parts, cot, wdown, out, b2g, mine, other):
    @pl.when(pl.program_id(0) == 0)
    def _():
        c = cot[...].astype(F32)
        b2g[...] = jnp.sum(c, axis=0, keepdims=True)
        put_halves(c.T.astype(BF16), mine, other, 0, lax.rem(lax.axis_index("freq"), 2), freq_parts)

    out[...] = mm(cot[...], wdown[...], NT).astype(BF16)


def active_grad_call(cot, wdown, cut, freq_parts, after=(), carry=()):
    rows, width = cot.shape
    ff = wdown.shape[0]
    half = shape((width // 2, rows), BF16)
    return launch(
        functools.partial(active_grad_kernel, freq_parts),
        (ff // cut,),
        (cot, wdown),
        [pl.BlockSpec((rows, width), lambda i: (0, 0)), pl.BlockSpec((cut, width), lambda i: (i, 0))],
        (shape((rows, ff), BF16), shape((1, width), F32), half, half),
        (pl.BlockSpec((rows, cut), lambda i: (0, i)), whole((1, width)), whole(half.shape), whole(half.shape)),
        [],
        cost(2 * rows * width * ff, wdown.size * 2 + rows * ff * 2),
        "active_grad",
        after,
        carry,
    )


def gelu_parts(h):
    square = h * h
    t = jnp.tanh(GELU_C * h * (1.0 + GELU_A * square))
    half = 0.5 + 0.5 * t
    slope = half + (0.5 * GELU_C) * h * (1.0 - t * t) * (1.0 + (3.0 * GELU_A) * square)
    return h * half, slope


def mlp_kernel(paired, freq_parts, tok, convt, second, wo, ob, gain, bias, wup, b1, ag_ref, cot, pack, res, b1g, rgrad, convgt, sgrad, mine_t, other_t, vecs, *rest):
    mine, (n2, gn, conv, acc) = rest[:-4], rest[-4:]
    step = pl.program_id(0)
    cut, part = wup.shape[1], gn.shape[2]
    core = lax.rem(lax.axis_index("freq"), 2)

    @pl.when(step == 0)
    def _():
        c = convt[...].astype(F32).T
        conv[...] = c.astype(BF16)
        g = (second[...].astype(F32) * c).astype(BF16)
        r = tok[...].astype(F32) + (mm(g, wo[...]) + ob[...])
        res[...] = r
        n, _ = normalized(r)
        m = (n * gain[...] + bias[...]).astype(BF16)
        n2[...] = m
        both = [g, m]
        for k in range(gn.shape[0]):
            start = k * part
            gn[k] = both[start // g.shape[1]][:, start % g.shape[1] : start % g.shape[1] + part]
        acc[...] = jnp.zeros_like(acc)

    h = mm(n2[...], wup[...]) + b1[...]
    a, slope = gelu_parts(h)
    pack[:, :cut] = a.astype(BF16)
    hg = (ag_ref[...].astype(F32) * slope).astype(BF16)
    acc[...] += mm(hg, wup[...], NT)
    b1g[...] = jnp.sum(hg.astype(F32), axis=0, keepdims=True)
    pack[:, pack.shape[1] - part :] = gn[step]
    if not paired:
        pack[:, cut : 2 * cut] = hg
    else:
        half = cut // 2

        @pl.when(core == 0)
        def _():
            mine[0][...] = hg[:, :half]
            pack[:, cut : cut + half] = hg[:, half:]

        @pl.when(core == 1)
        def _():
            mine[0][...] = hg[:, half:]
            pack[:, cut : cut + half] = hg[:, :half]

    @pl.when(step == pl.num_programs(0) - 1)
    def _():
        ng = acc[...]
        n, rate = normalized(res[...])
        e = ng * gain[...]
        pulled = e - jnp.mean(e, axis=-1, keepdims=True) - n * jnp.mean(e * n, axis=-1, keepdims=True)
        r = cot[...].astype(F32) + rate * pulled
        rgrad[...] = r
        br = r.astype(BF16)
        brf = br.astype(F32)
        gg = mm(br, wo[...], NT)
        convgt[...] = (gg * second[...].astype(F32)).T.astype(BF16)
        sg = (gg * conv[...].astype(F32)).astype(BF16)
        sgrad[...] = sg
        sgf = sg.astype(F32)
        vecs[0:1] = jnp.sum(ng * n, axis=0, keepdims=True)
        vecs[1:2] = jnp.sum(ng, axis=0, keepdims=True)
        vecs[2:3] = jnp.sum(brf, axis=0, keepdims=True)
        vecs[3:4] = jnp.sum(sgf, axis=0, keepdims=True)
        put_halves(brf.T.astype(BF16), mine_t, other_t, 0, core, freq_parts)
        put_halves(sgf.T.astype(BF16), mine_t, other_t, 1, core, freq_parts)


def mlp_call(tok, convt, second, wo, ob, gain, bias, wup, b1, active_grad, cot, cut, paired, freq_parts, after=(), carry=()):
    rows, width = tok.shape
    ff = wup.shape[1]
    steps = ff // cut
    part = 2 * width // steps
    span = cut + (cut // 2 if paired else cut) + part

    def full(i):
        return (0, 0)

    def along(i):
        return (0, i)

    token = pl.BlockSpec((rows, width), full)
    vec = pl.BlockSpec((1, width), full)
    act = shape((rows, width), BF16)
    mine = [shape((rows, ff // 2), BF16)] if paired else []
    turned, turned_spec = shape((width, rows), BF16), pl.BlockSpec((width, rows), full)
    wide = shape((rows, width), F32)
    return launch(
        functools.partial(mlp_kernel, paired, freq_parts),
        (steps,),
        (tok, convt, second, wo, ob, gain, bias, wup, b1, active_grad, cot),
        [
            token,
            turned_spec,
            token,
            pl.BlockSpec((width, width), full),
            vec,
            vec,
            vec,
            pl.BlockSpec((width, cut), along),
            pl.BlockSpec((1, cut), along),
            pl.BlockSpec((rows, cut), along),
            token,
        ],
        (shape((rows, span * steps), BF16), wide, shape((1, ff), F32), wide, turned, act, turned, turned, shape((8, width), F32), *mine),
        (
            pl.BlockSpec((rows, span), along),
            token,
            pl.BlockSpec((1, cut), along),
            token,
            turned_spec,
            token,
            turned_spec,
            turned_spec,
            pl.BlockSpec((8, width), full),
            *[pl.BlockSpec((rows, cut // 2), along) for _ in mine],
        ),
        [pltpu.VMEM((rows, width), BF16), pltpu.VMEM((steps, rows, part), BF16), pltpu.VMEM((rows, width), BF16), pltpu.VMEM((rows, width), F32)],
        cost(2 * rows * width * (2 * ff + width), wup.size * 4 + rows * ff * 4 + rows * width * 14, rows * ff),
        "mix_out_mlp",
        after,
        carry,
    )


def unpacked(pack, hidden, steps, cut):
    rows = pack.shape[0]
    blocks = pack.reshape(rows, steps, -1)
    tail = blocks[:, :, cut + hidden :].reshape(rows, -1)
    return blocks[:, :, :cut].reshape(rows, -1), blocks[:, :, cut : cut + hidden].reshape(rows, -1), tail[:, : tail.shape[1] // 2], tail[:, tail.shape[1] // 2 :]


def put_halves(value, mine, other, half, core, freq_parts):
    per = value.shape[0] // freq_parts
    even = [value[(2 * k) * per : (2 * k + 1) * per] for k in range(freq_parts // 2)]
    odd = [value[(2 * k + 1) * per : (2 * k + 2) * per] for k in range(freq_parts // 2)]

    base = half * per * (freq_parts // 2)

    def put(ref, blocks):
        for k, block in enumerate(blocks):
            ref[base + k * per : base + (k + 1) * per] = block

    @pl.when(core == 0)
    def _():
        put(mine, even)
        put(other, odd)

    @pl.when(core == 1)
    def _():
        put(mine, odd)
        put(other, even)


def block_out_kernel(act, wdown, res, b2, out, acc):
    step = pl.program_id(0)
    part = mm(act[...], wdown[...])

    @pl.when(step == 0)
    def _():
        acc[...] = res[...] + b2[...] + part

    @pl.when(step > 0)
    def _():
        acc[...] += part

    @pl.when(step == pl.num_programs(0) - 1)
    def _():
        out[...] = acc[...].astype(BF16)


def block_out_call(pack, wdown, res, b2, cut, after=(), carry=()):
    rows, width = res.shape
    ff = wdown.shape[0]
    step = pack.shape[1] // ff
    if step * ff != pack.shape[1]:
        pack, step = unpacked(pack, cut, ff // cut, cut)[0], 1

    def full(i):
        return (0, 0)

    token = pl.BlockSpec((rows, width), full)
    return launch(
        block_out_kernel,
        (ff // cut,),
        (pack, wdown, res, b2),
        [pl.BlockSpec((rows, cut), lambda i: (0, step * i)), pl.BlockSpec((cut, width), lambda i: (i, 0)), token, pl.BlockSpec((1, width), full)],
        (shape((rows, width), BF16),),
        (token,),
        [pltpu.VMEM((rows, width), F32)],
        cost(2 * rows * width * ff, wdown.size * 2 + rows * ff * 2 + rows * width * 8),
        "block_out",
        after,
        carry,
    )


def back_kernel(mgt, value, gate, sgrad, weight, tok, gain, rgrad, out, vecs, mg, acc):
    step = pl.program_id(0)

    @pl.when(step == 0)
    def _():
        mg[...] = mgt[...].astype(F32).T.astype(BF16)
        acc[...] = mm(sgrad[...], weight[...], NT)

    @pl.when(step == 1)
    def _():
        pv = (gate[...].astype(F32) * mg[...].astype(F32)).astype(BF16)
        acc[...] += mm(pv, weight[...], NT)
        vecs[2:3] = jnp.sum(pv.astype(F32), axis=0, keepdims=True)

    @pl.when(step == 2)
    def _():
        pg = (value[...].astype(F32) * mg[...].astype(F32)).astype(BF16)
        ng = acc[...] + mm(pg, weight[...], NT)
        vecs[3:4] = jnp.sum(pg.astype(F32), axis=0, keepdims=True)
        n, rate = normalized(tok[...].astype(F32))
        vecs[0:1] = jnp.sum(ng * n, axis=0, keepdims=True)
        vecs[1:2] = jnp.sum(ng, axis=0, keepdims=True)
        e = ng * gain[...]
        pulled = e - jnp.mean(e, axis=-1, keepdims=True) - n * jnp.mean(e * n, axis=-1, keepdims=True)
        out[...] = (rgrad[...] + rate * pulled).astype(BF16)


def back_call(mgt, value, gate, sgrad, weight, tok, gain, rgrad, after=(), carry=()):
    rows, width = tok.shape

    def full(i):
        return (0, 0)

    token = pl.BlockSpec((rows, width), full)
    return launch(
        back_kernel,
        (3,),
        (mgt, value, gate, sgrad, weight, tok, gain, rgrad,),
        [
            pl.BlockSpec((width, rows), full),
            token,
            token,
            token,
            pl.BlockSpec((width, width), lambda i: (0, lax.rem(i + 2, 3))),
            token,
            pl.BlockSpec((1, width), full),
            token,
        ],
        (shape((rows, width), BF16), shape((8, width), F32)),
        (token, pl.BlockSpec((8, width), full)),
        [pltpu.VMEM((rows, width), BF16), pltpu.VMEM((rows, width), F32)],
        cost(2048 * 2 * rows * width * width * 3, 2048 * (weight.size * 2 + rows * width * 16)),
        "project_back",
        after,
        carry,
    )


def owner_part(offs_ref, wt, bias, x, mg, source, batch, tok_rows):
    chans = wt.shape[0] // 2
    vg = mm(wt, x, NT) + bias
    lane = lax.broadcasted_iota(jnp.int32, (1, x.shape[0]), 1)
    limit = jnp.zeros_like(lane)
    for b in range(batch):
        inside = jnp.logical_and(lane >= b * tok_rows, lane < (b + 1) * tok_rows)
        limit = jnp.where(inside, offs_ref[b] + b * tok_rows, limit)
    m = jnp.where(source * tok_rows + lane >= limit, mg.astype(F32), 0.0)
    return jnp.concatenate([vg[chans:] * m, vg[:chans] * m], axis=0).astype(BF16)


def owner_list_kernel(batch, tok_rows, parts, offs_ref, wt, bias, mg, *refs):
    xs, out = refs[:parts], refs[parts]
    me = lax.axis_index("freq")
    total = None
    for r in range(parts):
        x = xs[r][...]
        source = me ^ r
        pg = owner_part(offs_ref, wt[...], bias[...], x, mg[source], source, batch, tok_rows)
        part = mm(pg, x)
        total = part if total is None else total + part
    out[...] = total.astype(BF16)


def owner_grid_kernel(batch, tok_rows, offs_ref, wt, bias, mg, x, out, acc):
    step = pl.program_id(0)

    @pl.when(step == 0)
    def _():
        acc[...] = jnp.zeros_like(acc)

    pg = owner_part(offs_ref, wt[...], bias[...], x[0], mg[0], step, batch, tok_rows)
    acc[...] += mm(pg, x[0])

    @pl.when(step == pl.num_programs(0) - 1)
    def _():
        out[...] = acc[...].astype(BF16)


def owner_call(offsets, wt, bias, mg, xs, batch, tok_rows, after=(), carry=()):
    chans, rows = mg.shape[1:]
    width = wt.shape[1]
    listed = isinstance(xs, list)
    count = mg.shape[0]
    if listed:
        kernel = functools.partial(owner_list_kernel, batch, tok_rows, count)
        grid, x_specs, scratch, mg_spec = (1,), [whole((rows, width))] * count, [], whole(mg.shape)
    else:
        kernel = functools.partial(owner_grid_kernel, batch, tok_rows)
        xs = [xs]
        grid, x_specs = (count,), [pl.BlockSpec((1, rows, width), lambda i: (i, 0, 0))]
        scratch = [pltpu.VMEM((2 * chans, width), F32)]
        mg_spec = pl.BlockSpec((1, chans, rows), lambda i: (i, 0, 0))
    return launch(
        kernel,
        grid,
        (offsets, wt, bias, mg, *xs,),
        [smem(), whole(wt.shape), whole(bias.shape), mg_spec] + x_specs,
        (shape((2 * chans, width), BF16),),
        (whole((2 * chans, width)),),
        scratch,
        cost(8 * count * rows * chans * width, count * rows * width * 2),
        "owner_gradients",
        after,
        carry,
    )


def once(value, after):
    def nothing(after_ref, value_ref, out_ref):
        pass

    return pl.pallas_call(
        nothing,
        out_shape=shape(value.shape, value.dtype),
        in_specs=[anywhere(), anywhere()],
        out_specs=anywhere(),
        input_output_aliases={1: 0},
        name="gate",
    )(after, value)


def bit_order(chips, low_first):
    bits = list(range(chips.bit_length() - 1))
    return bits if low_first else bits[::-1]


def place_of(rel, order):
    place = 0
    for level, bit in enumerate(order):
        digit = lax.shift_right_logical(rel, bit) & 1
        place = place + digit * (1 << (len(order) - 1 - level))
    return place


def store_slot(keep, send, place, index, block):
    half = keep.shape[0]

    @pl.when(place < half)
    def _():
        keep[(place,) + index] = block

    @pl.when(place >= half)
    def _():
        send[(place - half,) + index] = block


def rows_kernel(chips, per, chip_order, dp_order, cot, act, cot_p, act_p, keep, send):
    chip = lax.axis_index("freq") // 2
    quarter = pl.program_id(0) ^ lax.axis_index("dp")
    total = (mm(cot[...], act[...]) + mm(cot_p[...], act_p[...])).astype(BF16)
    for k in range(chips):
        place = place_of(jnp.int32(k) ^ chip, chip_order)
        store_slot(keep, send, place_of(quarter, dp_order), (place,), total[k * per : (k + 1) * per])


def rows_pair(own, partner, width, dp, chips, low_first, after=(), carry=()):
    half, inner = own[0].shape
    per = half // chips
    out = shape((dp // 2, chips, per, width), BF16)
    arrays, specs = [], []
    for cot, pack in (own, partner):
        arrays += [cot, pack]
        specs += [whole(cot.shape), pl.BlockSpec((inner, width), lambda i: (0, 2 * i))]
    return launch(
        functools.partial(rows_kernel, chips, per, bit_order(chips, low_first), bit_order(dp, True)),
        (dp,),
        tuple(arrays),
        specs,
        (out, out),
        (whole(out.shape), whole(out.shape)),
        [],
        cost(4 * dp * half * inner * width, dp * inner * width * 4),
        "fc2_gradient",
        after,
        carry,
    )


def rows_plain(cot, act, cot_p, act_p, dp, chips, low_first):
    total = (mm(cot, act) + mm(cot_p, act_p)).astype(BF16)
    blocks = total.reshape(chips, cot.shape[0] // chips, dp, -1).transpose(2, 0, 1, 3)
    blocks = jnp.concatenate(halves_of(blocks.transpose(1, 0, 2, 3), bit_order(chips, low_first)), axis=0).transpose(1, 0, 2, 3)
    return halves_of(blocks, bit_order(dp, True), lax.axis_index("dp"))


def mixer_kernel(chips, per, order, turned, ga, gb, normed, turned_p, ga_p, gb_p, normed_p, keep, send):
    step = pl.program_id(0)
    chip = lax.axis_index("freq") // 2

    def put(half, total):
        for k in range(chips):
            place = place_of(jnp.int32(k) ^ chip, order)
            store_slot(keep, send, place, (slice(half * per, (half + 1) * per), slice(None)), total[k * per : (k + 1) * per].astype(BF16))

    @pl.when(step == 0)
    def _():
        def out(t, a, b):
            return jnp.concatenate([mm(t[...], a[...]), mm(t[...], b[...])], axis=1)

        put(0, out(turned, ga, gb) + out(turned_p, ga_p, gb_p))

    @pl.when(step == 1)
    def _():
        put(1, mm(turned[...], normed[...]) + mm(turned_p[...], normed_p[...]))


def mixer_pair(own, partner, width, chips, low_first, after=(), carry=()):
    order = bit_order(chips, low_first)
    half = width // 2
    per = half // chips
    out = shape((chips // 2, 2 * per, width), BF16)
    arrays, specs = [], []
    for turned, pack, normed in (own, partner):
        inner = turned.shape[1]
        arrays += [turned, pack, pack, normed]
        specs += [
            pl.BlockSpec((half, inner), lambda i: (i, 0)),
            pl.BlockSpec((inner, half), lambda i: (0, 3)),
            pl.BlockSpec((inner, half), lambda i: (0, 7)),
            whole(normed.shape),
        ]
    return launch(
        functools.partial(mixer_kernel, chips, per, order),
        (2,),
        tuple(arrays),
        specs,
        (out, out),
        (whole(out.shape), whole(out.shape)),
        [],
        cost(8 * half * inner * width, 4 * inner * width * 4),
        "mixer_gradient",
        after,
        carry,
    )


def halves_of(blocks, order, chip=None):
    chips = blocks.shape[0]
    chip = lax.axis_index("freq") // 2 if chip is None else chip
    picks = np.zeros(chips, np.int32)
    for rel in range(chips):
        place = sum(((rel >> bit) & 1) << (len(order) - 1 - level) for level, bit in enumerate(order))
        picks[place] = rel
    moved = jnp.take(blocks, jnp.asarray(picks) ^ chip, axis=0)
    return moved[: chips // 2], moved[chips // 2 :]


def cols_kernel(order, la, lb, rt, lap, lbp, rtp, keep, send, left):
    step = pl.program_id(0)
    chip = lax.axis_index("freq") // 2
    half = la.shape[1]

    @pl.when(step == 0)
    def _():
        for k, ref in enumerate((la, lb, lap, lbp)):
            left[k // 2, (k % 2) * half : (k % 2 + 1) * half] = ref[...].astype(F32).T.astype(BF16)

    total = (mm(left[0], rt[...]) + mm(left[1], rtp[...])).astype(BF16)
    store_slot(keep, send, place_of(step ^ chip, order), (), total)


def cols_pair(mine, pack, pack_p, width, cut, chips, low_first, after=(), carry=()):
    order = bit_order(chips, low_first)
    rows = mine.shape[0]
    per = mine.shape[1] // chips
    last = pack.shape[1] // per - 1
    step = pack.shape[1] // chips // per
    out = shape((chips // 2, width, per), BF16)
    out_spec = pl.BlockSpec((chips // 2, width, per), lambda i: (0, 0, 0))

    def at(place):
        return pl.BlockSpec((rows, per), place)

    first, second = (lambda i: (0, last - step)), (lambda i: (0, last))
    return launch(
        functools.partial(cols_kernel, order),
        (chips,),
        (pack, pack, mine, pack_p, pack_p, pack_p),
        [at(first), at(second), at(lambda i: (0, i)), at(first), at(second), at(lambda i: (0, step * i + 2))],
        (out, out),
        (out_spec, out_spec),
        [pltpu.VMEM((2, width, rows), BF16)],
        cost(4 * width * rows * mine.shape[1], (width * rows + rows * mine.shape[1] * 2) * 4),
        "fc1_gradient",
        after,
        carry,
    )


def cols_plain(lt, rt, ltp, rtp, chips, low_first):
    total = (mm(lt.T, rt) + mm(ltp.T, rtp)).astype(BF16)
    return halves_of(total.reshape(lt.shape[1], chips, -1).transpose(1, 0, 2), bit_order(chips, low_first))


def flip(value, freq_parts, bit):
    return lax.ppermute(value, "freq", [(i, i ^ bit) for i in range(freq_parts)])


def begin(keep, send, axis, bit):
    count = lax.axis_size(axis)
    return keep, lax.ppermute(send, axis, [(i, i ^ bit) for i in range(count)])


def finish(pending):
    return pending[0].astype(F32) + pending[1].astype(F32)


def step_on(pending, axis, bits, level):
    if level == len(bits):
        return finish(pending)[0], None
    half = pending[0].shape[0] // 2
    send = finish([v[half:] for v in pending]).astype(BF16)
    keep = finish([v[:half] for v in pending]).astype(BF16)
    return begin(keep, send, axis, bits[level]), send


def across_first(blocks):
    blocks = blocks.astype(BF16)
    count = blocks.shape[0]
    me = lax.axis_index("dp")
    blocks = blocks.reshape((count // 2, 2) + blocks.shape[1:])
    send = lax.dynamic_index_in_dim(blocks, 1 - me % 2, 1, keepdims=False)
    keep = lax.dynamic_index_in_dim(blocks, me % 2, 1, keepdims=False)
    return begin(keep, send, "dp", 1), send


def across_next(pending):
    total = finish(pending)
    me, count = lax.axis_index("dp"), lax.axis_size("dp")
    step = count // total.shape[0]
    total = total.astype(BF16)
    total = total.reshape((total.shape[0] // 2, 2) + total.shape[1:])
    mine = me // step % 2
    send = lax.dynamic_index_in_dim(total, 1 - mine, 1, keepdims=False)
    keep = lax.dynamic_index_in_dim(total, mine, 1, keepdims=False)
    return begin(keep, send, "dp", step), send


def across_rest(pending):
    while pending[0].shape[0] > 1:
        pending, _ = across_next(pending)
    return finish(pending)[0]


def pack_kernel(chans, one, two, b2, b1, skip, out):
    dp, freq = out.shape[:2]
    me = lax.axis_index("freq")
    column = jnp.broadcast_to(skip[...], (chans, 128)).T[0:1, :]
    per = b1.shape[1] // (freq * chans)

    def put(f, start, value):
        for d in range(dp):
            out[d, f, start : start + value.shape[0]] = value

    for f in range(freq):
        cut = slice(f * chans, (f + 1) * chans)
        put(f, 0, one[0:2, cut])
        for r in range(3):
            group, chunk = divmod(3 * f + r, freq)
            source = (one[2:3], one[3:4], two[3:4])[group]
            put(f, 2 + r, source[:, chunk * chans : (chunk + 1) * chans])
        put(f, 5, two[0:3, cut])
        put(f, 8, b2[:, cut])
        for r in range(per):
            start = (f * per + r) * chans
            put(f, 9 + r, b1[:, start : start + chans])
        put(f, 9 + per, jnp.where(me == f, column, 0.0))
    for d in range(dp):
        for f in range(freq):
            out[d, f, 10 + per :] = jnp.zeros((out.shape[2] - 10 - per, chans), F32)


def packed_vectors(one, two, b2, b1, skip, dp, freq, after=(), carry=()):
    chans = one.shape[1] // freq
    lines = 16
    if freq == 8:
        return launch(
            functools.partial(pack_kernel, chans),
            (1,),
            (one, two, b2, b1, skip),
            [whole(v.shape) for v in (one, two, b2, b1, skip)],
            (shape((dp, freq, lines, chans), F32),),
            (whole((dp, freq, lines, chans)),),
            [],
            cost(1, 1),
            "pack_vectors",
            after,
            carry,
        )
    own = (jnp.arange(freq, dtype=jnp.int32) == lax.axis_index("freq")).astype(F32)[:, None, None] * skip.reshape(1, 1, chans)
    rows = jnp.concatenate([one[:2], two[:3], b2]).reshape(6, freq, chans).transpose(1, 0, 2)
    bias_in = jnp.concatenate([one[2:4], two[3:4]]).reshape(freq, 3, chans)
    rows = jnp.concatenate([rows[:, :2], bias_in, rows[:, 2:], b1.reshape(freq, -1, chans), own], axis=1)
    return jnp.broadcast_to(rows[None], (dp,) + rows.shape), carry


def to_all(block):
    dp, freq = lax.axis_size("dp"), lax.axis_size("freq")
    wide = block if block.ndim == 4 else jnp.broadcast_to(block[None], (dp,) + block.shape)
    wide = wide.reshape((dp * freq,) + wide.shape[2:])
    return lax.all_to_all(wide, ("dp", "freq"), split_axis=0, concat_axis=0, tiled=True)


def reblocked(blocks, count, width):
    if blocks.shape[0] == count and blocks.shape[2] == width:
        return blocks
    whole = blocks.transpose(1, 0, 2).reshape(blocks.shape[1], -1)
    need = count * width
    whole = jnp.pad(whole, ((0, 0), (0, max(0, need - whole.shape[1]))))[:, :need]
    return whole.reshape(-1, count, width).transpose(1, 0, 2)


def body(tokens, offsets, kernel_lengths, norm1_gain, norm1_bias, w_in, in_bias, kernel_taps, skip_gain, w_out, out_bias, norm2_gain, norm2_bias, w_up, fc1_bias, w_down, fc2_bias, cotangent):
    freq = lax.axis_size("freq")
    dp = lax.axis_size("dp")
    chips = freq // 2
    batch, tok_rows, width = tokens.shape
    rows = batch * tok_rows
    ff = w_up.shape[1]
    chans = width // freq
    me = lax.axis_index("freq")
    core = lax.rem(me, 2)

    def row(v):
        return v.reshape(1, -1)

    tok = tokens.reshape(rows, width)
    cot = cotangent.reshape(rows, width)
    tap_rows = kernel_taps.shape[1]
    reach = -(-freq * tap_rows // tok_rows)
    lens = lax.dynamic_slice_in_dim(kernel_lengths, me * chans, chans).reshape(chans, 1)
    skip = skip_gain.reshape(chans, 1)

    def swap(v):
        return flip(v, freq, 1)

    cut = 768
    normed, mixed_t, value, gate, gate_two = front_call(
        tok, offsets, norm1_gain, norm1_bias, w_in, row(in_bias), kernel_taps, batch, tok_rows
    )
    mixed = lax.all_to_all(mixed_t.reshape(freq, chans, -1), "freq", split_axis=0, concat_axis=0, tiled=True)
    taps = mixed if tap_rows == tok_rows else reblocked(mixed[:, :, rows:], reach, tok_rows)
    active_grad, b2g, cot_mine, cot_other = active_grad_call(cot, w_down, cut, freq, after=(mixed_t,))
    own_w = jnp.concatenate([lax.dynamic_slice_in_dim(w_in, k * width + me * chans, chans, axis=1) for k in range(2)], axis=1).T
    own_b = jnp.concatenate([lax.dynamic_slice_in_dim(in_bias, k * width + me * chans, chans) for k in range(2)]).reshape(-1, 1)
    (conv, k_spec), (cot_p, normed_p, normed) = forward_call(mixed, batch, tok_rows, taps, lens, skip, after=(active_grad, own_w, own_b), carry=(swap(cot_other), swap(normed), normed))
    conv_t = lax.all_to_all(conv, "freq", split_axis=0, concat_axis=0, tiled=True).reshape(width, rows)
    near = []
    if freq == 8:
        near = [flip(normed, freq, 2), flip(normed, freq, 4), flip(normed, freq, 6)]
    paired = freq == 8 and ff == 4 * cut
    pack, res, b1g, rgrad, convg_t, sgrad, turned, turned_other, vec_two, *mine = mlp_call(
        tok, conv_t, gate_two, w_out, row(out_bias), row(norm2_gain), row(norm2_bias), w_up, row(fc1_bias), active_grad, cot, cut, paired, freq
    )
    mine = mine[0] if paired else None
    block_out = block_out_call(pack, w_down, res, row(fc2_bias), cut)
    convg = lax.all_to_all(convg_t.reshape(freq, chans, rows), "freq", split_axis=0, concat_axis=0, tiled=True)
    half = width // 2
    if paired:
        pack_p, turned_p = swap(pack), swap(turned_other)
        fc2, near = rows_pair((cot_mine, pack), (cot_p, pack_p), width, dp, chips, True, after=(block_out,), carry=near)
        fc1 = cols_pair(mine, pack, pack_p, width, cut, chips, False, after=(fc2[1],))
        far = [swap(v) for v in near]
        mixed_grad = adjoint_call(convg, batch, k_spec, skip, after=(fc1[1],))
        mixer = mixer_pair((turned, pack, normed), (turned_p, pack_p, normed_p), width, chips, True, after=(mixed_grad,))
        normed_all = [v for pair_of in zip([normed, *near], [normed_p, *far]) for v in pair_of]
    else:
        normed_all = lax.all_gather(normed, "freq", axis=0, tiled=False)
        act, hg, gated, n2 = unpacked(pack, cut, ff // cut, cut)
        hg = hg.reshape(rows, chips, 2, ff // freq)
        hg_mine = jnp.take(hg, core, axis=2).reshape(rows, ff // 2)
        hg_other = jnp.take(hg, 1 - core, axis=2).reshape(rows, ff // 2)
        act_p, gated_p, n2_p, turned_p = swap(act), swap(gated), swap(n2), swap(turned_other)
        fc2 = rows_plain(cot_mine, act, cot_p, act_p, dp, chips, True)
        fc1 = cols_plain(n2, hg_mine, n2_p, swap(hg_other), chips, False)
        mixer = []
        for lt, rt, ltp, rtp in ((turned[:half], gated, turned_p[:half], gated_p), (turned[half:], normed, turned_p[half:], normed_p)):
            mixer.append((mm(lt, rt) + mm(ltp, rtp)).astype(BF16).reshape(chips, -1, width))
        mixer = halves_of(jnp.concatenate(mixer, axis=1), bit_order(chips, True))
        mixed_grad = adjoint_call(convg, batch, k_spec, skip)
    mixed_grad_t = lax.all_to_all(mixed_grad, "freq", split_axis=0, concat_axis=0, tiled=True).reshape(width, rows)
    low, high = ([2 << bit for bit in bit_order(chips, first)] for first in (True, False))
    deep = [1 << bit for bit in bit_order(dp, True)]
    fc2_sum, fc1_sum, mixer_sum = begin(*fc2, "dp", deep[0]), begin(*fc1, "freq", high[0]), begin(*mixer, "freq", low[0])
    owned, (keep, keep_m) = owner_call(
        offsets, own_w, own_b, mixed_grad, normed_all, batch, tok_rows, after=(mixer[1],), carry=(fc2_sum[0], mixer_sum[0])
    )
    fc2_sum, sent = step_on((keep, fc2_sum[1]), "dp", deep, 1)
    mixer_sum, sent_m = step_on((once(keep_m, sent), mixer_sum[1]), "freq", low, 1)
    (taps_g, skip_g), (keep, keep_1, keep_m) = taps_grad_call(
        mixed, convg, lens, tok_rows, reach, after=(owned, sent_m), carry=(fc2_sum[0], fc1_sum[0], mixer_sum[0])
    )
    fc2_sum = (keep, fc2_sum[1])
    taps_g = reblocked(taps_g, freq, tap_rows).reshape(freq, dp, chans // dp, tap_rows).transpose(1, 0, 2, 3).reshape(dp, width // dp, tap_rows)
    taps_sum, sent_t = across_first(taps_g)
    fc1_sum, sent_1 = step_on((once(keep_1, sent_t), fc1_sum[1]), "freq", high, 1)
    mixer_sum = (once(keep_m, sent_1), mixer_sum[1])
    for level in range(2, len(low) + 1):
        mixer_sum, _ = step_on(mixer_sum, "freq", low, level)
    mixer = mixer_sum.astype(BF16)
    parts = jnp.concatenate([owned, mixer[chans:]]).reshape(3, chans, width)
    pieces, moved = [], []
    for r in range(3):
        part = lax.rem((freq % 3) * (r - me + 3 * freq), 3)
        moved.append(lax.dynamic_index_in_dim(parts, part, 0, keepdims=False))
        pieces.append(lax.ppermute(moved[-1], "freq", [((3 * d + r) % freq, d) for d in range(freq)]))
    (input_grad, vec_one), (keep, keep_1, keep_t) = back_call(
        mixed_grad_t, value, gate, sgrad, w_in, tok, row(norm1_gain), rgrad,
        after=tuple(moved), carry=(fc2_sum[0], fc1_sum[0], taps_sum[0]),
    )
    fa = ff // freq
    fc1_sum = (keep_1, fc1_sum[1])
    for level in range(2, len(high) + 1):
        fc1_sum, _ = step_on(fc1_sum, "freq", high, level)
    first, sent_1 = across_first(fc1_sum.reshape(dp, width // dp, fa))
    vectors, (keep, keep_t) = packed_vectors(vec_one, vec_two, b2g, b1g, skip_g, dp, freq, after=(sent_1,), carry=(keep, keep_t))
    final = to_all(vectors)
    taps_sum, sent_t = across_next((keep_t, taps_sum[1]))
    second = jnp.concatenate(pieces + [once(mixer[:chans], sent_t)], axis=0).T.reshape(dp, width // dp, 4 * chans)
    second, sent = across_first(second)
    first = (once(first[0], sent), first[1])
    first, sent = across_next(first)
    fc2_sum = (once(keep, sent), fc2_sum[1])
    for level in range(2, len(deep)):
        fc2_sum, _ = step_on(fc2_sum, "dp", deep, level)
    half = chips // 2
    sent = finish([v[0, half:] for v in fc2_sum]).astype(BF16)
    fc2_sum = begin(finish([v[0, :half] for v in fc2_sum]).astype(BF16), sent, "freq", low[0])
    second, sent = across_next((once(second[0], sent), second[1]))
    quarter_sum = across_rest((once(taps_sum[0], sent), taps_sum[1])).astype(BF16).reshape(freq, chans // dp, tap_rows)
    spread = to_all(quarter_sum)
    for level in range(1, len(low) + 1):
        fc2_sum, _ = step_on(fc2_sum, "freq", low, level)
    first, second = across_rest(first), across_rest(second)
    fc1_final, in_final, out_final = first, second[:, : 3 * chans], second[:, 3 * chans :]
    fc2_final = fc2_sum.T
    spread = spread.reshape(dp, freq, chans // dp, tap_rows).transpose(1, 0, 2, 3).reshape(width, tap_rows)
    taps_final = spread.astype(F32) * jnp.square(jnp.tanh(kernel_taps / SHRINK))
    final = jnp.sum(final, axis=0)
    n1g, n1b = final[0], final[1]
    inb = final[2:5].reshape(-1)
    n2g, n2b, outb, b2f = (final[k] for k in range(5, 9))
    lines = ff // width
    b1f, skg = final[9 : 9 + lines].reshape(-1), final[9 + lines]
    return (
        block_out.reshape(tokens.shape),
        input_grad.reshape(tokens.shape),
        n1g,
        n1b,
        in_final,
        inb,
        taps_final,
        skg,
        out_final,
        outb,
        n2g,
        n2b,
        fc1_final,
        b1f,
        fc2_final,
        b2f,
    )


def solution(mesh):
    token, whole, lead = P("dp", "freq", None), P(), P("freq")
    both = P("dp", "freq")
    in_specs = (token, P("dp"), whole, whole, whole, whole, whole, P(None, "freq"), lead) + (whole,) * 8 + (token,)
    out_specs = (token, token, lead, lead, both, lead, P(None, "freq"), lead, both, lead, lead, lead, both, lead, both, lead)
    return jax.shard_map(body, mesh=mesh, in_specs=in_specs, out_specs=out_specs, check_vma=False)
```

```python
import functools

import jax
import jax.numpy as jnp
import numpy as np
from jax import lax
from jax.experimental import pallas as pl
from jax.experimental.pallas import tpu as pltpu
from jax.sharding import PartitionSpec as P

NORM_EPS = 1e-05
SHRINK = 0.003
GELU_C = 0.7978845608028654
GELU_A = 0.044715
F32 = jnp.float32
BF16 = jnp.bfloat16
MIB = 1 << 20

NN = (((1,), (0,)), ((), ()))
NT = (((1,), (1,)), ((), ()))


def mm(left, right, dims=NN):
    return lax.dot_general(left, right, dims, preferred_element_type=F32)


def whole(dims):
    return pl.BlockSpec(tuple(dims), lambda i: (0,) * len(dims))


def anywhere():
    return pl.BlockSpec(memory_space=pl.ANY)


def smem():
    return pl.BlockSpec(memory_space=pltpu.SMEM)


def shape(dims, dtype):
    return jax.ShapeDtypeStruct(dims, dtype)


def launch(kernel, grid, ins, in_specs, outs, out_specs, scratch, estimate, name, after=(), carry=()):
    count, extra, given = len(ins), len(after) + len(carry), len(outs)

    def run(*refs):
        made = refs[count + extra : count + extra + given]
        kernel(*refs[:count], *made, *refs[count + extra + given + len(carry) :])

    first = count + len(after)
    results = pl.pallas_call(
        run,
        grid=grid,
        out_shape=tuple(outs) + tuple(shape(v.shape, v.dtype) for v in carry),
        in_specs=list(in_specs) + [anywhere()] * extra,
        out_specs=tuple(out_specs) + (anywhere(),) * len(carry),
        scratch_shapes=scratch,
        input_output_aliases={first + k: given + k for k in range(len(carry))},
        compiler_params=pltpu.CompilerParams(vmem_limit_bytes=60 * MIB, dimension_semantics=("arbitrary",)),
        cost_estimate=estimate,
        name=name,
    )(*ins, *after, *carry)
    made = results[0] if given == 1 else results[:given]
    return (made, results[given:]) if carry else made


def cost(flops, moved, special=0):
    return pl.CostEstimate(flops=int(flops) * 64, bytes_accessed=int(moved) * 64, transcendentals=0)


def split16(table):
    high = np.asarray(table, np.float32).astype(jnp.bfloat16)
    low = (np.asarray(table, np.float64) - high.astype(np.float64)).astype(np.float32).astype(jnp.bfloat16)
    return high, low


@functools.lru_cache(maxsize=None)
def tables(width):
    order = np.concatenate([np.arange(0, width, 2), np.arange(1, width, 2)])
    turns = (2 * order[None, :] + 1) * np.arange(width)[:, None] % (4 * width)
    angle = np.pi * turns / (2 * width)
    forward = np.concatenate([np.cos(angle), -np.sin(angle)], axis=1)
    inverse = forward.T / width
    return split16(forward) + split16(inverse)


def split_value(value):
    high = value.astype(BF16)
    return high, (value - high.astype(F32)).astype(BF16)


def spectrum_of(block, fhi):
    return mm(block, fhi)


def signal_of(spec, ghi):
    high, low = split_value(spec)
    return mm(high, ghi) + mm(low, ghi)


def each(count, step, unroll):
    if unroll:
        for i in range(count):
            step(i)
    else:
        lax.fori_loop(0, count, lambda i, c: (step(i), c)[1], 0)


def blocks_to_spectra(x_ref, spec_ref, fhi, batch, width):
    count, chans = x_ref.shape[0], x_ref.shape[1]
    for b in range(batch):
        lanes = slice(b * width, (b + 1) * width)
        if chans % 16 == 0:
            rows = x_ref[:, :, lanes].reshape(count * chans, width)
            spec_ref[b] = spectrum_of(rows, fhi[...]).reshape(count, chans, 2 * width)
        else:

            def step(j, b=b, lanes=lanes):
                spec_ref[b, j] = spectrum_of(x_ref[j, :, lanes], fhi[...])

            each(count, step, False)


def tiles(chans, width, step):
    lane_tiles = width // 128

    def rows_step(rt):
        start = rt * 8 if isinstance(rt, int) else pl.multiple_of(rt * 8, 8)
        for lane in range(lane_tiles):
            step(pl.ds(start, 8), lane)

    each(chans // 8, rows_step, False)


def pair(ref, lead, rows, lane, width):
    return (
        ref[lead + (rows, slice(lane * 128, (lane + 1) * 128))],
        ref[lead + (rows, slice(width + lane * 128, width + (lane + 1) * 128))],
    )


def put_pair(ref, lead, rows, lane, width, value):
    ref[lead + (rows, slice(lane * 128, (lane + 1) * 128))] = value[0]
    ref[lead + (rows, slice(width + lane * 128, width + (lane + 1) * 128))] = value[1]


def times(a, k):
    return a[0] * k[0] - a[1] * k[1], a[0] * k[1] + a[1] * k[0]


def times_conj(a, k):
    return a[0] * k[0] + a[1] * k[1], a[1] * k[0] - a[0] * k[1]


def plus(a, b):
    return b if a is None else (a[0] + b[0], a[1] + b[1])


def quarter(now, before, sign):
    if before is None:
        return now
    if sign > 0:
        return now[0] - before[1], now[1] + before[0]
    return now[0] + before[1], now[1] - before[0]


def wide_quarter(now, before, width):
    lane = lax.broadcasted_iota(jnp.int32, (1, width), 1)
    sign = jnp.where(lane < width // 2, 1.0, -1.0)
    return jnp.concatenate(
        [now[:, :width] - sign * before[:, width:], now[:, width:] + sign * before[:, :width]], axis=1
    )


def wide_times(a, k, width, conj):
    ar, ai, kr, ki = a[:, :width], a[:, width:], k[:, :width], k[:, width:]
    if conj:
        return jnp.concatenate([ar * kr + ai * ki, ai * kr - ar * ki], axis=1)
    return jnp.concatenate([ar * kr - ai * ki, ar * ki + ai * kr], axis=1)


UNROLLED = 8


def small(count, chans, width):
    return count <= UNROLLED and chans % 16 == 0 and width % 256 == 0


def conv_products(spec_ref, k_ref, z_ref, batch, width, adjoint):
    reach, chans = k_ref.shape[0], k_ref.shape[1]
    count = spec_ref.shape[1]
    if small(count, chans, width):

        def step(rows, lane):
            k = [pair(k_ref, (d,), rows, lane, width) for d in range(reach)]
            for b in range(batch):
                x = [pair(spec_ref, (b, j), rows, lane, width) for j in range(count)]
                for i in range(count):
                    total = None
                    if adjoint:
                        for d in range(min(count - i, reach)):
                            total = plus(total, times_conj(x[i + d], k[d]))
                    else:
                        for d in range(min(i + 1, reach)):
                            total = plus(total, times(x[i - d], k[d]))
                    put_pair(z_ref, (b, i), rows, lane, width, total)

        tiles(chans, width, step)
        return
    for b in range(batch):

        def row(i, b=b):
            def term(d, total):
                src = i + d if adjoint else i - d
                return total + wide_times(spec_ref[b, src], k_ref[d], width, adjoint)

            terms = jnp.minimum(count - i if adjoint else i + 1, reach)
            z_ref[b, i] = lax.fori_loop(0, terms, term, jnp.zeros((chans, 2 * width), F32))

        each(count, row, False)


def conv_body(adjoint, batch, x_ref, k_ref, skip_ref, fhi, ghi, out_ref, spec_ref, z_ref):
    count, chans = x_ref.shape[:2]
    width = fhi.shape[0]
    blocks_to_spectra(x_ref, spec_ref, fhi, batch, width)
    conv_products(spec_ref, k_ref, z_ref, batch, width, adjoint)
    for b in range(batch):
        cut = slice(b * width, (b + 1) * width)
        if chans % 16 == 0:
            y = signal_of(z_ref[b].reshape(count * chans, 2 * width), ghi[...])
            y = y.reshape(count, chans, width) + skip_ref[...][None] * x_ref[:, :, cut].astype(F32)
            out_ref[:, :, cut] = y.astype(BF16)
        else:

            def step(j, b=b, cut=cut):
                y = signal_of(z_ref[b, j], ghi[...])
                out_ref[j, :, cut] = (y + skip_ref[...] * x_ref[j, :, cut].astype(F32)).astype(BF16)

            each(count, step, False)


def forward_kernel(batch, x_ref, s_ref, len_ref, skip_ref, fhi, flo, ghi, out_ref, k_ref, spec_ref, z_ref, raw_ref):
    taps_spectra(s_ref, s_ref.shape[2] - fhi.shape[0], len_ref, fhi, flo, k_ref, raw_ref)
    conv_body(False, batch, x_ref, k_ref, skip_ref, fhi, ghi, out_ref, spec_ref, z_ref)


def forward_call(x, batch, width, taps, lens, skip, after=(), carry=()):
    count, chans = x.shape[:2]
    reach = taps.shape[0]
    tabs = tables(width)
    spec = pltpu.VMEM((batch, count, chans, 2 * width), F32)
    span = min(reach + 1, count)
    same = taps is x
    args = (x,) if same else (x, taps)

    def kernel(*refs):
        forward_kernel(batch, refs[0], *(refs if same else refs[1:]))

    return launch(
        kernel,
        (1,),
        (*args, lens, skip, *tabs[:3]),
        [whole(v.shape) for v in (*args, lens, skip, *tabs[:3])],
        (shape((count, chans, batch * width), BF16), shape((span, chans, 2 * width), F32)),
        (whole((count, chans, batch * width)), whole((span, chans, 2 * width))),
        [spec, spec, pltpu.VMEM((reach, chans, 2 * width), F32)],
        cost(x.size * width * 20, x.size * 8 + 4 * width * width * 4),
        "conv_forward",
        after,
        carry,
    )


def adjoint_kernel(batch, *refs):
    conv_body(True, batch, *refs)


def adjoint_call(x, batch, k_spec, skip, after=(), carry=()):
    count, chans, lanes = x.shape
    width = k_spec.shape[2] // 2
    tabs = tables(width)
    spec = pltpu.VMEM((batch, count, chans, 2 * width), F32)
    return launch(
        functools.partial(adjoint_kernel, batch),
        (1,),
        (x, k_spec, skip, tabs[0], tabs[2]),
        [whole(v.shape) for v in (x, k_spec, skip, tabs[0], tabs[2])],
        (shape(x.shape, BF16),),
        (whole(x.shape),),
        [spec, spec],
        cost(x.size * width * 20, x.size * 4 + k_spec.size * 4 + 4 * width * width * 4),
        "conv_adjoint",
        after,
        carry,
    )


def pooled_rows(full):
    span = full.shape[1]
    place = lax.broadcasted_iota(jnp.int32, (1, span), 1)
    before = jnp.where(place == 0, 0.0, pltpu.roll(full, 1, 1))
    after = jnp.where(place == span - 1, 0.0, pltpu.roll(full, span - 1, 1))
    return (before + full + after) / 3.0


def taps_spectra(s_ref, start, len_ref, fhi, flo, out_ref, raw_ref):
    count, chans = s_ref.shape[:2]
    width = fhi.shape[0]
    full = jnp.concatenate([s_ref[d, :, start : start + width].astype(F32) for d in range(count)], axis=1)
    place = lax.broadcasted_iota(jnp.int32, (1, count * width), 1)
    kernel = jnp.where(place < len_ref[...], pooled_rows(full), 0.0)
    for d in range(count):
        high, low = split_value(kernel[:, d * width : (d + 1) * width])
        raw_ref[d] = mm(high, fhi[...]) + (mm(low, fhi[...]) + mm(high, flo[...]))
    out_ref[0] = raw_ref[0]
    for d in range(1, count):
        out_ref[d] = wide_quarter(raw_ref[d], raw_ref[d - 1], width)
    if out_ref.shape[0] > count:
        out_ref[count] = wide_quarter(jnp.zeros((chans, 2 * width), F32), raw_ref[count - 1], width)


def taps_grad_kernel(x_ref, g_ref, len_ref, fhi, ghi, out_ref, skip_ref, xs_ref, gs_ref, z_ref):
    count, chans, lanes = g_ref.shape
    reach = z_ref.shape[0]
    width = fhi.shape[0]
    batch = lanes // width
    blocks_to_spectra(x_ref, xs_ref, fhi, batch, width)
    blocks_to_spectra(g_ref, gs_ref, fhi, batch, width)
    if small(count, chans, width):

        def step(rows, lane):
            sign = 1 if lane < width // 256 else -1
            total = [None] * reach
            for b in range(batch):
                x = [pair(xs_ref, (b, j), rows, lane, width) for j in range(count)]
                x = [quarter(x[j], x[j - 1] if j else None, sign) for j in range(count)]
                for i in range(count):
                    g = pair(gs_ref, (b, i), rows, lane, width)
                    for d in range(min(i + 1, reach)):
                        total[d] = plus(total[d], times_conj(g, x[i - d]))
            for d in range(reach):
                put_pair(z_ref, (d,), rows, lane, width, total[d])

        tiles(chans, width, step)
        rows = signal_of(z_ref[...].reshape(reach * chans, 2 * width), ghi[...])
        rows = rows.reshape(reach, chans, width)
        pieces = [rows[d] for d in range(reach)]
    else:

        def shift(t, c):
            j = count - 1 - t
            for b in range(batch):
                xs_ref[b, j] = wide_quarter(xs_ref[b, j], xs_ref[b, j - 1], width)
            return c

        lax.fori_loop(0, count - 1, shift, 0)

        def lag(d):
            total = jnp.zeros((chans, 2 * width), F32)
            for b in range(batch):

                def term(i, acc, b=b):
                    return acc + wide_times(gs_ref[b, i], xs_ref[b, i - d], width, True)

                total = lax.fori_loop(d, count, term, total)
            z_ref[d] = total

        each(reach, lag, False)
        pieces = [signal_of(z_ref[d], ghi[...]) for d in range(reach)]
    full = jnp.concatenate(pieces, axis=1)
    place = lax.broadcasted_iota(jnp.int32, (1, reach * width), 1)
    full = pooled_rows(jnp.where(place < len_ref[...], full, 0.0))
    if len(out_ref.shape) == 4:
        per = out_ref.shape[2]
        for q in range(out_ref.shape[0]):
            for d in range(reach):
                out_ref[q, d] = full[q * per : (q + 1) * per, d * width : (d + 1) * width].astype(BF16)
    else:
        for d in range(reach):
            out_ref[d] = full[:, d * width : (d + 1) * width].astype(BF16)
    dot = jnp.zeros((chans, lanes), F32)
    for j in range(count):
        dot = dot + x_ref[j, :, :lanes].astype(F32) * g_ref[j].astype(F32)
    skip_ref[...] = jnp.sum(dot, axis=1, keepdims=True)


def taps_grad_call(x, g, lens, width, reach, split, after=(), carry=()):
    count, chans, lanes = g.shape
    batch = lanes // width
    tabs = tables(width)
    spec = pltpu.VMEM((batch, count, chans, 2 * width), F32)
    made = (split, reach, chans // split, width) if split else (reach, chans, width)
    return launch(
        taps_grad_kernel,
        (1,),
        (x, g, lens, tabs[0], tabs[2]),
        [whole(v.shape) for v in (x, g, lens, tabs[0], tabs[2])],
        (shape(made, BF16), shape((chans, 1), F32)),
        (whole(made), whole((chans, 1))),
        [spec, spec, pltpu.VMEM((reach, chans, 2 * width), F32)],
        cost(x.size * width * 20, x.size * 6),
        "taps_gradient",
        after,
        carry,
    )


def normalized(values):
    centred = values - jnp.mean(values, axis=-1, keepdims=True)
    rate = lax.rsqrt(jnp.mean(centred * centred, axis=-1, keepdims=True) + NORM_EPS)
    return centred * rate, rate


def live_rows(offs_ref, batch, tok_rows, rows):
    row = lax.broadcasted_iota(jnp.int32, (rows, 1), 0)
    limit = jnp.zeros((rows, 1), jnp.int32)
    base = lax.axis_index("freq") * tok_rows
    position = base + row
    for b in range(batch):
        inside = jnp.logical_and(row >= b * tok_rows, row < (b + 1) * tok_rows)
        limit = jnp.where(inside, offs_ref[b] + b * tok_rows, limit)
    return position >= limit


def front_kernel(batch, tok_rows, offs_ref, tok, gain, bias, wv, wg, ws, in_bias, taps, normed, mixed, value, gate, second, spread):
    rows = tok.shape[0]
    cut = wv.shape[1]
    per = in_bias.shape[0] // (3 * cut)

    @pl.when(pl.program_id(0) == 0)
    def _():
        n, _ = normalized(tok[...].astype(F32))
        row = in_bias[...].reshape(1, -1)
        for k in range(3 * per):
            spread[k] = row[:, k * cut : (k + 1) * cut]
        normed[...] = (n * gain[...].reshape(1, -1) + bias[...].reshape(1, -1)).astype(BF16)

    x = normed[...]
    step = pl.program_id(0)
    v = mm(x, wv[...]) + spread[step]
    g = mm(x, wg[...]) + spread[per + step]
    live = live_rows(offs_ref, batch, tok_rows, rows)
    mixed[:, :rows] = jnp.where(live, g * v, 0.0).T.astype(BF16)
    t = taps[...]
    mixed[:, rows:] = (t - SHRINK * jnp.tanh(t / SHRINK)).astype(BF16)
    value[...] = jnp.where(live, v, 0.0).astype(BF16)
    gate[...] = jnp.where(live, g, 0.0).astype(BF16)
    second[...] = (mm(x, ws[...]) + spread[2 * per + step]).astype(BF16)


def front_call(tok, offsets, gain, bias, weight, in_bias, taps, batch, tok_rows):
    rows, width = tok.shape
    span = rows + taps.shape[1]
    cut = 256
    per = width // cut

    def full(i):
        return (0, 0)

    def col(part):
        return lambda i: (0, part * per + i)

    act = shape((rows, width), BF16)
    return launch(
        functools.partial(front_kernel, batch, tok_rows),
        (per,),
        (offsets, tok, gain, bias, weight, weight, weight, in_bias, taps),
        [smem(), pl.BlockSpec((rows, width), full), whole((width,)), whole((width,))]
        + [pl.BlockSpec((width, cut), col(k)) for k in range(3)]
        + [whole(in_bias.shape)]
        + [pl.BlockSpec((cut, taps.shape[1]), lambda i: (i, 0))],
        (act, shape((width, span), BF16), act, act, act),
        (
            pl.BlockSpec((rows, width), full),
            pl.BlockSpec((cut, span), lambda i: (i, 0)),
            pl.BlockSpec((rows, cut), lambda i: (0, i)),
            pl.BlockSpec((rows, cut), lambda i: (0, i)),
            pl.BlockSpec((rows, cut), lambda i: (0, i)),
        ),
        [pltpu.VMEM((3 * per, 1, cut), F32)],
        cost(2 * rows * width * 3 * width, weight.size * 2 + rows * width * 12),
        "norm_project",
            )


def active_grad_kernel(freq_parts, cot, wdown, out, b2g, mine, other):
    @pl.when(pl.program_id(0) == 0)
    def _():
        c = cot[...].astype(F32)
        b2g[...] = jnp.sum(c, axis=0, keepdims=True)
        put_halves(c.T.astype(BF16), mine, other, 0, lax.rem(lax.axis_index("freq"), 2), freq_parts)

    out[...] = mm(cot[...], wdown[...], NT).astype(BF16)


def active_grad_call(cot, wdown, cut, freq_parts, after=(), carry=()):
    rows, width = cot.shape
    ff = wdown.shape[0]
    half = shape((width // 2, rows), BF16)
    return launch(
        functools.partial(active_grad_kernel, freq_parts),
        (ff // cut,),
        (cot, wdown),
        [pl.BlockSpec((rows, width), lambda i: (0, 0)), pl.BlockSpec((cut, width), lambda i: (i, 0))],
        (shape((rows, ff), BF16), shape((1, width), F32), half, half),
        (pl.BlockSpec((rows, cut), lambda i: (0, i)), whole((1, width)), whole(half.shape), whole(half.shape)),
        [],
        cost(2 * rows * width * ff, wdown.size * 2 + rows * ff * 2),
        "active_grad",
        after,
        carry,
    )


def gelu_parts(h):
    square = h * h
    t = jnp.tanh(GELU_C * h * (1.0 + GELU_A * square))
    half = 0.5 + 0.5 * t
    slope = half + (0.5 * GELU_C) * h * (1.0 - t * t) * (1.0 + (3.0 * GELU_A) * square)
    return h * half, slope


def mlp_kernel(paired, freq_parts, tok, convt, second, wo, ob, gain, bias, wup, b1, ag_ref, cot, pack, res, b1g, rgrad, convgt, sgrad, mine_t, other_t, vecs, *rest):
    mine, (n2, gn, conv, acc, wide) = rest[:-5], rest[-5:]
    step = pl.program_id(0)
    cut, part = wup.shape[1], gn.shape[2]
    core = lax.rem(lax.axis_index("freq"), 2)

    @pl.when(step == 0)
    def _():
        c = convt[...].astype(F32).T
        conv[...] = c.astype(BF16)
        g = (second[...].astype(F32) * c).astype(BF16)
        r = tok[...].astype(F32) + (mm(g, wo[...]) + ob[...])
        res[...] = r.astype(BF16)
        wide[...] = r
        n, _ = normalized(r)
        m = (n * gain[...] + bias[...]).astype(BF16)
        n2[...] = m
        both = [g, m]
        for k in range(gn.shape[0]):
            start = k * part
            gn[k] = both[start // g.shape[1]][:, start % g.shape[1] : start % g.shape[1] + part]
        acc[...] = jnp.zeros_like(acc)

    h = mm(n2[...], wup[...]) + b1[...]
    a, slope = gelu_parts(h)
    pack[:, :cut] = a.astype(BF16)
    hg = (ag_ref[...].astype(F32) * slope).astype(BF16)
    acc[...] += mm(hg, wup[...], NT)
    b1g[...] = jnp.sum(hg.astype(F32), axis=0, keepdims=True)
    pack[:, pack.shape[1] - part :] = gn[step]
    if not paired:
        pack[:, cut : 2 * cut] = hg
    else:
        half = cut // 2

        @pl.when(core == 0)
        def _():
            mine[0][...] = hg[:, :half]
            pack[:, cut : cut + half] = hg[:, half:]

        @pl.when(core == 1)
        def _():
            mine[0][...] = hg[:, half:]
            pack[:, cut : cut + half] = hg[:, :half]

    @pl.when(step == pl.num_programs(0) - 1)
    def _():
        ng = acc[...]
        n, rate = normalized(wide[...])
        e = ng * gain[...]
        pulled = e - jnp.mean(e, axis=-1, keepdims=True) - n * jnp.mean(e * n, axis=-1, keepdims=True)
        r = cot[...].astype(F32) + rate * pulled
        br = r.astype(BF16)
        rgrad[...] = br
        brf = br.astype(F32)
        gg = mm(br, wo[...], NT)
        convgt[...] = (gg * second[...].astype(F32)).T.astype(BF16)
        sg = (gg * conv[...].astype(F32)).astype(BF16)
        sgrad[...] = sg
        sgf = sg.astype(F32)
        vecs[0:1] = jnp.sum(ng * n, axis=0, keepdims=True)
        vecs[1:2] = jnp.sum(ng, axis=0, keepdims=True)
        vecs[2:3] = jnp.sum(brf, axis=0, keepdims=True)
        vecs[3:4] = jnp.sum(sgf, axis=0, keepdims=True)
        put_halves(brf.T.astype(BF16), mine_t, other_t, 0, core, freq_parts)
        put_halves(sgf.T.astype(BF16), mine_t, other_t, 1, core, freq_parts)


def mlp_call(tok, convt, second, wo, ob, gain, bias, wup, b1, active_grad, cot, cut, paired, freq_parts, after=(), carry=()):
    rows, width = tok.shape
    ff = wup.shape[1]
    steps = ff // cut
    part = 2 * width // steps
    span = cut + (cut // 2 if paired else cut) + part

    def full(i):
        return (0, 0)

    def along(i):
        return (0, i)

    token = pl.BlockSpec((rows, width), full)
    vec = pl.BlockSpec((1, width), full)
    act = shape((rows, width), BF16)
    mine = [shape((rows, ff // 2), BF16)] if paired else []
    turned, turned_spec = shape((width, rows), BF16), pl.BlockSpec((width, rows), full)
    wide = act
    return launch(
        functools.partial(mlp_kernel, paired, freq_parts),
        (steps,),
        (tok, convt, second, wo, ob, gain, bias, wup, b1, active_grad, cot),
        [
            token,
            turned_spec,
            token,
            pl.BlockSpec((width, width), full),
            vec,
            vec,
            vec,
            pl.BlockSpec((width, cut), along),
            pl.BlockSpec((1, cut), along),
            pl.BlockSpec((rows, cut), along),
            token,
        ],
        (shape((rows, span * steps), BF16), wide, shape((1, ff), F32), wide, turned, act, turned, turned, shape((8, width), F32), *mine),
        (
            pl.BlockSpec((rows, span), along),
            token,
            pl.BlockSpec((1, cut), along),
            token,
            turned_spec,
            token,
            turned_spec,
            turned_spec,
            pl.BlockSpec((8, width), full),
            *[pl.BlockSpec((rows, cut // 2), along) for _ in mine],
        ),
        [pltpu.VMEM((rows, width), BF16), pltpu.VMEM((steps, rows, part), BF16), pltpu.VMEM((rows, width), BF16), pltpu.VMEM((rows, width), F32), pltpu.VMEM((rows, width), F32)],
        cost(2 * rows * width * (2 * ff + width), wup.size * 4 + rows * ff * 4 + rows * width * 14, rows * ff),
        "mix_out_mlp",
        after,
        carry,
    )


def unpacked(pack, hidden, steps, cut):
    rows = pack.shape[0]
    blocks = pack.reshape(rows, steps, -1)
    tail = blocks[:, :, cut + hidden :].reshape(rows, -1)
    return blocks[:, :, :cut].reshape(rows, -1), blocks[:, :, cut : cut + hidden].reshape(rows, -1), tail[:, : tail.shape[1] // 2], tail[:, tail.shape[1] // 2 :]


def put_halves(value, mine, other, half, core, freq_parts):
    per = value.shape[0] // freq_parts
    even = [value[(2 * k) * per : (2 * k + 1) * per] for k in range(freq_parts // 2)]
    odd = [value[(2 * k + 1) * per : (2 * k + 2) * per] for k in range(freq_parts // 2)]

    base = half * per * (freq_parts // 2)

    def put(ref, blocks):
        for k, block in enumerate(blocks):
            ref[base + k * per : base + (k + 1) * per] = block

    @pl.when(core == 0)
    def _():
        put(mine, even)
        put(other, odd)

    @pl.when(core == 1)
    def _():
        put(mine, odd)
        put(other, even)


def block_out_kernel(act, wdown, res, b2, out, acc):
    step = pl.program_id(0)
    part = mm(act[...], wdown[...])

    @pl.when(step == 0)
    def _():
        acc[...] = res[...].astype(F32) + b2[...] + part

    @pl.when(step > 0)
    def _():
        acc[...] += part

    @pl.when(step == pl.num_programs(0) - 1)
    def _():
        out[...] = acc[...].astype(BF16)


def block_out_call(pack, wdown, res, b2, cut, after=(), carry=()):
    rows, width = res.shape
    ff = wdown.shape[0]
    step = pack.shape[1] // ff
    if step * ff != pack.shape[1]:
        pack, step = unpacked(pack, cut, ff // cut, cut)[0], 1

    def full(i):
        return (0, 0)

    token = pl.BlockSpec((rows, width), full)
    return launch(
        block_out_kernel,
        (ff // cut,),
        (pack, wdown, res, b2),
        [pl.BlockSpec((rows, cut), lambda i: (0, step * i)), pl.BlockSpec((cut, width), lambda i: (i, 0)), token, pl.BlockSpec((1, width), full)],
        (shape((rows, width), BF16),),
        (token,),
        [pltpu.VMEM((rows, width), F32)],
        cost(2 * rows * width * ff, wdown.size * 2 + rows * ff * 2 + rows * width * 8),
        "block_out",
        after,
        carry,
    )


def back_kernel(mgt, value, gate, sgrad, weight, tok, gain, rgrad, out, vecs, mg, acc):
    step = pl.program_id(0)

    @pl.when(step == 0)
    def _():
        mg[...] = mgt[...].astype(F32).T.astype(BF16)
        acc[...] = mm(sgrad[...], weight[...], NT)

    @pl.when(step == 1)
    def _():
        pv = (gate[...].astype(F32) * mg[...].astype(F32)).astype(BF16)
        acc[...] += mm(pv, weight[...], NT)
        vecs[2:3] = jnp.sum(pv.astype(F32), axis=0, keepdims=True)

    @pl.when(step == 2)
    def _():
        pg = (value[...].astype(F32) * mg[...].astype(F32)).astype(BF16)
        ng = acc[...] + mm(pg, weight[...], NT)
        vecs[3:4] = jnp.sum(pg.astype(F32), axis=0, keepdims=True)
        n, rate = normalized(tok[...].astype(F32))
        vecs[0:1] = jnp.sum(ng * n, axis=0, keepdims=True)
        vecs[1:2] = jnp.sum(ng, axis=0, keepdims=True)
        e = ng * gain[...]
        pulled = e - jnp.mean(e, axis=-1, keepdims=True) - n * jnp.mean(e * n, axis=-1, keepdims=True)
        out[...] = (rgrad[...].astype(F32) + rate * pulled).astype(BF16)


def back_call(mgt, value, gate, sgrad, weight, tok, gain, rgrad, after=(), carry=()):
    rows, width = tok.shape

    def full(i):
        return (0, 0)

    token = pl.BlockSpec((rows, width), full)
    return launch(
        back_kernel,
        (3,),
        (mgt, value, gate, sgrad, weight, tok, gain, rgrad,),
        [
            pl.BlockSpec((width, rows), full),
            token,
            token,
            token,
            pl.BlockSpec((width, width), lambda i: (0, lax.rem(i + 2, 3))),
            token,
            pl.BlockSpec((1, width), full),
            token,
        ],
        (shape((rows, width), BF16), shape((8, width), F32)),
        (token, pl.BlockSpec((8, width), full)),
        [pltpu.VMEM((rows, width), BF16), pltpu.VMEM((rows, width), F32)],
        cost(2048 * 2 * rows * width * width * 3, 2048 * (weight.size * 2 + rows * width * 16)),
        "project_back",
        after,
        carry,
    )


def owner_part(offs_ref, wt, bias, x, mg, source, batch, tok_rows):
    chans = wt.shape[0] // 2
    vg = mm(wt, x, NT) + bias
    lane = lax.broadcasted_iota(jnp.int32, (1, x.shape[0]), 1)
    limit = jnp.zeros_like(lane)
    for b in range(batch):
        inside = jnp.logical_and(lane >= b * tok_rows, lane < (b + 1) * tok_rows)
        limit = jnp.where(inside, offs_ref[b] + b * tok_rows, limit)
    m = jnp.where(source * tok_rows + lane >= limit, mg.astype(F32), 0.0)
    return jnp.concatenate([vg[chans:] * m, vg[:chans] * m], axis=0).astype(BF16)


def owner_list_kernel(batch, tok_rows, parts, offs_ref, wt, bias, mg, *refs):
    xs, out = refs[:parts], refs[parts]
    me = lax.axis_index("freq")
    total = None
    for r in range(parts):
        x = xs[r][...]
        source = me ^ r
        pg = owner_part(offs_ref, wt[...], bias[...], x, mg[source], source, batch, tok_rows)
        part = mm(pg, x)
        total = part if total is None else total + part
    out[...] = total.astype(BF16)


def owner_grid_kernel(batch, tok_rows, offs_ref, wt, bias, mg, x, out, acc):
    step = pl.program_id(0)

    @pl.when(step == 0)
    def _():
        acc[...] = jnp.zeros_like(acc)

    pg = owner_part(offs_ref, wt[...], bias[...], x[0], mg[0], step, batch, tok_rows)
    acc[...] += mm(pg, x[0])

    @pl.when(step == pl.num_programs(0) - 1)
    def _():
        out[...] = acc[...].astype(BF16)


def owner_call(offsets, wt, bias, mg, xs, batch, tok_rows, after=(), carry=()):
    chans, rows = mg.shape[1:]
    width = wt.shape[1]
    listed = isinstance(xs, list)
    count = mg.shape[0]
    if listed:
        kernel = functools.partial(owner_list_kernel, batch, tok_rows, count)
        grid, x_specs, scratch, mg_spec = (1,), [whole((rows, width))] * count, [], whole(mg.shape)
    else:
        kernel = functools.partial(owner_grid_kernel, batch, tok_rows)
        xs = [xs]
        grid, x_specs = (count,), [pl.BlockSpec((1, rows, width), lambda i: (i, 0, 0))]
        scratch = [pltpu.VMEM((2 * chans, width), F32)]
        mg_spec = pl.BlockSpec((1, chans, rows), lambda i: (i, 0, 0))
    return launch(
        kernel,
        grid,
        (offsets, wt, bias, mg, *xs,),
        [smem(), whole(wt.shape), whole(bias.shape), mg_spec] + x_specs,
        (shape((2 * chans, width), BF16),),
        (whole((2 * chans, width)),),
        scratch,
        cost(8 * count * rows * chans * width, count * rows * width * 2),
        "owner_gradients",
        after,
        carry,
    )


def once(value, after):
    def nothing(after_ref, value_ref, out_ref):
        pass

    return pl.pallas_call(
        nothing,
        out_shape=shape(value.shape, value.dtype),
        in_specs=[anywhere(), anywhere()],
        out_specs=anywhere(),
        input_output_aliases={1: 0},
        name="gate",
    )(after, value)


def bit_order(chips, low_first):
    bits = list(range(chips.bit_length() - 1))
    return bits if low_first else bits[::-1]


def place_of(rel, order):
    place = 0
    for level, bit in enumerate(order):
        digit = lax.shift_right_logical(rel, bit) & 1
        place = place + digit * (1 << (len(order) - 1 - level))
    return place


def store_slot(keep, send, place, index, block):
    half = keep.shape[0]

    @pl.when(place < half)
    def _():
        keep[(place,) + index] = block

    @pl.when(place >= half)
    def _():
        send[(place - half,) + index] = block


def rows_kernel(chips, per, chip_order, dp_order, cot, act, cot_p, act_p, keep, send):
    chip = lax.axis_index("freq") // 2
    quarter = pl.program_id(0) ^ lax.axis_index("dp")
    total = (mm(cot[...], act[...]) + mm(cot_p[...], act_p[...])).astype(BF16)
    for k in range(chips):
        place = place_of(jnp.int32(k) ^ chip, chip_order)
        store_slot(keep, send, place_of(quarter, dp_order), (place,), total[k * per : (k + 1) * per])


def rows_pair(own, partner, width, dp, chips, low_first, after=(), carry=()):
    half, inner = own[0].shape
    per = half // chips
    out = shape((dp // 2, chips, per, width), BF16)
    arrays, specs = [], []
    for cot, pack in (own, partner):
        arrays += [cot, pack]
        specs += [whole(cot.shape), pl.BlockSpec((inner, width), lambda i: (0, 2 * i))]
    return launch(
        functools.partial(rows_kernel, chips, per, bit_order(chips, low_first), bit_order(dp, True)),
        (dp,),
        tuple(arrays),
        specs,
        (out, out),
        (whole(out.shape), whole(out.shape)),
        [],
        cost(4 * dp * half * inner * width, dp * inner * width * 4),
        "fc2_gradient",
        after,
        carry,
    )


def rows_plain(cot, act, cot_p, act_p, dp, chips, low_first):
    total = (mm(cot, act) + mm(cot_p, act_p)).astype(BF16)
    blocks = total.reshape(chips, cot.shape[0] // chips, dp, -1).transpose(2, 0, 1, 3)
    blocks = jnp.concatenate(halves_of(blocks.transpose(1, 0, 2, 3), bit_order(chips, low_first)), axis=0).transpose(1, 0, 2, 3)
    return halves_of(blocks, bit_order(dp, True), lax.axis_index("dp"))


def mixer_kernel(chips, per, order, turned, ga, gb, normed, turned_p, ga_p, gb_p, normed_p, keep, send):
    step = pl.program_id(0)
    chip = lax.axis_index("freq") // 2

    def put(half, total):
        for k in range(chips):
            place = place_of(jnp.int32(k) ^ chip, order)
            store_slot(keep, send, place, (slice(half * per, (half + 1) * per), slice(None)), total[k * per : (k + 1) * per].astype(BF16))

    @pl.when(step == 0)
    def _():
        def out(t, a, b):
            return jnp.concatenate([mm(t[...], a[...]), mm(t[...], b[...])], axis=1)

        put(0, out(turned, ga, gb) + out(turned_p, ga_p, gb_p))

    @pl.when(step == 1)
    def _():
        put(1, mm(turned[...], normed[...]) + mm(turned_p[...], normed_p[...]))


def mixer_pair(own, partner, width, chips, low_first, after=(), carry=()):
    order = bit_order(chips, low_first)
    half = width // 2
    per = half // chips
    out = shape((chips // 2, 2 * per, width), BF16)
    arrays, specs = [], []
    for turned, pack, normed in (own, partner):
        inner = turned.shape[1]
        arrays += [turned, pack, pack, normed]
        specs += [
            pl.BlockSpec((half, inner), lambda i: (i, 0)),
            pl.BlockSpec((inner, half), lambda i: (0, 3)),
            pl.BlockSpec((inner, half), lambda i: (0, 7)),
            whole(normed.shape),
        ]
    return launch(
        functools.partial(mixer_kernel, chips, per, order),
        (2,),
        tuple(arrays),
        specs,
        (out, out),
        (whole(out.shape), whole(out.shape)),
        [],
        cost(8 * half * inner * width, 4 * inner * width * 4),
        "mixer_gradient",
        after,
        carry,
    )


def halves_of(blocks, order, chip=None):
    chips = blocks.shape[0]
    chip = lax.axis_index("freq") // 2 if chip is None else chip
    picks = np.zeros(chips, np.int32)
    for rel in range(chips):
        place = sum(((rel >> bit) & 1) << (len(order) - 1 - level) for level, bit in enumerate(order))
        picks[place] = rel
    moved = jnp.take(blocks, jnp.asarray(picks) ^ chip, axis=0)
    return moved[: chips // 2], moved[chips // 2 :]


def cols_kernel(order, la, lb, rt, lap, lbp, rtp, keep, send, left):
    step = pl.program_id(0)
    chip = lax.axis_index("freq") // 2
    half = la.shape[1]

    @pl.when(step == 0)
    def _():
        for k, ref in enumerate((la, lb, lap, lbp)):
            left[k // 2, (k % 2) * half : (k % 2 + 1) * half] = ref[...].astype(F32).T.astype(BF16)

    total = (mm(left[0], rt[...]) + mm(left[1], rtp[...])).astype(BF16)
    store_slot(keep, send, place_of(step ^ chip, order), (), total)


def cols_pair(mine, pack, pack_p, width, cut, chips, low_first, after=(), carry=()):
    order = bit_order(chips, low_first)
    rows = mine.shape[0]
    per = mine.shape[1] // chips
    last = pack.shape[1] // per - 1
    step = pack.shape[1] // chips // per
    out = shape((chips // 2, width, per), BF16)
    out_spec = pl.BlockSpec((chips // 2, width, per), lambda i: (0, 0, 0))

    def at(place):
        return pl.BlockSpec((rows, per), place)

    first, second = (lambda i: (0, last - step)), (lambda i: (0, last))
    return launch(
        functools.partial(cols_kernel, order),
        (chips,),
        (pack, pack, mine, pack_p, pack_p, pack_p),
        [at(first), at(second), at(lambda i: (0, i)), at(first), at(second), at(lambda i: (0, step * i + 2))],
        (out, out),
        (out_spec, out_spec),
        [pltpu.VMEM((2, width, rows), BF16)],
        cost(4 * width * rows * mine.shape[1], (width * rows + rows * mine.shape[1] * 2) * 4),
        "fc1_gradient",
        after,
        carry,
    )


def cols_plain(lt, rt, ltp, rtp, chips, low_first):
    total = (mm(lt.T, rt) + mm(ltp.T, rtp)).astype(BF16)
    return halves_of(total.reshape(lt.shape[1], chips, -1).transpose(1, 0, 2), bit_order(chips, low_first))


def flip(value, freq_parts, bit):
    return lax.ppermute(value, "freq", [(i, i ^ bit) for i in range(freq_parts)])


def begin(keep, send, axis, bit):
    count = lax.axis_size(axis)
    return keep, lax.ppermute(send, axis, [(i, i ^ bit) for i in range(count)])


def finish(pending):
    return pending[0].astype(F32) + pending[1].astype(F32)


def step_on(pending, axis, bits, level):
    if level == len(bits):
        return finish(pending)[0], None
    half = pending[0].shape[0] // 2
    send = finish([v[half:] for v in pending]).astype(BF16)
    keep = finish([v[:half] for v in pending]).astype(BF16)
    return begin(keep, send, axis, bits[level]), send


def across_first(blocks):
    blocks = blocks.astype(BF16)
    count = blocks.shape[0]
    me = lax.axis_index("dp")
    blocks = blocks.reshape((count // 2, 2) + blocks.shape[1:])
    send = lax.dynamic_index_in_dim(blocks, 1 - me % 2, 1, keepdims=False)
    keep = lax.dynamic_index_in_dim(blocks, me % 2, 1, keepdims=False)
    return begin(keep, send, "dp", 1), send


def across_next(pending):
    total = finish(pending)
    me, count = lax.axis_index("dp"), lax.axis_size("dp")
    step = count // total.shape[0]
    total = total.astype(BF16)
    total = total.reshape((total.shape[0] // 2, 2) + total.shape[1:])
    mine = me // step % 2
    send = lax.dynamic_index_in_dim(total, 1 - mine, 1, keepdims=False)
    keep = lax.dynamic_index_in_dim(total, mine, 1, keepdims=False)
    return begin(keep, send, "dp", step), send


def across_rest(pending):
    while pending[0].shape[0] > 1:
        pending, _ = across_next(pending)
    return finish(pending)[0]


def pack_kernel(chans, one, two, b2, b1, skip, out):
    dp, freq = out.shape[:2]
    me = lax.axis_index("freq")
    column = jnp.broadcast_to(skip[...], (chans, 128)).T[0:1, :]
    per = b1.shape[1] // (freq * chans)

    def put(f, start, value):
        for d in range(dp):
            out[d, f, start : start + value.shape[0]] = value

    for f in range(freq):
        cut = slice(f * chans, (f + 1) * chans)
        put(f, 0, one[0:2, cut])
        for r in range(3):
            group, chunk = divmod(3 * f + r, freq)
            source = (one[2:3], one[3:4], two[3:4])[group]
            put(f, 2 + r, source[:, chunk * chans : (chunk + 1) * chans])
        put(f, 5, two[0:3, cut])
        put(f, 8, b2[:, cut])
        for r in range(per):
            start = (f * per + r) * chans
            put(f, 9 + r, b1[:, start : start + chans])
        put(f, 9 + per, jnp.where(me == f, column, 0.0))
    for d in range(dp):
        for f in range(freq):
            out[d, f, 10 + per :] = jnp.zeros((out.shape[2] - 10 - per, chans), F32)


def packed_vectors(one, two, b2, b1, skip, dp, freq, after=(), carry=()):
    chans = one.shape[1] // freq
    lines = 16
    if freq == 8:
        return launch(
            functools.partial(pack_kernel, chans),
            (1,),
            (one, two, b2, b1, skip),
            [whole(v.shape) for v in (one, two, b2, b1, skip)],
            (shape((dp, freq, lines, chans), F32),),
            (whole((dp, freq, lines, chans)),),
            [],
            cost(1, 1),
            "pack_vectors",
            after,
            carry,
        )
    own = (jnp.arange(freq, dtype=jnp.int32) == lax.axis_index("freq")).astype(F32)[:, None, None] * skip.reshape(1, 1, chans)
    rows = jnp.concatenate([one[:2], two[:3], b2]).reshape(6, freq, chans).transpose(1, 0, 2)
    bias_in = jnp.concatenate([one[2:4], two[3:4]]).reshape(freq, 3, chans)
    rows = jnp.concatenate([rows[:, :2], bias_in, rows[:, 2:], b1.reshape(freq, -1, chans), own], axis=1)
    return jnp.broadcast_to(rows[None], (dp,) + rows.shape), carry


def to_all(block):
    dp, freq = lax.axis_size("dp"), lax.axis_size("freq")
    wide = block if block.ndim == 4 else jnp.broadcast_to(block[None], (dp,) + block.shape)
    wide = wide.reshape((dp * freq,) + wide.shape[2:])
    return lax.all_to_all(wide, ("dp", "freq"), split_axis=0, concat_axis=0, tiled=True)


def reblocked(blocks, count, width):
    if blocks.shape[0] == count and blocks.shape[2] == width:
        return blocks
    whole = blocks.transpose(1, 0, 2).reshape(blocks.shape[1], -1)
    need = count * width
    whole = jnp.pad(whole, ((0, 0), (0, max(0, need - whole.shape[1]))))[:, :need]
    return whole.reshape(-1, count, width).transpose(1, 0, 2)


def body(tokens, offsets, kernel_lengths, norm1_gain, norm1_bias, w_in, in_bias, kernel_taps, skip_gain, w_out, out_bias, norm2_gain, norm2_bias, w_up, fc1_bias, w_down, fc2_bias, cotangent):
    freq = lax.axis_size("freq")
    dp = lax.axis_size("dp")
    chips = freq // 2
    batch, tok_rows, width = tokens.shape
    rows = batch * tok_rows
    ff = w_up.shape[1]
    chans = width // freq
    me = lax.axis_index("freq")
    core = lax.rem(me, 2)

    def row(v):
        return v.reshape(1, -1)

    tok = tokens.reshape(rows, width)
    cot = cotangent.reshape(rows, width)
    tap_rows = kernel_taps.shape[1]
    reach = -(-freq * tap_rows // tok_rows)
    lens = lax.dynamic_slice_in_dim(kernel_lengths, me * chans, chans).reshape(chans, 1)
    skip = skip_gain.reshape(chans, 1)

    def swap(v):
        return flip(v, freq, 1)

    cut = 768
    normed, mixed_t, value, gate, gate_two = front_call(
        tok, offsets, norm1_gain, norm1_bias, w_in, in_bias, kernel_taps, batch, tok_rows
    )
    mixed = lax.all_to_all(mixed_t.reshape(freq, chans, -1), "freq", split_axis=0, concat_axis=0, tiled=True)
    taps = mixed if tap_rows == tok_rows else reblocked(mixed[:, :, rows:], reach, tok_rows)
    active_grad, b2g, cot_mine, cot_other = active_grad_call(cot, w_down, cut, freq, after=(mixed_t,))
    own_w = jnp.concatenate([lax.dynamic_slice_in_dim(w_in, k * width + me * chans, chans, axis=1) for k in range(2)], axis=1).T
    own_b = jnp.concatenate([lax.dynamic_slice_in_dim(in_bias, k * width + me * chans, chans) for k in range(2)]).reshape(-1, 1)
    (conv, k_spec), (cot_p, normed_p, normed) = forward_call(mixed, batch, tok_rows, taps, lens, skip, after=(active_grad, own_w, own_b), carry=(swap(cot_other), swap(normed), normed))
    conv_t = lax.all_to_all(conv, "freq", split_axis=0, concat_axis=0, tiled=True).reshape(width, rows)
    near = []
    if freq == 8:
        near = [flip(normed, freq, 2), flip(normed, freq, 4), flip(normed, freq, 6)]
    paired = freq == 8 and ff == 4 * cut
    pack, res, b1g, rgrad, convg_t, sgrad, turned, turned_other, vec_two, *mine = mlp_call(
        tok, conv_t, gate_two, w_out, row(out_bias), row(norm2_gain), row(norm2_bias), w_up, row(fc1_bias), active_grad, cot, cut, paired, freq
    )
    mine = mine[0] if paired else None
    block_out = block_out_call(pack, w_down, res, row(fc2_bias), cut)
    convg = lax.all_to_all(convg_t.reshape(freq, chans, rows), "freq", split_axis=0, concat_axis=0, tiled=True)
    half = width // 2
    if paired:
        pack_p, turned_p = swap(pack), swap(turned_other)
        fc2, near = rows_pair((cot_mine, pack), (cot_p, pack_p), width, dp, chips, True, after=(block_out,), carry=near)
        fc1 = cols_pair(mine, pack, pack_p, width, cut, chips, False, after=(fc2[1],))
        far = [swap(v) for v in near]
        mixed_grad = adjoint_call(convg, batch, k_spec, skip, after=(fc1[1],))
        mixer = mixer_pair((turned, pack, normed), (turned_p, pack_p, normed_p), width, chips, True, after=(mixed_grad,))
        normed_all = [v for pair_of in zip([normed, *near], [normed_p, *far]) for v in pair_of]
    else:
        normed_all = lax.all_gather(normed, "freq", axis=0, tiled=False)
        act, hg, gated, n2 = unpacked(pack, cut, ff // cut, cut)
        hg = hg.reshape(rows, chips, 2, ff // freq)
        hg_mine = jnp.take(hg, core, axis=2).reshape(rows, ff // 2)
        hg_other = jnp.take(hg, 1 - core, axis=2).reshape(rows, ff // 2)
        act_p, gated_p, n2_p, turned_p = swap(act), swap(gated), swap(n2), swap(turned_other)
        fc2 = rows_plain(cot_mine, act, cot_p, act_p, dp, chips, True)
        fc1 = cols_plain(n2, hg_mine, n2_p, swap(hg_other), chips, False)
        mixer = []
        for lt, rt, ltp, rtp in ((turned[:half], gated, turned_p[:half], gated_p), (turned[half:], normed, turned_p[half:], normed_p)):
            mixer.append((mm(lt, rt) + mm(ltp, rtp)).astype(BF16).reshape(chips, -1, width))
        mixer = halves_of(jnp.concatenate(mixer, axis=1), bit_order(chips, True))
        mixed_grad = adjoint_call(convg, batch, k_spec, skip)
    mixed_grad_t = lax.all_to_all(mixed_grad, "freq", split_axis=0, concat_axis=0, tiled=True).reshape(width, rows)
    low, high = ([2 << bit for bit in bit_order(chips, first)] for first in (True, False))
    deep = [1 << bit for bit in bit_order(dp, True)]
    fc2_sum, fc1_sum, mixer_sum = begin(*fc2, "dp", deep[0]), begin(*fc1, "freq", high[0]), begin(*mixer, "freq", low[0])
    owned, (keep, keep_m) = owner_call(
        offsets, own_w, own_b, mixed_grad, normed_all, batch, tok_rows, after=(mixer[1],), carry=(fc2_sum[0], mixer_sum[0])
    )
    fc2_sum, sent = step_on((keep, fc2_sum[1]), "dp", deep, 1)
    mixer_sum, sent_m = step_on((once(keep_m, sent), mixer_sum[1]), "freq", low, 1)
    (taps_g, skip_g), (keep, keep_1, keep_m) = taps_grad_call(
        mixed, convg, lens, tok_rows, reach, dp if tap_rows == tok_rows else 0, after=(owned, sent_m), carry=(fc2_sum[0], fc1_sum[0], mixer_sum[0])
    )
    fc2_sum = (keep, fc2_sum[1])
    if tap_rows != tok_rows:
        taps_g = reblocked(taps_g, freq, tap_rows).reshape(freq, dp, chans // dp, tap_rows).transpose(1, 0, 2, 3)
    taps_g = taps_g.reshape(dp, width // dp, tap_rows)
    taps_sum, sent_t = across_first(taps_g)
    fc1_sum, sent_1 = step_on((once(keep_1, sent_t), fc1_sum[1]), "freq", high, 1)
    mixer_sum = (once(keep_m, sent_1), mixer_sum[1])
    for level in range(2, len(low) + 1):
        mixer_sum, _ = step_on(mixer_sum, "freq", low, level)
    mixer = mixer_sum.astype(BF16)
    parts = jnp.concatenate([owned, mixer[chans:]]).reshape(3, chans, width)
    pieces, moved = [], []
    for r in range(3):
        part = lax.rem((freq % 3) * (r - me + 3 * freq), 3)
        moved.append(lax.dynamic_index_in_dim(parts, part, 0, keepdims=False))
        pieces.append(lax.ppermute(moved[-1], "freq", [((3 * d + r) % freq, d) for d in range(freq)]))
    fc2_sum = (once(keep, moved[0]), fc2_sum[1])
    for level in range(2, len(deep)):
        fc2_sum, _ = step_on(fc2_sum, "dp", deep, level)
    half = chips // 2
    sent = finish([v[0, half:] for v in fc2_sum]).astype(BF16)
    fc2_sum = begin(finish([v[0, :half] for v in fc2_sum]).astype(BF16), sent, "freq", low[0])
    (input_grad, vec_one), (keep, keep_1, keep_t) = back_call(
        mixed_grad_t, value, gate, sgrad, w_in, tok, row(norm1_gain), rgrad,
        after=(*moved, sent), carry=(fc2_sum[0], fc1_sum[0], taps_sum[0]),
    )
    fa = ff // freq
    fc1_sum = (keep_1, fc1_sum[1])
    for level in range(2, len(high) + 1):
        fc1_sum, _ = step_on(fc1_sum, "freq", high, level)
    first, sent_1 = across_first(fc1_sum.reshape(dp, width // dp, fa))
    vectors, (keep, keep_t) = packed_vectors(vec_one, vec_two, b2g, b1g, skip_g, dp, freq, after=(sent_1,), carry=(keep, keep_t))
    final = to_all(vectors)
    taps_sum, sent_t = across_next((keep_t, taps_sum[1]))
    second = jnp.concatenate(pieces + [once(mixer[:chans], sent_t)], axis=0).T.reshape(dp, width // dp, 4 * chans)
    second, sent = across_first(second)
    first = (once(once(first[0], sent), final), first[1])
    first, sent = across_next(first)
    fc2_sum = (once(keep, sent), fc2_sum[1])
    fc2_sum, sent = step_on(fc2_sum, "freq", low, 1)
    second, sent = across_next((once(second[0], sent), second[1]))
    quarter_sum = across_rest((once(taps_sum[0], sent), taps_sum[1])).astype(BF16).reshape(freq, chans // dp, tap_rows)
    spread = to_all(quarter_sum)
    for level in range(2, len(low) + 1):
        fc2_sum, _ = step_on(fc2_sum, "freq", low, level)
    first, second = across_rest(first), across_rest(second)
    fc1_final, in_final, out_final = first, second[:, : 3 * chans], second[:, 3 * chans :]
    fc2_final = fc2_sum.T
    spread = spread.reshape(dp, freq, chans // dp, tap_rows).transpose(1, 0, 2, 3).reshape(width, tap_rows)
    taps_final = spread.astype(F32) * jnp.square(jnp.tanh(kernel_taps / SHRINK))
    final = jnp.sum(final, axis=0)
    n1g, n1b = final[0], final[1]
    inb = final[2:5].reshape(-1)
    n2g, n2b, outb, b2f = (final[k] for k in range(5, 9))
    lines = ff // width
    b1f, skg = final[9 : 9 + lines].reshape(-1), final[9 + lines]
    return (
        block_out.reshape(tokens.shape),
        input_grad.reshape(tokens.shape),
        n1g,
        n1b,
        in_final,
        inb,
        taps_final,
        skg,
        out_final,
        outb,
        n2g,
        n2b,
        fc1_final,
        b1f,
        fc2_final,
        b2f,
    )


def solution(mesh):
    token, whole, lead = P("dp", "freq", None), P(), P("freq")
    both = P("dp", "freq")
    in_specs = (token, P("dp"), whole, whole, whole, whole, whole, P(None, "freq"), lead) + (whole,) * 8 + (token,)
    out_specs = (token, token, lead, lead, both, lead, P(None, "freq"), lead, both, lead, lead, lead, both, lead, both, lead)
    return jax.shard_map(body, mesh=mesh, in_specs=in_specs, out_specs=out_specs, check_vma=False)
```

```python
import functools

import jax
import jax.numpy as jnp
import numpy as np
from jax import lax
from jax.experimental import pallas as pl
from jax.experimental.pallas import tpu as pltpu
from jax.sharding import PartitionSpec as P

NORM_EPS = 1e-05
SHRINK = 0.003
GELU_C = 0.7978845608028654
GELU_A = 0.044715
F32 = jnp.float32
BF16 = jnp.bfloat16
MIB = 1 << 20

NN = (((1,), (0,)), ((), ()))
NT = (((1,), (1,)), ((), ()))


def mm(left, right, dims=NN):
    return lax.dot_general(left, right, dims, preferred_element_type=F32)


def whole(dims):
    return pl.BlockSpec(tuple(dims), lambda i: (0,) * len(dims))


def anywhere():
    return pl.BlockSpec(memory_space=pl.ANY)


def smem():
    return pl.BlockSpec(memory_space=pltpu.SMEM)


def shape(dims, dtype):
    return jax.ShapeDtypeStruct(dims, dtype)


def launch(kernel, grid, ins, in_specs, outs, out_specs, scratch, estimate, name, after=(), carry=()):
    count, extra, given = len(ins), len(after) + len(carry), len(outs)

    def run(*refs):
        made = refs[count + extra : count + extra + given]
        kernel(*refs[:count], *made, *refs[count + extra + given + len(carry) :])

    first = count + len(after)
    results = pl.pallas_call(
        run,
        grid=grid,
        out_shape=tuple(outs) + tuple(shape(v.shape, v.dtype) for v in carry),
        in_specs=list(in_specs) + [anywhere()] * extra,
        out_specs=tuple(out_specs) + (anywhere(),) * len(carry),
        scratch_shapes=scratch,
        input_output_aliases={first + k: given + k for k in range(len(carry))},
        compiler_params=pltpu.CompilerParams(vmem_limit_bytes=60 * MIB, dimension_semantics=("arbitrary",)),
        cost_estimate=estimate,
        name=name,
    )(*ins, *after, *carry)
    made = results[0] if given == 1 else results[:given]
    return (made, results[given:]) if carry else made


def cost(flops, moved, special=0):
    return pl.CostEstimate(flops=int(flops) * 64, bytes_accessed=int(moved) * 64, transcendentals=0)


def split16(table):
    high = np.asarray(table, np.float32).astype(jnp.bfloat16)
    low = (np.asarray(table, np.float64) - high.astype(np.float64)).astype(np.float32).astype(jnp.bfloat16)
    return high, low


@functools.lru_cache(maxsize=None)
def tables(width):
    order = np.concatenate([np.arange(0, width, 2), np.arange(1, width, 2)])
    turns = (2 * order[None, :] + 1) * np.arange(width)[:, None] % (4 * width)
    angle = np.pi * turns / (2 * width)
    forward = np.concatenate([np.cos(angle), -np.sin(angle)], axis=1)
    inverse = forward.T / width
    return split16(forward) + split16(inverse)


def split_value(value):
    high = value.astype(BF16)
    return high, (value - high.astype(F32)).astype(BF16)


def spectrum_of(block, fhi):
    return mm(block, fhi)


def signal_of(spec, ghi):
    return mm(spec.astype(BF16), ghi)


def each(count, step, unroll):
    if unroll:
        for i in range(count):
            step(i)
    else:
        lax.fori_loop(0, count, lambda i, c: (step(i), c)[1], 0)


def blocks_to_spectra(x_ref, spec_ref, fhi, batch, width):
    count, chans = x_ref.shape[0], x_ref.shape[1]
    for b in range(batch):
        lanes = slice(b * width, (b + 1) * width)
        if chans % 16 == 0:
            rows = x_ref[:, :, lanes].reshape(count * chans, width)
            spec_ref[b] = spectrum_of(rows, fhi[...]).reshape(count, chans, 2 * width)
        else:

            def step(j, b=b, lanes=lanes):
                spec_ref[b, j] = spectrum_of(x_ref[j, :, lanes], fhi[...])

            each(count, step, False)


def tiles(chans, width, step):
    lane_tiles = width // 128

    def rows_step(rt):
        start = rt * 8 if isinstance(rt, int) else pl.multiple_of(rt * 8, 8)
        for lane in range(lane_tiles):
            step(pl.ds(start, 8), lane)

    each(chans // 8, rows_step, False)


def pair(ref, lead, rows, lane, width):
    return (
        ref[lead + (rows, slice(lane * 128, (lane + 1) * 128))],
        ref[lead + (rows, slice(width + lane * 128, width + (lane + 1) * 128))],
    )


def put_pair(ref, lead, rows, lane, width, value):
    ref[lead + (rows, slice(lane * 128, (lane + 1) * 128))] = value[0]
    ref[lead + (rows, slice(width + lane * 128, width + (lane + 1) * 128))] = value[1]


def times(a, k):
    return a[0] * k[0] - a[1] * k[1], a[0] * k[1] + a[1] * k[0]


def times_conj(a, k):
    return a[0] * k[0] + a[1] * k[1], a[1] * k[0] - a[0] * k[1]


def plus(a, b):
    return b if a is None else (a[0] + b[0], a[1] + b[1])


def quarter(now, before, sign):
    if before is None:
        return now
    if sign > 0:
        return now[0] - before[1], now[1] + before[0]
    return now[0] + before[1], now[1] - before[0]


def wide_quarter(now, before, width):
    lane = lax.broadcasted_iota(jnp.int32, (1, width), 1)
    sign = jnp.where(lane < width // 2, 1.0, -1.0)
    return jnp.concatenate(
        [now[:, :width] - sign * before[:, width:], now[:, width:] + sign * before[:, :width]], axis=1
    )


def wide_times(a, k, width, conj):
    ar, ai, kr, ki = a[:, :width], a[:, width:], k[:, :width], k[:, width:]
    if conj:
        return jnp.concatenate([ar * kr + ai * ki, ai * kr - ar * ki], axis=1)
    return jnp.concatenate([ar * kr - ai * ki, ar * ki + ai * kr], axis=1)


UNROLLED = 8


def small(count, chans, width):
    return count <= UNROLLED and chans % 16 == 0 and width % 256 == 0


def conv_products(spec_ref, k_ref, z_ref, batch, width, adjoint):
    reach, chans = k_ref.shape[0], k_ref.shape[1]
    count = spec_ref.shape[1]
    if small(count, chans, width):

        def step(rows, lane):
            k = [pair(k_ref, (d,), rows, lane, width) for d in range(reach)]
            for b in range(batch):
                x = [pair(spec_ref, (b, j), rows, lane, width) for j in range(count)]
                for i in range(count):
                    total = None
                    if adjoint:
                        for d in range(min(count - i, reach)):
                            total = plus(total, times_conj(x[i + d], k[d]))
                    else:
                        for d in range(min(i + 1, reach)):
                            total = plus(total, times(x[i - d], k[d]))
                    put_pair(z_ref, (b, i), rows, lane, width, total)

        tiles(chans, width, step)
        return
    for b in range(batch):

        def row(i, b=b):
            def term(d, total):
                src = i + d if adjoint else i - d
                return total + wide_times(spec_ref[b, src], k_ref[d], width, adjoint)

            terms = jnp.minimum(count - i if adjoint else i + 1, reach)
            z_ref[b, i] = lax.fori_loop(0, terms, term, jnp.zeros((chans, 2 * width), F32))

        each(count, row, False)


def conv_body(adjoint, batch, x_ref, k_ref, skip_ref, fhi, ghi, out_ref, spec_ref, z_ref):
    count, chans = x_ref.shape[:2]
    width = fhi.shape[0]
    blocks_to_spectra(x_ref, spec_ref, fhi, batch, width)
    conv_products(spec_ref, k_ref, z_ref, batch, width, adjoint)
    for b in range(batch):
        cut = slice(b * width, (b + 1) * width)
        if chans % 16 == 0:
            y = signal_of(z_ref[b].reshape(count * chans, 2 * width), ghi[...])
            y = y.reshape(count, chans, width) + skip_ref[...][None] * x_ref[:, :, cut].astype(F32)
            out_ref[:, :, cut] = y.astype(BF16)
        else:

            def step(j, b=b, cut=cut):
                y = signal_of(z_ref[b, j], ghi[...])
                out_ref[j, :, cut] = (y + skip_ref[...] * x_ref[j, :, cut].astype(F32)).astype(BF16)

            each(count, step, False)


def forward_kernel(batch, x_ref, s_ref, len_ref, skip_ref, fhi, flo, ghi, out_ref, k_ref, spec_ref, z_ref, raw_ref):
    taps_spectra(s_ref, s_ref.shape[2] - fhi.shape[0], len_ref, fhi, flo, k_ref, raw_ref)
    conv_body(False, batch, x_ref, k_ref, skip_ref, fhi, ghi, out_ref, spec_ref, z_ref)


def forward_call(x, batch, width, taps, lens, skip, after=(), carry=()):
    count, chans = x.shape[:2]
    reach = taps.shape[0]
    tabs = tables(width)
    spec = pltpu.VMEM((batch, count, chans, 2 * width), F32)
    span = min(reach + 1, count)
    same = taps is x
    args = (x,) if same else (x, taps)

    def kernel(*refs):
        forward_kernel(batch, refs[0], *(refs if same else refs[1:]))

    return launch(
        kernel,
        (1,),
        (*args, lens, skip, *tabs[:3]),
        [whole(v.shape) for v in (*args, lens, skip, *tabs[:3])],
        (shape((count, chans, batch * width), BF16), shape((span, chans, 2 * width), F32)),
        (whole((count, chans, batch * width)), whole((span, chans, 2 * width))),
        [spec, spec, pltpu.VMEM((reach, chans, 2 * width), F32)],
        cost(x.size * width * 20, x.size * 8 + 4 * width * width * 4),
        "conv_forward",
        after,
        carry,
    )


def adjoint_kernel(batch, *refs):
    conv_body(True, batch, *refs)


def adjoint_call(x, batch, k_spec, skip, after=(), carry=()):
    count, chans, lanes = x.shape
    width = k_spec.shape[2] // 2
    tabs = tables(width)
    spec = pltpu.VMEM((batch, count, chans, 2 * width), F32)
    return launch(
        functools.partial(adjoint_kernel, batch),
        (1,),
        (x, k_spec, skip, tabs[0], tabs[2]),
        [whole(v.shape) for v in (x, k_spec, skip, tabs[0], tabs[2])],
        (shape(x.shape, BF16),),
        (whole(x.shape),),
        [spec, spec],
        cost(x.size * width * 20, x.size * 4 + k_spec.size * 4 + 4 * width * width * 4),
        "conv_adjoint",
        after,
        carry,
    )


def pooled_rows(full):
    span = full.shape[1]
    place = lax.broadcasted_iota(jnp.int32, (1, span), 1)
    before = jnp.where(place == 0, 0.0, pltpu.roll(full, 1, 1))
    after = jnp.where(place == span - 1, 0.0, pltpu.roll(full, span - 1, 1))
    return (before + full + after) / 3.0


def taps_spectra(s_ref, start, len_ref, fhi, flo, out_ref, raw_ref):
    count, chans = s_ref.shape[:2]
    width = fhi.shape[0]
    full = jnp.concatenate([s_ref[d, :, start : start + width].astype(F32) for d in range(count)], axis=1)
    place = lax.broadcasted_iota(jnp.int32, (1, count * width), 1)
    kernel = jnp.where(place < len_ref[...], pooled_rows(full), 0.0)
    for d in range(count):
        high, low = split_value(kernel[:, d * width : (d + 1) * width])
        raw_ref[d] = mm(high, fhi[...]) + (mm(low, fhi[...]) + mm(high, flo[...]))
    out_ref[0] = raw_ref[0]
    for d in range(1, count):
        out_ref[d] = wide_quarter(raw_ref[d], raw_ref[d - 1], width)
    if out_ref.shape[0] > count:
        out_ref[count] = wide_quarter(jnp.zeros((chans, 2 * width), F32), raw_ref[count - 1], width)


def taps_grad_kernel(x_ref, g_ref, len_ref, fhi, ghi, out_ref, skip_ref, xs_ref, gs_ref, z_ref):
    count, chans, lanes = g_ref.shape
    reach = z_ref.shape[0]
    width = fhi.shape[0]
    batch = lanes // width
    blocks_to_spectra(x_ref, xs_ref, fhi, batch, width)
    blocks_to_spectra(g_ref, gs_ref, fhi, batch, width)
    if small(count, chans, width):

        def step(rows, lane):
            sign = 1 if lane < width // 256 else -1
            total = [None] * reach
            for b in range(batch):
                x = [pair(xs_ref, (b, j), rows, lane, width) for j in range(count)]
                x = [quarter(x[j], x[j - 1] if j else None, sign) for j in range(count)]
                for i in range(count):
                    g = pair(gs_ref, (b, i), rows, lane, width)
                    for d in range(min(i + 1, reach)):
                        total[d] = plus(total[d], times_conj(g, x[i - d]))
            for d in range(reach):
                put_pair(z_ref, (d,), rows, lane, width, total[d])

        tiles(chans, width, step)
        rows = signal_of(z_ref[...].reshape(reach * chans, 2 * width), ghi[...])
        rows = rows.reshape(reach, chans, width)
        pieces = [rows[d] for d in range(reach)]
    else:

        def shift(t, c):
            j = count - 1 - t
            for b in range(batch):
                xs_ref[b, j] = wide_quarter(xs_ref[b, j], xs_ref[b, j - 1], width)
            return c

        lax.fori_loop(0, count - 1, shift, 0)

        def lag(d):
            total = jnp.zeros((chans, 2 * width), F32)
            for b in range(batch):

                def term(i, acc, b=b):
                    return acc + wide_times(gs_ref[b, i], xs_ref[b, i - d], width, True)

                total = lax.fori_loop(d, count, term, total)
            z_ref[d] = total

        each(reach, lag, False)
        pieces = [signal_of(z_ref[d], ghi[...]) for d in range(reach)]
    full = jnp.concatenate(pieces, axis=1)
    place = lax.broadcasted_iota(jnp.int32, (1, reach * width), 1)
    full = pooled_rows(jnp.where(place < len_ref[...], full, 0.0))
    if len(out_ref.shape) == 4:
        per = out_ref.shape[2]
        for q in range(out_ref.shape[0]):
            for d in range(reach):
                out_ref[q, d] = full[q * per : (q + 1) * per, d * width : (d + 1) * width].astype(BF16)
    else:
        for d in range(reach):
            out_ref[d] = full[:, d * width : (d + 1) * width].astype(BF16)
    dot = jnp.zeros((chans, lanes), F32)
    for j in range(count):
        dot = dot + x_ref[j, :, :lanes].astype(F32) * g_ref[j].astype(F32)
    skip_ref[...] = jnp.sum(dot, axis=1, keepdims=True)


def taps_grad_call(x, g, lens, width, reach, split, after=(), carry=()):
    count, chans, lanes = g.shape
    batch = lanes // width
    tabs = tables(width)
    spec = pltpu.VMEM((batch, count, chans, 2 * width), F32)
    made = (split, reach, chans // split, width) if split else (reach, chans, width)
    return launch(
        taps_grad_kernel,
        (1,),
        (x, g, lens, tabs[0], tabs[2]),
        [whole(v.shape) for v in (x, g, lens, tabs[0], tabs[2])],
        (shape(made, BF16), shape((chans, 1), F32)),
        (whole(made), whole((chans, 1))),
        [spec, spec, pltpu.VMEM((reach, chans, 2 * width), F32)],
        cost(x.size * width * 20, x.size * 6),
        "taps_gradient",
        after,
        carry,
    )


def normalized(values):
    centred = values - jnp.mean(values, axis=-1, keepdims=True)
    rate = lax.rsqrt(jnp.mean(centred * centred, axis=-1, keepdims=True) + NORM_EPS)
    return centred * rate, rate


def live_rows(offs_ref, batch, tok_rows, rows):
    row = lax.broadcasted_iota(jnp.int32, (rows, 1), 0)
    limit = jnp.zeros((rows, 1), jnp.int32)
    base = lax.axis_index("freq") * tok_rows
    position = base + row
    for b in range(batch):
        inside = jnp.logical_and(row >= b * tok_rows, row < (b + 1) * tok_rows)
        limit = jnp.where(inside, offs_ref[b] + b * tok_rows, limit)
    return position >= limit


def front_kernel(batch, tok_rows, offs_ref, tok, gain, bias, wv, wg, ws, in_bias, taps, normed, mixed, value, gate, second, spread):
    rows = tok.shape[0]
    cut = wv.shape[1]
    per = in_bias.shape[0] // (3 * cut)

    @pl.when(pl.program_id(0) == 0)
    def _():
        n, _ = normalized(tok[...].astype(F32))
        row = in_bias[...].reshape(1, -1)
        for k in range(3 * per):
            spread[k] = row[:, k * cut : (k + 1) * cut]
        normed[...] = (n * gain[...].reshape(1, -1) + bias[...].reshape(1, -1)).astype(BF16)

    x = normed[...]
    step = pl.program_id(0)
    v = mm(x, wv[...]) + spread[step]
    g = mm(x, wg[...]) + spread[per + step]
    live = live_rows(offs_ref, batch, tok_rows, rows)
    mixed[:, :rows] = jnp.where(live, g * v, 0.0).T.astype(BF16)
    t = taps[...]
    mixed[:, rows:] = (t - SHRINK * jnp.tanh(t / SHRINK)).astype(BF16)
    value[...] = jnp.where(live, v, 0.0).astype(BF16)
    gate[...] = jnp.where(live, g, 0.0).astype(BF16)
    second[...] = (mm(x, ws[...]) + spread[2 * per + step]).astype(BF16)


def front_call(tok, offsets, gain, bias, weight, in_bias, taps, batch, tok_rows):
    rows, width = tok.shape
    span = rows + taps.shape[1]
    cut = 384
    per = width // cut

    def full(i):
        return (0, 0)

    def col(part):
        return lambda i: (0, part * per + i)

    act = shape((rows, width), BF16)
    return launch(
        functools.partial(front_kernel, batch, tok_rows),
        (per,),
        (offsets, tok, gain, bias, weight, weight, weight, in_bias, taps),
        [smem(), pl.BlockSpec((rows, width), full), whole((width,)), whole((width,))]
        + [pl.BlockSpec((width, cut), col(k)) for k in range(3)]
        + [whole(in_bias.shape)]
        + [pl.BlockSpec((cut, taps.shape[1]), lambda i: (i, 0))],
        (act, shape((width, span), BF16), act, act, act),
        (
            pl.BlockSpec((rows, width), full),
            pl.BlockSpec((cut, span), lambda i: (i, 0)),
            pl.BlockSpec((rows, cut), lambda i: (0, i)),
            pl.BlockSpec((rows, cut), lambda i: (0, i)),
            pl.BlockSpec((rows, cut), lambda i: (0, i)),
        ),
        [pltpu.VMEM((3 * per, 1, cut), F32)],
        cost(2 * rows * width * 3 * width, weight.size * 2 + rows * width * 12),
        "norm_project",
            )


def active_grad_kernel(freq_parts, cot, wdown, out, b2g, mine, other):
    @pl.when(pl.program_id(0) == 0)
    def _():
        c = cot[...].astype(F32)
        b2g[...] = jnp.sum(c, axis=0, keepdims=True)
        put_halves(c.T.astype(BF16), mine, other, 0, lax.rem(lax.axis_index("freq"), 2), freq_parts)

    out[...] = mm(cot[...], wdown[...], NT).astype(BF16)


def active_grad_call(cot, wdown, cut, freq_parts, after=(), carry=()):
    rows, width = cot.shape
    ff = wdown.shape[0]
    half = shape((width // 2, rows), BF16)
    return launch(
        functools.partial(active_grad_kernel, freq_parts),
        (ff // cut,),
        (cot, wdown),
        [pl.BlockSpec((rows, width), lambda i: (0, 0)), pl.BlockSpec((cut, width), lambda i: (i, 0))],
        (shape((rows, ff), BF16), shape((1, width), F32), half, half),
        (pl.BlockSpec((rows, cut), lambda i: (0, i)), whole((1, width)), whole(half.shape), whole(half.shape)),
        [],
        cost(2 * rows * width * ff, wdown.size * 2 + rows * ff * 2),
        "active_grad",
        after,
        carry,
    )


def gelu_parts(h):
    square = h * h
    t = jnp.tanh(GELU_C * h * (1.0 + GELU_A * square))
    half = 0.5 + 0.5 * t
    slope = half + (0.5 * GELU_C) * h * (1.0 - t * t) * (1.0 + (3.0 * GELU_A) * square)
    return h * half, slope


def mlp_kernel(paired, freq_parts, tok, convt, second, wo, ob, gain, bias, wup, b1, ag_ref, cot, pack, res, b1g, rgrad, convgt, sgrad, mine_t, other_t, vecs, *rest):
    mine, (n2, gn, conv, acc, wide) = rest[:-5], rest[-5:]
    step = pl.program_id(0)
    cut, part = wup.shape[1], gn.shape[2]
    core = lax.rem(lax.axis_index("freq"), 2)

    @pl.when(step == 0)
    def _():
        c = convt[...].astype(F32).T
        conv[...] = c.astype(BF16)
        g = (second[...].astype(F32) * c).astype(BF16)
        r = tok[...].astype(F32) + (mm(g, wo[...]) + ob[...])
        res[...] = r.astype(BF16)
        wide[...] = r
        n, _ = normalized(r)
        m = (n * gain[...] + bias[...]).astype(BF16)
        n2[...] = m
        both = [g, m]
        for k in range(gn.shape[0]):
            start = k * part
            gn[k] = both[start // g.shape[1]][:, start % g.shape[1] : start % g.shape[1] + part]
        acc[...] = jnp.zeros_like(acc)

    h = mm(n2[...], wup[...]) + b1[...]
    a, slope = gelu_parts(h)
    pack[:, :cut] = a.astype(BF16)
    hg = (ag_ref[...].astype(F32) * slope).astype(BF16)
    acc[...] += mm(hg, wup[...], NT)
    b1g[...] = jnp.sum(hg.astype(F32), axis=0, keepdims=True)
    pack[:, pack.shape[1] - part :] = gn[step]
    if not paired:
        pack[:, cut : 2 * cut] = hg
    else:
        half = cut // 2

        @pl.when(core == 0)
        def _():
            mine[0][...] = hg[:, :half]
            pack[:, cut : cut + half] = hg[:, half:]

        @pl.when(core == 1)
        def _():
            mine[0][...] = hg[:, half:]
            pack[:, cut : cut + half] = hg[:, :half]

    @pl.when(step == pl.num_programs(0) - 1)
    def _():
        ng = acc[...]
        n, rate = normalized(wide[...])
        e = ng * gain[...]
        pulled = e - jnp.mean(e, axis=-1, keepdims=True) - n * jnp.mean(e * n, axis=-1, keepdims=True)
        r = cot[...].astype(F32) + rate * pulled
        br = r.astype(BF16)
        rgrad[...] = br
        brf = br.astype(F32)
        gg = mm(br, wo[...], NT)
        convgt[...] = (gg * second[...].astype(F32)).T.astype(BF16)
        sg = (gg * conv[...].astype(F32)).astype(BF16)
        sgrad[...] = sg
        sgf = sg.astype(F32)
        vecs[0:1] = jnp.sum(ng * n, axis=0, keepdims=True)
        vecs[1:2] = jnp.sum(ng, axis=0, keepdims=True)
        vecs[2:3] = jnp.sum(brf, axis=0, keepdims=True)
        vecs[3:4] = jnp.sum(sgf, axis=0, keepdims=True)
        put_halves(brf.T.astype(BF16), mine_t, other_t, 0, core, freq_parts)
        put_halves(sgf.T.astype(BF16), mine_t, other_t, 1, core, freq_parts)


def mlp_call(tok, convt, second, wo, ob, gain, bias, wup, b1, active_grad, cot, cut, paired, freq_parts, after=(), carry=()):
    rows, width = tok.shape
    ff = wup.shape[1]
    steps = ff // cut
    part = 2 * width // steps
    span = cut + (cut // 2 if paired else cut) + part

    def full(i):
        return (0, 0)

    def along(i):
        return (0, i)

    token = pl.BlockSpec((rows, width), full)
    vec = pl.BlockSpec((1, width), full)
    act = shape((rows, width), BF16)
    mine = [shape((rows, ff // 2), BF16)] if paired else []
    turned, turned_spec = shape((width, rows), BF16), pl.BlockSpec((width, rows), full)
    wide = act
    return launch(
        functools.partial(mlp_kernel, paired, freq_parts),
        (steps,),
        (tok, convt, second, wo, ob, gain, bias, wup, b1, active_grad, cot),
        [
            token,
            turned_spec,
            token,
            pl.BlockSpec((width, width), full),
            vec,
            vec,
            vec,
            pl.BlockSpec((width, cut), along),
            pl.BlockSpec((1, cut), along),
            pl.BlockSpec((rows, cut), along),
            token,
        ],
        (shape((rows, span * steps), BF16), wide, shape((1, ff), F32), wide, turned, act, turned, turned, shape((8, width), F32), *mine),
        (
            pl.BlockSpec((rows, span), along),
            token,
            pl.BlockSpec((1, cut), along),
            token,
            turned_spec,
            token,
            turned_spec,
            turned_spec,
            pl.BlockSpec((8, width), full),
            *[pl.BlockSpec((rows, cut // 2), along) for _ in mine],
        ),
        [pltpu.VMEM((rows, width), BF16), pltpu.VMEM((steps, rows, part), BF16), pltpu.VMEM((rows, width), BF16), pltpu.VMEM((rows, width), F32), pltpu.VMEM((rows, width), F32)],
        cost(2 * rows * width * (2 * ff + width), wup.size * 4 + rows * ff * 4 + rows * width * 14, rows * ff),
        "mix_out_mlp",
        after,
        carry,
    )


def unpacked(pack, hidden, steps, cut):
    rows = pack.shape[0]
    blocks = pack.reshape(rows, steps, -1)
    tail = blocks[:, :, cut + hidden :].reshape(rows, -1)
    return blocks[:, :, :cut].reshape(rows, -1), blocks[:, :, cut : cut + hidden].reshape(rows, -1), tail[:, : tail.shape[1] // 2], tail[:, tail.shape[1] // 2 :]


def put_halves(value, mine, other, half, core, freq_parts):
    per = value.shape[0] // freq_parts
    even = [value[(2 * k) * per : (2 * k + 1) * per] for k in range(freq_parts // 2)]
    odd = [value[(2 * k + 1) * per : (2 * k + 2) * per] for k in range(freq_parts // 2)]

    base = half * per * (freq_parts // 2)

    def put(ref, blocks):
        for k, block in enumerate(blocks):
            ref[base + k * per : base + (k + 1) * per] = block

    @pl.when(core == 0)
    def _():
        put(mine, even)
        put(other, odd)

    @pl.when(core == 1)
    def _():
        put(mine, odd)
        put(other, even)


def block_out_kernel(act, wdown, res, b2, out, acc):
    step = pl.program_id(0)
    part = mm(act[...], wdown[...])

    @pl.when(step == 0)
    def _():
        acc[...] = res[...].astype(F32) + b2[...] + part

    @pl.when(step > 0)
    def _():
        acc[...] += part

    @pl.when(step == pl.num_programs(0) - 1)
    def _():
        out[...] = acc[...].astype(BF16)


def block_out_call(pack, wdown, res, b2, cut, after=(), carry=()):
    rows, width = res.shape
    ff = wdown.shape[0]
    step = pack.shape[1] // ff
    if step * ff != pack.shape[1]:
        pack, step = unpacked(pack, cut, ff // cut, cut)[0], 1

    def full(i):
        return (0, 0)

    token = pl.BlockSpec((rows, width), full)
    return launch(
        block_out_kernel,
        (ff // cut,),
        (pack, wdown, res, b2),
        [pl.BlockSpec((rows, cut), lambda i: (0, step * i)), pl.BlockSpec((cut, width), lambda i: (i, 0)), token, pl.BlockSpec((1, width), full)],
        (shape((rows, width), BF16),),
        (token,),
        [pltpu.VMEM((rows, width), F32)],
        cost(2 * rows * width * ff, wdown.size * 2 + rows * ff * 2 + rows * width * 8),
        "block_out",
        after,
        carry,
    )


def back_kernel(mgt, value, gate, sgrad, weight, tok, gain, rgrad, out, vecs, mg, acc):
    step = pl.program_id(0)

    @pl.when(step == 0)
    def _():
        mg[...] = mgt[...].astype(F32).T.astype(BF16)
        acc[...] = mm(sgrad[...], weight[...], NT)

    @pl.when(step == 1)
    def _():
        pv = (gate[...].astype(F32) * mg[...].astype(F32)).astype(BF16)
        acc[...] += mm(pv, weight[...], NT)
        vecs[2:3] = jnp.sum(pv.astype(F32), axis=0, keepdims=True)

    @pl.when(step == 2)
    def _():
        pg = (value[...].astype(F32) * mg[...].astype(F32)).astype(BF16)
        ng = acc[...] + mm(pg, weight[...], NT)
        vecs[3:4] = jnp.sum(pg.astype(F32), axis=0, keepdims=True)
        n, rate = normalized(tok[...].astype(F32))
        vecs[0:1] = jnp.sum(ng * n, axis=0, keepdims=True)
        vecs[1:2] = jnp.sum(ng, axis=0, keepdims=True)
        e = ng * gain[...]
        pulled = e - jnp.mean(e, axis=-1, keepdims=True) - n * jnp.mean(e * n, axis=-1, keepdims=True)
        out[...] = (rgrad[...].astype(F32) + rate * pulled).astype(BF16)


def back_call(mgt, value, gate, sgrad, weight, tok, gain, rgrad, after=(), carry=()):
    rows, width = tok.shape

    def full(i):
        return (0, 0)

    token = pl.BlockSpec((rows, width), full)
    return launch(
        back_kernel,
        (3,),
        (mgt, value, gate, sgrad, weight, tok, gain, rgrad,),
        [
            pl.BlockSpec((width, rows), full),
            token,
            token,
            token,
            pl.BlockSpec((width, width), lambda i: (0, lax.rem(i + 2, 3))),
            token,
            pl.BlockSpec((1, width), full),
            token,
        ],
        (shape((rows, width), BF16), shape((8, width), F32)),
        (token, pl.BlockSpec((8, width), full)),
        [pltpu.VMEM((rows, width), BF16), pltpu.VMEM((rows, width), F32)],
        cost(2048 * 2 * rows * width * width * 3, 2048 * (weight.size * 2 + rows * width * 16)),
        "project_back",
        after,
        carry,
    )


def owner_part(offs_ref, wt, bias, x, mg, source, batch, tok_rows):
    chans = wt.shape[0] // 2
    vg = mm(wt, x, NT) + bias
    lane = lax.broadcasted_iota(jnp.int32, (1, x.shape[0]), 1)
    limit = jnp.zeros_like(lane)
    for b in range(batch):
        inside = jnp.logical_and(lane >= b * tok_rows, lane < (b + 1) * tok_rows)
        limit = jnp.where(inside, offs_ref[b] + b * tok_rows, limit)
    m = jnp.where(source * tok_rows + lane >= limit, mg.astype(F32), 0.0)
    return jnp.concatenate([vg[chans:] * m, vg[:chans] * m], axis=0).astype(BF16)


def owner_list_kernel(batch, tok_rows, parts, offs_ref, wt, bias, mg, *refs):
    xs, out = refs[:parts], refs[parts]
    me = lax.axis_index("freq")
    total = None
    for r in range(parts):
        x = xs[r][...]
        source = me ^ r
        pg = owner_part(offs_ref, wt[...], bias[...], x, mg[source], source, batch, tok_rows)
        part = mm(pg, x)
        total = part if total is None else total + part
    out[...] = total.astype(BF16)


def owner_grid_kernel(batch, tok_rows, offs_ref, wt, bias, mg, x, out, acc):
    step = pl.program_id(0)

    @pl.when(step == 0)
    def _():
        acc[...] = jnp.zeros_like(acc)

    pg = owner_part(offs_ref, wt[...], bias[...], x[0], mg[0], step, batch, tok_rows)
    acc[...] += mm(pg, x[0])

    @pl.when(step == pl.num_programs(0) - 1)
    def _():
        out[...] = acc[...].astype(BF16)


def owner_call(offsets, wt, bias, mg, xs, batch, tok_rows, after=(), carry=()):
    chans, rows = mg.shape[1:]
    width = wt.shape[1]
    listed = isinstance(xs, list)
    count = mg.shape[0]
    if listed:
        kernel = functools.partial(owner_list_kernel, batch, tok_rows, count)
        grid, x_specs, scratch, mg_spec = (1,), [whole((rows, width))] * count, [], whole(mg.shape)
    else:
        kernel = functools.partial(owner_grid_kernel, batch, tok_rows)
        xs = [xs]
        grid, x_specs = (count,), [pl.BlockSpec((1, rows, width), lambda i: (i, 0, 0))]
        scratch = [pltpu.VMEM((2 * chans, width), F32)]
        mg_spec = pl.BlockSpec((1, chans, rows), lambda i: (i, 0, 0))
    return launch(
        kernel,
        grid,
        (offsets, wt, bias, mg, *xs,),
        [smem(), whole(wt.shape), whole(bias.shape), mg_spec] + x_specs,
        (shape((2 * chans, width), BF16),),
        (whole((2 * chans, width)),),
        scratch,
        cost(8 * count * rows * chans * width, count * rows * width * 2),
        "owner_gradients",
        after,
        carry,
    )


def once(value, after):
    def nothing(after_ref, value_ref, out_ref):
        pass

    return pl.pallas_call(
        nothing,
        out_shape=shape(value.shape, value.dtype),
        in_specs=[anywhere(), anywhere()],
        out_specs=anywhere(),
        input_output_aliases={1: 0},
        name="gate",
    )(after, value)


def bit_order(chips, low_first):
    bits = list(range(chips.bit_length() - 1))
    return bits if low_first else bits[::-1]


def place_of(rel, order):
    place = 0
    for level, bit in enumerate(order):
        digit = lax.shift_right_logical(rel, bit) & 1
        place = place + digit * (1 << (len(order) - 1 - level))
    return place


def store_slot(keep, send, place, index, block):
    half = keep.shape[0]

    @pl.when(place < half)
    def _():
        keep[(place,) + index] = block

    @pl.when(place >= half)
    def _():
        send[(place - half,) + index] = block


def rows_kernel(chips, per, chip_order, dp_order, cot, act, cot_p, act_p, keep, send):
    chip = lax.axis_index("freq") // 2
    quarter = pl.program_id(0) ^ lax.axis_index("dp")
    total = (mm(cot[...], act[...]) + mm(cot_p[...], act_p[...])).astype(BF16)
    for k in range(chips):
        place = place_of(jnp.int32(k) ^ chip, chip_order)
        store_slot(keep, send, place_of(quarter, dp_order), (place,), total[k * per : (k + 1) * per])


def rows_pair(own, partner, width, dp, chips, low_first, after=(), carry=()):
    half, inner = own[0].shape
    per = half // chips
    out = shape((dp // 2, chips, per, width), BF16)
    arrays, specs = [], []
    for cot, pack in (own, partner):
        arrays += [cot, pack]
        specs += [whole(cot.shape), pl.BlockSpec((inner, width), lambda i: (0, 2 * i))]
    return launch(
        functools.partial(rows_kernel, chips, per, bit_order(chips, low_first), bit_order(dp, True)),
        (dp,),
        tuple(arrays),
        specs,
        (out, out),
        (whole(out.shape), whole(out.shape)),
        [],
        cost(4 * dp * half * inner * width, dp * inner * width * 4),
        "fc2_gradient",
        after,
        carry,
    )


def rows_plain(cot, act, cot_p, act_p, dp, chips, low_first):
    total = (mm(cot, act) + mm(cot_p, act_p)).astype(BF16)
    blocks = total.reshape(chips, cot.shape[0] // chips, dp, -1).transpose(2, 0, 1, 3)
    blocks = jnp.concatenate(halves_of(blocks.transpose(1, 0, 2, 3), bit_order(chips, low_first)), axis=0).transpose(1, 0, 2, 3)
    return halves_of(blocks, bit_order(dp, True), lax.axis_index("dp"))


def mixer_kernel(chips, per, order, turned, ga, gb, normed, turned_p, ga_p, gb_p, normed_p, keep, send):
    step = pl.program_id(0)
    chip = lax.axis_index("freq") // 2

    def put(half, total):
        for k in range(chips):
            place = place_of(jnp.int32(k) ^ chip, order)
            store_slot(keep, send, place, (slice(half * per, (half + 1) * per), slice(None)), total[k * per : (k + 1) * per].astype(BF16))

    @pl.when(step == 0)
    def _():
        def out(t, a, b):
            return jnp.concatenate([mm(t[...], a[...]), mm(t[...], b[...])], axis=1)

        put(0, out(turned, ga, gb) + out(turned_p, ga_p, gb_p))

    @pl.when(step == 1)
    def _():
        put(1, mm(turned[...], normed[...]) + mm(turned_p[...], normed_p[...]))


def mixer_pair(own, partner, width, chips, low_first, after=(), carry=()):
    order = bit_order(chips, low_first)
    half = width // 2
    per = half // chips
    out = shape((chips // 2, 2 * per, width), BF16)
    arrays, specs = [], []
    for turned, pack, normed in (own, partner):
        inner = turned.shape[1]
        arrays += [turned, pack, pack, normed]
        specs += [
            pl.BlockSpec((half, inner), lambda i: (i, 0)),
            pl.BlockSpec((inner, half), lambda i: (0, 3)),
            pl.BlockSpec((inner, half), lambda i: (0, 7)),
            whole(normed.shape),
        ]
    return launch(
        functools.partial(mixer_kernel, chips, per, order),
        (2,),
        tuple(arrays),
        specs,
        (out, out),
        (whole(out.shape), whole(out.shape)),
        [],
        cost(8 * half * inner * width, 4 * inner * width * 4),
        "mixer_gradient",
        after,
        carry,
    )


def halves_of(blocks, order, chip=None):
    chips = blocks.shape[0]
    chip = lax.axis_index("freq") // 2 if chip is None else chip
    picks = np.zeros(chips, np.int32)
    for rel in range(chips):
        place = sum(((rel >> bit) & 1) << (len(order) - 1 - level) for level, bit in enumerate(order))
        picks[place] = rel
    moved = jnp.take(blocks, jnp.asarray(picks) ^ chip, axis=0)
    return moved[: chips // 2], moved[chips // 2 :]


def cols_kernel(order, la, lb, rt, lap, lbp, rtp, keep, send, left):
    step = pl.program_id(0)
    chip = lax.axis_index("freq") // 2
    half = la.shape[1]

    @pl.when(step == 0)
    def _():
        for k, ref in enumerate((la, lb, lap, lbp)):
            left[k // 2, (k % 2) * half : (k % 2 + 1) * half] = ref[...].astype(F32).T.astype(BF16)

    total = (mm(left[0], rt[...]) + mm(left[1], rtp[...])).astype(BF16)
    store_slot(keep, send, place_of(step ^ chip, order), (), total)


def cols_pair(mine, pack, pack_p, width, cut, chips, low_first, after=(), carry=()):
    order = bit_order(chips, low_first)
    rows = mine.shape[0]
    per = mine.shape[1] // chips
    last = pack.shape[1] // per - 1
    step = pack.shape[1] // chips // per
    out = shape((chips // 2, width, per), BF16)
    out_spec = pl.BlockSpec((chips // 2, width, per), lambda i: (0, 0, 0))

    def at(place):
        return pl.BlockSpec((rows, per), place)

    first, second = (lambda i: (0, last - step)), (lambda i: (0, last))
    return launch(
        functools.partial(cols_kernel, order),
        (chips,),
        (pack, pack, mine, pack_p, pack_p, pack_p),
        [at(first), at(second), at(lambda i: (0, i)), at(first), at(second), at(lambda i: (0, step * i + 2))],
        (out, out),
        (out_spec, out_spec),
        [pltpu.VMEM((2, width, rows), BF16)],
        cost(4 * width * rows * mine.shape[1], (width * rows + rows * mine.shape[1] * 2) * 4),
        "fc1_gradient",
        after,
        carry,
    )


def cols_plain(lt, rt, ltp, rtp, chips, low_first):
    total = (mm(lt.T, rt) + mm(ltp.T, rtp)).astype(BF16)
    return halves_of(total.reshape(lt.shape[1], chips, -1).transpose(1, 0, 2), bit_order(chips, low_first))


def flip(value, freq_parts, bit):
    return lax.ppermute(value, "freq", [(i, i ^ bit) for i in range(freq_parts)])


def begin(keep, send, axis, bit):
    count = lax.axis_size(axis)
    return keep, lax.ppermute(send, axis, [(i, i ^ bit) for i in range(count)])


def finish(pending):
    return pending[0].astype(F32) + pending[1].astype(F32)


def step_on(pending, axis, bits, level):
    if level == len(bits):
        return finish(pending)[0], None
    half = pending[0].shape[0] // 2
    send = finish([v[half:] for v in pending]).astype(BF16)
    keep = finish([v[:half] for v in pending]).astype(BF16)
    return begin(keep, send, axis, bits[level]), send


def across_first(blocks):
    blocks = blocks.astype(BF16)
    count = blocks.shape[0]
    me = lax.axis_index("dp")
    blocks = blocks.reshape((count // 2, 2) + blocks.shape[1:])
    send = lax.dynamic_index_in_dim(blocks, 1 - me % 2, 1, keepdims=False)
    keep = lax.dynamic_index_in_dim(blocks, me % 2, 1, keepdims=False)
    return begin(keep, send, "dp", 1), send


def across_next(pending):
    total = finish(pending)
    me, count = lax.axis_index("dp"), lax.axis_size("dp")
    step = count // total.shape[0]
    total = total.astype(BF16)
    total = total.reshape((total.shape[0] // 2, 2) + total.shape[1:])
    mine = me // step % 2
    send = lax.dynamic_index_in_dim(total, 1 - mine, 1, keepdims=False)
    keep = lax.dynamic_index_in_dim(total, mine, 1, keepdims=False)
    return begin(keep, send, "dp", step), send


def across_rest(pending):
    while pending[0].shape[0] > 1:
        pending, _ = across_next(pending)
    return finish(pending)[0]


def pack_kernel(chans, one, two, b2, b1, skip, out):
    dp, freq = out.shape[:2]
    me = lax.axis_index("freq")
    column = jnp.broadcast_to(skip[...], (chans, 128)).T[0:1, :]
    per = b1.shape[1] // (freq * chans)

    def put(f, start, value):
        for d in range(dp):
            out[d, f, start : start + value.shape[0]] = value

    for f in range(freq):
        cut = slice(f * chans, (f + 1) * chans)
        put(f, 0, one[0:2, cut])
        for r in range(3):
            group, chunk = divmod(3 * f + r, freq)
            source = (one[2:3], one[3:4], two[3:4])[group]
            put(f, 2 + r, source[:, chunk * chans : (chunk + 1) * chans])
        put(f, 5, two[0:3, cut])
        put(f, 8, b2[:, cut])
        for r in range(per):
            start = (f * per + r) * chans
            put(f, 9 + r, b1[:, start : start + chans])
        put(f, 9 + per, jnp.where(me == f, column, 0.0))
    for d in range(dp):
        for f in range(freq):
            out[d, f, 10 + per :] = jnp.zeros((out.shape[2] - 10 - per, chans), F32)


def packed_vectors(one, two, b2, b1, skip, dp, freq, after=(), carry=()):
    chans = one.shape[1] // freq
    lines = 16
    if freq == 8:
        return launch(
            functools.partial(pack_kernel, chans),
            (1,),
            (one, two, b2, b1, skip),
            [whole(v.shape) for v in (one, two, b2, b1, skip)],
            (shape((dp, freq, lines, chans), F32),),
            (whole((dp, freq, lines, chans)),),
            [],
            cost(1, 1),
            "pack_vectors",
            after,
            carry,
        )
    own = (jnp.arange(freq, dtype=jnp.int32) == lax.axis_index("freq")).astype(F32)[:, None, None] * skip.reshape(1, 1, chans)
    rows = jnp.concatenate([one[:2], two[:3], b2]).reshape(6, freq, chans).transpose(1, 0, 2)
    bias_in = jnp.concatenate([one[2:4], two[3:4]]).reshape(freq, 3, chans)
    rows = jnp.concatenate([rows[:, :2], bias_in, rows[:, 2:], b1.reshape(freq, -1, chans), own], axis=1)
    return jnp.broadcast_to(rows[None], (dp,) + rows.shape), carry


def to_all(block):
    dp, freq = lax.axis_size("dp"), lax.axis_size("freq")
    wide = block if block.ndim == 4 else jnp.broadcast_to(block[None], (dp,) + block.shape)
    wide = wide.reshape((dp * freq,) + wide.shape[2:])
    return lax.all_to_all(wide, ("dp", "freq"), split_axis=0, concat_axis=0, tiled=True)


def reblocked(blocks, count, width):
    if blocks.shape[0] == count and blocks.shape[2] == width:
        return blocks
    whole = blocks.transpose(1, 0, 2).reshape(blocks.shape[1], -1)
    need = count * width
    whole = jnp.pad(whole, ((0, 0), (0, max(0, need - whole.shape[1]))))[:, :need]
    return whole.reshape(-1, count, width).transpose(1, 0, 2)


def body(tokens, offsets, kernel_lengths, norm1_gain, norm1_bias, w_in, in_bias, kernel_taps, skip_gain, w_out, out_bias, norm2_gain, norm2_bias, w_up, fc1_bias, w_down, fc2_bias, cotangent):
    freq = lax.axis_size("freq")
    dp = lax.axis_size("dp")
    chips = freq // 2
    batch, tok_rows, width = tokens.shape
    rows = batch * tok_rows
    ff = w_up.shape[1]
    chans = width // freq
    me = lax.axis_index("freq")
    core = lax.rem(me, 2)

    def row(v):
        return v.reshape(1, -1)

    tok = tokens.reshape(rows, width)
    cot = cotangent.reshape(rows, width)
    tap_rows = kernel_taps.shape[1]
    reach = -(-freq * tap_rows // tok_rows)
    lens = lax.dynamic_slice_in_dim(kernel_lengths, me * chans, chans).reshape(chans, 1)
    skip = skip_gain.reshape(chans, 1)

    def swap(v):
        return flip(v, freq, 1)

    cut = 768
    normed, mixed_t, value, gate, gate_two = front_call(
        tok, offsets, norm1_gain, norm1_bias, w_in, in_bias, kernel_taps, batch, tok_rows
    )
    mixed = lax.all_to_all(mixed_t.reshape(freq, chans, -1), "freq", split_axis=0, concat_axis=0, tiled=True)
    taps = mixed if tap_rows == tok_rows else reblocked(mixed[:, :, rows:], reach, tok_rows)
    active_grad, b2g, cot_mine, cot_other = active_grad_call(cot, w_down, cut, freq, after=(mixed_t,))
    own_w = jnp.concatenate([lax.dynamic_slice_in_dim(w_in, k * width + me * chans, chans, axis=1) for k in range(2)], axis=1).T
    own_b = jnp.concatenate([lax.dynamic_slice_in_dim(in_bias, k * width + me * chans, chans) for k in range(2)]).reshape(-1, 1)
    (conv, k_spec), (cot_p, normed_p, normed) = forward_call(mixed, batch, tok_rows, taps, lens, skip, after=(active_grad, own_w, own_b), carry=(swap(cot_other), swap(normed), normed))
    conv_t = lax.all_to_all(conv, "freq", split_axis=0, concat_axis=0, tiled=True).reshape(width, rows)
    near = []
    if freq == 8:
        near = [flip(normed, freq, 2), flip(normed, freq, 4), flip(normed, freq, 6)]
    paired = freq == 8 and ff == 4 * cut
    pack, res, b1g, rgrad, convg_t, sgrad, turned, turned_other, vec_two, *mine = mlp_call(
        tok, conv_t, gate_two, w_out, row(out_bias), row(norm2_gain), row(norm2_bias), w_up, row(fc1_bias), active_grad, cot, cut, paired, freq
    )
    mine = mine[0] if paired else None
    block_out = block_out_call(pack, w_down, res, row(fc2_bias), cut)
    convg = lax.all_to_all(convg_t.reshape(freq, chans, rows), "freq", split_axis=0, concat_axis=0, tiled=True)
    half = width // 2
    if paired:
        pack_p, turned_p = swap(pack), swap(turned_other)
        fc2, near = rows_pair((cot_mine, pack), (cot_p, pack_p), width, dp, chips, True, after=(block_out,), carry=near)
        fc1 = cols_pair(mine, pack, pack_p, width, cut, chips, False, after=(fc2[1],))
        far = [swap(v) for v in near]
        mixed_grad = adjoint_call(convg, batch, k_spec, skip, after=(fc1[1],))
        mixer = mixer_pair((turned, pack, normed), (turned_p, pack_p, normed_p), width, chips, True, after=(mixed_grad,))
        normed_all = [v for pair_of in zip([normed, *near], [normed_p, *far]) for v in pair_of]
    else:
        normed_all = lax.all_gather(normed, "freq", axis=0, tiled=False)
        act, hg, gated, n2 = unpacked(pack, cut, ff // cut, cut)
        hg = hg.reshape(rows, chips, 2, ff // freq)
        hg_mine = jnp.take(hg, core, axis=2).reshape(rows, ff // 2)
        hg_other = jnp.take(hg, 1 - core, axis=2).reshape(rows, ff // 2)
        act_p, gated_p, n2_p, turned_p = swap(act), swap(gated), swap(n2), swap(turned_other)
        fc2 = rows_plain(cot_mine, act, cot_p, act_p, dp, chips, True)
        fc1 = cols_plain(n2, hg_mine, n2_p, swap(hg_other), chips, False)
        mixer = []
        for lt, rt, ltp, rtp in ((turned[:half], gated, turned_p[:half], gated_p), (turned[half:], normed, turned_p[half:], normed_p)):
            mixer.append((mm(lt, rt) + mm(ltp, rtp)).astype(BF16).reshape(chips, -1, width))
        mixer = halves_of(jnp.concatenate(mixer, axis=1), bit_order(chips, True))
        mixed_grad = adjoint_call(convg, batch, k_spec, skip)
    mixed_grad_t = lax.all_to_all(mixed_grad, "freq", split_axis=0, concat_axis=0, tiled=True).reshape(width, rows)
    low, high = ([2 << bit for bit in bit_order(chips, first)] for first in (True, False))
    deep = [1 << bit for bit in bit_order(dp, True)]
    fc2_sum, fc1_sum, mixer_sum = begin(*fc2, "dp", deep[0]), begin(*fc1, "freq", high[0]), begin(*mixer, "freq", low[0])
    owned, (keep, keep_m) = owner_call(
        offsets, own_w, own_b, mixed_grad, normed_all, batch, tok_rows, after=(mixer[1],), carry=(fc2_sum[0], mixer_sum[0])
    )
    fc2_sum, sent = step_on((keep, fc2_sum[1]), "dp", deep, 1)
    mixer_sum, sent_m = step_on((once(keep_m, sent), mixer_sum[1]), "freq", low, 1)
    (taps_g, skip_g), (keep, keep_1, keep_m) = taps_grad_call(
        mixed, convg, lens, tok_rows, reach, dp if tap_rows == tok_rows else 0, after=(owned, sent_m), carry=(fc2_sum[0], fc1_sum[0], mixer_sum[0])
    )
    fc2_sum = (keep, fc2_sum[1])
    if tap_rows != tok_rows:
        taps_g = reblocked(taps_g, freq, tap_rows).reshape(freq, dp, chans // dp, tap_rows).transpose(1, 0, 2, 3)
    taps_g = taps_g.reshape(dp, width // dp, tap_rows)
    taps_sum, sent_t = across_first(taps_g)
    fc1_sum, sent_1 = step_on((once(keep_1, sent_t), fc1_sum[1]), "freq", high, 1)
    mixer_sum = (once(keep_m, sent_1), mixer_sum[1])
    for level in range(2, len(low) + 1):
        mixer_sum, _ = step_on(mixer_sum, "freq", low, level)
    mixer = mixer_sum.astype(BF16)
    parts = jnp.concatenate([owned, mixer[chans:]]).reshape(3, chans, width)
    pieces, moved = [], []
    for r in range(3):
        part = lax.rem((freq % 3) * (r - me + 3 * freq), 3)
        moved.append(lax.dynamic_index_in_dim(parts, part, 0, keepdims=False))
        pieces.append(lax.ppermute(moved[-1], "freq", [((3 * d + r) % freq, d) for d in range(freq)]))
    fc2_sum = (once(keep, moved[0]), fc2_sum[1])
    for level in range(2, len(deep)):
        fc2_sum, _ = step_on(fc2_sum, "dp", deep, level)
    half = chips // 2
    sent = finish([v[0, half:] for v in fc2_sum]).astype(BF16)
    fc2_sum = begin(finish([v[0, :half] for v in fc2_sum]).astype(BF16), sent, "freq", low[0])
    (input_grad, vec_one), (keep, keep_1, keep_t) = back_call(
        mixed_grad_t, value, gate, sgrad, w_in, tok, row(norm1_gain), rgrad,
        after=(*moved, sent), carry=(fc2_sum[0], fc1_sum[0], taps_sum[0]),
    )
    fa = ff // freq
    fc1_sum = (keep_1, fc1_sum[1])
    for level in range(2, len(high) + 1):
        fc1_sum, _ = step_on(fc1_sum, "freq", high, level)
    first, sent_1 = across_first(fc1_sum.reshape(dp, width // dp, fa))
    vectors, (keep, keep_t) = packed_vectors(vec_one, vec_two, b2g, b1g, skip_g, dp, freq, after=(sent_1,), carry=(keep, keep_t))
    final = to_all(vectors)
    taps_sum, sent_t = across_next((keep_t, taps_sum[1]))
    second = jnp.concatenate(pieces + [once(mixer[:chans], sent_t)], axis=0).T.reshape(dp, width // dp, 4 * chans)
    second, sent = across_first(second)
    first = (once(once(first[0], sent), final), first[1])
    first, sent = across_next(first)
    fc2_sum = (once(keep, sent), fc2_sum[1])
    fc2_sum, sent = step_on(fc2_sum, "freq", low, 1)
    second, sent = across_next((once(second[0], sent), second[1]))
    quarter_sum = across_rest((once(taps_sum[0], sent), taps_sum[1])).astype(BF16).reshape(freq, chans // dp, tap_rows)
    spread = to_all(quarter_sum)
    for level in range(2, len(low) + 1):
        fc2_sum, _ = step_on(fc2_sum, "freq", low, level)
    first, second = across_rest(first), across_rest(second)
    fc1_final, in_final, out_final = first, second[:, : 3 * chans], second[:, 3 * chans :]
    fc2_final = fc2_sum.T
    spread = spread.reshape(dp, freq, chans // dp, tap_rows).transpose(1, 0, 2, 3).reshape(width, tap_rows)
    taps_final = spread.astype(F32) * jnp.square(jnp.tanh(kernel_taps / SHRINK))
    final = jnp.sum(final, axis=0)
    n1g, n1b = final[0], final[1]
    inb = final[2:5].reshape(-1)
    n2g, n2b, outb, b2f = (final[k] for k in range(5, 9))
    lines = ff // width
    b1f, skg = final[9 : 9 + lines].reshape(-1), final[9 + lines]
    return (
        block_out.reshape(tokens.shape),
        input_grad.reshape(tokens.shape),
        n1g,
        n1b,
        in_final,
        inb,
        taps_final,
        skg,
        out_final,
        outb,
        n2g,
        n2b,
        fc1_final,
        b1f,
        fc2_final,
        b2f,
    )


def solution(mesh):
    token, whole, lead = P("dp", "freq", None), P(), P("freq")
    both = P("dp", "freq")
    in_specs = (token, P("dp"), whole, whole, whole, whole, whole, P(None, "freq"), lead) + (whole,) * 8 + (token,)
    out_specs = (token, token, lead, lead, both, lead, P(None, "freq"), lead, both, lead, lead, lead, both, lead, both, lead)
    return jax.shard_map(body, mesh=mesh, in_specs=in_specs, out_specs=out_specs, check_vma=False)
```
